32 devices in a mesh: seq: 8 (over z, x), mp: 4 (over y, core).
Axes of the slice: x: 2, y: 2, z: 4, core: 2. Of those that a mesh axis runs over, the one named last changes fastest.
Arguments:
- inputs: float32 [2, 2048, 1024], P(None, 'seq', 'mp'), may hold values from -6 to 6
- row_starts: int32 [2, 8], P(None, 'seq'), may hold values from 0 to 1, as said below
- norm_gain: float32 [1024], replicated, may hold values from 0.5 to 1.5
- in_weight: float32 [2, 1024, 2048], P(None, None, 'mp'), may hold values from -0.1875 to 0.1875
- conv_weight: float32 [4, 2048], P(None, 'mp'), may hold values from -3 to 3
- conv_bias: float32 [2048], P('mp'), may hold values from -0.5 to 0.5
- xproj_weight: float32 [2048, 96], P('mp'), may hold values from -0.125 to 0.125
- dtproj_weight: float32 [64, 2048], P(None, 'mp'), may hold values from -0.75 to 0.75
- dt_bias: float32 [2048], P('mp'), may hold values from -9 to -3
- decay_log: float32 [16, 2048], P(None, 'mp'), may hold values from 0 to 2.77
- skip_gain: float32 [2048], P('mp'), may hold values from 0.5 to 1.5
- out_weight: float32 [2048, 1024], P('mp'), may hold values from -0.25 to 0.25
- output_grad: float32 [2, 2048, 1024], P(None, 'seq', 'mp'), may hold values from -6 to 6
Outputs:
- output: float32 [2, 2048, 1024], P(None, 'seq', 'mp')
- input_grad: float32 [2, 2048, 1024], P(None, 'seq', 'mp')
- grad_norm_gain: float32 [1024], P('mp')
- grad_in_weight: float32 [2, 1024, 2048], P(None, None, 'mp')
- grad_conv_weight: float32 [4, 2048], P(None, 'mp')
- grad_conv_bias: float32 [2048], P('mp')
- grad_xproj_weight: float32 [2048, 96], P('mp')
- grad_dtproj_weight: float32 [64, 2048], P(None, 'mp')
- grad_dt_bias: float32 [2048], P('mp')
- grad_decay_log: float32 [16, 2048], P(None, 'mp')
- grad_skip_gain: float32 [2048], P('mp')
- grad_out_weight: float32 [2048, 1024], P('mp')
The draws below stay inside these ranges and needn't reach their ends.
Inputs may be any that keep to these rules, and one draw needn't show every extreme that they name: `row_starts`: in every lane group 0 begins a row and each row spans a multiple of 2 groups; in one lane, drawn from the seed, a single row spans all 8 groups.
All inputs are finite; a program needn't handle non-finite values.
Results may differ from the reference program's by a relative error of at most 0.024.
Values may be sent and summed in bfloat16 or wider, within the bound.
No kernel may reach another device: no remote copies, remote signals or barrier semaphores. Data moves between devices by JAX's collectives and lax.ppermute only.
A program may use at most 192 MiB of HBM per device.

```python
import jax
import jax.numpy as jnp
from jax import lax

D = 1024
E = 2048
DSTATE = 16
CONV = 4
DTRANK = 64
LANES = 2
GROUP = 256
BUCKET_GROUPS = 2
GROUPS = 8
SEQLEN = 2048


def draw_row_starts(key, part):
    key = jax.random.fold_in(key, 7)
    first_key, second_key = jax.random.split(key)
    slot_count = GROUPS // BUCKET_GROUPS
    picks = jax.random.randint(first_key, (LANES, slot_count), 0, 4)
    units = jnp.where(picks == 3, 4, jnp.where(picks == 2, 2, 1))
    bounds = jnp.cumsum(units, axis=1) * BUCKET_GROUPS
    column = jnp.arange(GROUPS)
    hits = jnp.any(bounds[:, :, None] == column[None, None, :], axis=1)
    first_col = column == 0
    starts = jnp.logical_or(hits, first_col[None, :])
    single = jax.random.randint(second_key, (), 0, LANES)
    lane_ids = jnp.arange(LANES)[:, None]
    starts = jnp.where(lane_ids == single, first_col[None, :], starts)
    return starts.astype(jnp.int32)


def block_levels(key, dims, shards, low, top_value):
    def one(position, parts):
        heights = jax.random.uniform(jax.random.fold_in(jax.random.fold_in(key, 6), position), (parts,), jnp.float32, low / len(shards), top_value / len(shards))
        return jnp.repeat(jnp.exp(heights), dims[position] // parts).reshape((-1,) + (1,) * (len(dims) - position - 1))

    gain = one(*shards[0])
    for cut in shards[1:]:
        gain = gain * one(*cut)
    return gain


def bell_draw(rng, shape, scale, most, shards=(), dtype=jnp.bfloat16):
    factor_of = block_levels(rng, shape, shards, -0.22, 0.18) if shards else 1.0
    result = jax.random.normal(rng, shape, jnp.float32) * scale * factor_of
    return jnp.minimum(jnp.maximum(result, -most), most).astype(dtype)


def setup_inputs(seed: int = 0) -> dict:
    key_of = jax.random.split(jax.random.key(seed), 14)
    return {
        "inputs": bell_draw(key_of[0], (LANES, SEQLEN, D), 1.0, 6.0, ((1, 8), (2, 4)), jnp.float32),
        "row_starts": draw_row_starts(jax.random.fold_in(key_of[13], 71), 0),
        "norm_gain": jnp.clip(1.0 + 0.1 * jax.random.normal(key_of[2], (D,), jnp.float32), 0.5, 1.5),
        "in_weight": bell_draw(key_of[3], (2, D, E), D ** -0.5, 0.1875, ((2, 4),), jnp.float32),
        "conv_weight": bell_draw(key_of[4], (CONV, E), CONV ** -0.5, 3.0, ((1, 4),), jnp.float32),
        "conv_bias": jnp.clip(jax.random.uniform(key_of[5], (E,), jnp.float32, -0.5, 0.5) * block_levels(key_of[5], (E,), ((0, 4),), -0.4, 0.0), -0.5, 0.5),
        "xproj_weight": bell_draw(key_of[6], (E, DTRANK + 2 * DSTATE), E ** -0.5, 0.125, ((0, 4),), jnp.float32),
        "dtproj_weight": bell_draw(key_of[7], (DTRANK, E), DTRANK ** -0.5, 0.75, ((1, 4),), jnp.float32),
        "dt_bias": jnp.clip(-9.0 + 6.0 * jax.random.uniform(key_of[8], (E,), jnp.float32) ** block_levels(key_of[8], (E,), ((0, 4),), -0.2, 0.2), -9.0, -3.0),
        "decay_log": jnp.clip(2.77 * jax.random.uniform(key_of[9], (DSTATE, E), jnp.float32) ** block_levels(key_of[9], (DSTATE, E), ((1, 4),), -0.2, 0.2), 0.0, 2.77),
        "skip_gain": jnp.clip(0.5 + 1.0 * jax.random.uniform(key_of[10], (E,), jnp.float32) ** block_levels(key_of[10], (E,), ((0, 4),), -0.2, 0.2), 0.5, 1.5),
        "out_weight": bell_draw(key_of[11], (E, D), (E // 4) ** -0.5, 0.25, ((0, 4),), jnp.float32),
        "output_grad": bell_draw(key_of[12], (LANES, SEQLEN, D), 1.0, 6.0, ((1, 8), (2, 4)), jnp.float32),
    }


@jax.custom_vjp
def low(v):
    return lax.optimization_barrier(v.astype(jnp.bfloat16)).astype(jnp.float32)

@jax.custom_vjp
def low_back(v):
    return v

def low_keep(v):
    return (low(v), None)

def low_pass(kept, grad):
    return (grad,)

def back_keep(v):
    return (v, None)

def back_low(kept, grad):
    return (low(grad),)
low.defvjp(low_keep, low_pass)
low_back.defvjp(back_keep, back_low)
HIGHEST = lax.Precision.HIGHEST

def product(pattern, left_op, right_op):
    return jnp.einsum(pattern, left_op, right_op, precision=HIGHEST)

def prepare(row_starts, seqlen):
    positions = jnp.arange(seqlen)
    offset = positions % GROUP
    group_first = jnp.repeat(row_starts, GROUP, axis=1).astype(jnp.float32)
    row_first = group_first * (offset == 0).astype(jnp.float32)
    valid_taps = []
    for offset_k in range(1, CONV):
        in_range = (positions >= offset_k).astype(jnp.float32)
        cut_off = group_first * (offset < offset_k).astype(jnp.float32)
        valid_taps.append(in_range * (1.0 - cut_off))
    return (row_first, valid_taps)

def scan_lane(step_size, mixed, input_mat, read_mat, row_first, decay_rate):
    lane_count, seqlen, inner_width = step_size.shape
    block_count = seqlen // GROUP

    def blocks(values):
        return jnp.moveaxis(values.reshape((lane_count, block_count, GROUP) + values.shape[2:]), 1, 0)

    def token_step(state, pieces):
        step_delta, step_mixed, step_input, step_read, step_first = pieces
        factor = jnp.exp(step_delta[:, None, :] * decay_rate) * (1.0 - step_first)[:, None, None]
        state = factor * state + step_delta[:, None, :] * step_input[:, :, None] * step_mixed[:, None, :]
        return (state, product('ln,lne->le', step_read, state))

    def block_step(state, pieces):
        shifted = tuple((jnp.moveaxis(piece, 1, 0) for piece in pieces))
        state, outputs = lax.scan(token_step, state, shifted)
        return (state, jnp.moveaxis(outputs, 0, 1))
    begin_state = jnp.zeros((lane_count, DSTATE, inner_width), jnp.float32)
    block_items = tuple((blocks(values) for values in (step_size, mixed, input_mat, read_mat, row_first)))
    _, outputs = lax.scan(jax.checkpoint(block_step), begin_state, block_items)
    return jnp.moveaxis(outputs, 0, 1).reshape(lane_count, seqlen, inner_width)

def forward(inputs, norm_gain, in_weight, conv_weight, conv_bias, xproj_weight, dtproj_weight, dt_bias, decay_log, skip_gain, out_weight, row_first, valid_taps):
    unit_rows = inputs * lax.rsqrt(lax.optimization_barrier(jnp.mean(inputs * inputs, axis=2, keepdims=True)) + 1e-05)
    normed = low(unit_rows * norm_gain)
    inner_act = low(low_back(product('ltd,de->lte', normed, low(in_weight[0]))))
    gate_in = low_back(product('ltd,de->lte', normed, low(in_weight[1])))
    conv_sum = conv_bias + conv_weight[CONV - 1] * inner_act
    for offset_k in range(1, CONV):
        shifted = jnp.pad(inner_act[:, :-offset_k], ((0, 0), (offset_k, 0), (0, 0)))
        conv_sum = conv_sum + conv_weight[CONV - 1 - offset_k] * shifted * valid_taps[offset_k - 1][:, :, None]
    mixed = jax.nn.silu(conv_sum)
    projected = low_back(product('lte,er->ltr', low(mixed), low(xproj_weight)))
    dt_low = low(projected[:, :, :DTRANK])
    input_mat = projected[:, :, DTRANK:DTRANK + DSTATE]
    read_mat = projected[:, :, DTRANK + DSTATE:]
    step_size = jax.nn.softplus(low_back(product('ltr,re->lte', dt_low, low(dtproj_weight))) + dt_bias)
    decay_rate = -jnp.exp(decay_log)
    scan_out = scan_lane(step_size, mixed, input_mat, read_mat, row_first, decay_rate) + skip_gain * mixed
    gated = low(scan_out * jax.nn.silu(gate_in))
    return inputs + low_back(product('lte,ed->ltd', gated, low(out_weight)))

def reference(inputs, row_starts, norm_gain, in_weight, conv_weight, conv_bias, xproj_weight, dtproj_weight, dt_bias, decay_log, skip_gain, out_weight, output_grad):
    row_first, valid_taps = prepare(row_starts, inputs.shape[1])

    def layer_fn(*params):
        return forward(*params, row_first, valid_taps)
    output, pullback = jax.vjp(layer_fn, inputs, norm_gain, in_weight, conv_weight, conv_bias, xproj_weight, dtproj_weight, dt_bias, decay_log, skip_gain, out_weight)
    gradients = pullback(output_grad)
    return (output, gradients[0], gradients[1], gradients[2], gradients[3], gradients[4], gradients[5], gradients[6], gradients[7], gradients[8], gradients[9], gradients[10])
```

```python
import functools

import jax
import jax.numpy as jnp
from jax import lax
from jax.experimental import pallas as pl
from jax.experimental.pallas import tpu as pltpu
from jax.sharding import PartitionSpec as P

F32 = jnp.float32
BF16 = jnp.bfloat16
LOG2E = 1.4426950408889634
CHUNK = 16
LANE = 128
FAR = 1.0e4


def swap(block, axis, bit):
    devices = lax.axis_size(axis)
    return lax.ppermute(block, axis, [(i, i ^ bit) for i in range(devices)])


def from_behind(block, axis, distance):
    devices = range(lax.axis_size(axis))
    route = [(i - distance, i) for i in devices if i - distance in devices]
    return lax.ppermute(block, axis, route)


def bits_of(axis):
    count = lax.axis_size(axis)
    bits = []
    while (1 << len(bits)) < count:
        bits.append(1 << len(bits))
    return bits


def gather_last(block, axis):
    index = lax.axis_index(axis)
    whole = block
    for bit in reversed(bits_of(axis)):
        other = swap(whole, axis, bit)
        upper = (index & bit) != 0
        first = jnp.where(upper, other, whole)
        second = jnp.where(upper, whole, other)
        whole = jnp.stack([first, second], axis=0)
    count = len(bits_of(axis))
    order = tuple(reversed(range(count)))
    lead = whole.ndim - count
    whole = jnp.transpose(whole, order + tuple(range(count, whole.ndim)))
    whole = whole.reshape((lax.axis_size(axis),) + whole.shape[count:])
    moved = jnp.moveaxis(whole, 0, lead - 1)
    return moved.reshape(block.shape[:-1] + (-1,))


def sum_all(block, axis):
    total = block
    for bit in bits_of(axis):
        sent = total.astype(BF16)
        total = sent.astype(F32) + swap(sent, axis, bit).astype(F32)
    return total


def halves(block, upper):
    half = block.shape[0] // 2
    low, high = block[:half], block[half:]
    return jnp.where(upper, high, low), jnp.where(upper, low, high)


def scatter_sum(block, axis, bits):
    index = lax.axis_index(axis)
    total = block
    for bit in bits:
        kept, sent = halves(total, (index & bit) != 0)
        total = kept.astype(F32) + swap(sent.astype(BF16), axis, bit).astype(F32)
    return total


def spread(block, axis, bits):
    index = lax.axis_index(axis)
    whole = block
    for bit in reversed(bits):
        other = swap(whole, axis, bit)
        upper = (index & bit) != 0
        whole = jnp.concatenate(
            [jnp.where(upper, other, whole), jnp.where(upper, whole, other)], axis=0
        )
    return whole


def sum_rows(block, axis):
    bits = bits_of(axis)
    rows = block.shape[0]
    unit = 16 << len(bits)
    padded = -(-rows // unit) * unit
    if padded != rows:
        block = jnp.pad(block, ((0, padded - rows), (0, 0)))
    part = scatter_sum(block, axis, bits).astype(BF16)
    return spread(part, axis, bits)[:rows]


def silu_slope(values):
    logistic = jax.nn.sigmoid(values)
    return logistic * (1.0 + values * (1.0 - logistic))


def iota(shape, dim):
    return lax.broadcasted_iota(jnp.int32, shape, dim)


def widen(part, width):
    return jnp.concatenate([part] * (width // part.shape[1]), axis=1)


def ends_kernel(dt_ref, u_ref, gy_ref, b_ref, c_ref, a_ref, end_ref, pull_ref, prod):
    length, width = dt_ref.shape
    states = a_ref.shape[0]
    rate = a_ref[...] * LOG2E
    wide = CHUNK * states
    per_state = (iota((states, wide), 1) % states == iota((states, wide), 0)).astype(BF16)

    def chunk(i, carried):
        state, factor, pulled = carried
        for j in range(CHUNK):
            t = i * CHUNK + j

            def row(ref):
                return jnp.broadcast_to(ref[pl.ds(t, 1), :], (states, width))

            b, c = widen(b_ref[t], width), widen(c_ref[t], width)
            decay = jnp.exp2(row(dt_ref) * rate)
            state = decay * state + row(u_ref) * b
            factor = factor * decay
            prod[j * states : (j + 1) * states, :] = factor.astype(BF16) * (row(gy_ref) * c).astype(
                BF16
            )
        pulled = pulled + jnp.dot(per_state, prod[...], preferred_element_type=F32)
        return state, factor, pulled

    zero = jnp.zeros((states, width), F32)
    state, _, pulled = lax.fori_loop(0, length // CHUNK, chunk, (zero, zero + 1.0, zero))
    end_ref[...] = state
    pull_ref[...] = pulled


def scan_ends(dt, u, gy, b, c, rate):
    lanes, length, width = dt.shape
    states = rate.shape[0]
    token = pl.BlockSpec((None, length, width), lambda l: (l, 0, 0))
    column = pl.BlockSpec((None, length, states, LANE), lambda l: (l, 0, 0, 0))
    whole = pl.BlockSpec((states, width), lambda l: (0, 0))
    state = pl.BlockSpec((None, states, width), lambda l: (l, 0, 0))
    shape = jax.ShapeDtypeStruct((lanes, states, width), F32)
    return pl.pallas_call(
        ends_kernel,
        grid=(lanes,),
        in_specs=[token, token, token, column, column, whole],
        out_specs=[state, state],
        out_shape=[shape, shape],
        scratch_shapes=[pltpu.VMEM((CHUNK * states, width), BF16)],
        compiler_params=pltpu.CompilerParams(vmem_limit_bytes=40 << 20),
        name="scan_ends",
    )(dt, u, gy, b, c, rate)


def scan_kernel(
    dt_ref,
    u_ref,
    gy_ref,
    b_ref,
    c_ref,
    a_ref,
    begin_ref,
    last_ref,
    y_ref,
    gq_ref,
    gs_ref,
    ga_ref,
    gbc_ref,
    states_buf,
    p1,
    p2,
    p3,
    p4,
    p5,
):
    length, width = dt_ref.shape
    states = a_ref.shape[0]
    plain = a_ref[...]
    rate = plain * LOG2E
    rate_low = plain.astype(BF16)
    wide = CHUNK * states
    per_state = (iota((states, wide), 1) % states == iota((states, wide), 0)).astype(BF16)
    per_step = (iota((CHUNK, wide), 1) // states == iota((CHUNK, wide), 0)).astype(BF16)
    pick_b = (iota((wide, LANE), 0) % states + 64 == iota((wide, LANE), 1)).astype(F32)
    pick_c = (iota((wide, LANE), 0) % states + 80 == iota((wide, LANE), 1)).astype(F32)
    ones = jnp.ones((width, LANE), BF16)

    def row(ref, t):
        return jnp.broadcast_to(ref[pl.ds(t, 1), :], (states, width))

    def slot(t):
        return pl.ds(pl.multiple_of(t * states, states), states)

    begin = begin_ref[...]
    states_buf[0:states, :] = begin.astype(BF16)

    def forward(i, state):
        for j in range(CHUNK):
            t = i * CHUNK + j
            b, c = widen(b_ref[t], width), widen(c_ref[t].astype(BF16), width)
            state = jnp.exp2(row(dt_ref, t) * rate) * state + row(u_ref, t) * b
            low = state.astype(BF16)
            states_buf[slot(t + 1), :] = low
            p1[j * states : (j + 1) * states, :] = low * c
        y_ref[pl.ds(pl.multiple_of(i * CHUNK, CHUNK), CHUNK), :] = jnp.dot(
            per_step, p1[...], preferred_element_type=F32
        )
        return state

    lax.fori_loop(0, length // CHUNK, forward, begin)

    def backward(k, carried):
        carry, ga = carried
        i = length // CHUNK - 1 - k
        for j in reversed(range(CHUNK)):
            t = i * CHUNK + j
            b, c = widen(b_ref[t].astype(BF16), width), widen(c_ref[t], width)
            dt, gy, u = row(dt_ref, t), row(gy_ref, t), row(u_ref, t)
            grad = carry + gy * c
            carry = jnp.exp2(dt * rate) * grad
            low = grad.astype(BF16)
            turn = carry.astype(BF16) * states_buf[slot(t), :]
            s = slice(j * states, (j + 1) * states)
            p1[s, :] = turn * rate_low
            p2[s, :] = turn * dt.astype(BF16)
            p3[s, :] = low * b
            p4[s, :] = states_buf[slot(t + 1), :] * gy.astype(BF16)
            p5[s, :] = low * u.astype(BF16)
        o = pl.ds(pl.multiple_of(i * CHUNK, CHUNK), CHUNK)
        gq_ref[o, :] = jnp.dot(per_step, p1[...], preferred_element_type=F32)
        ga = ga + jnp.dot(per_state, p2[...], preferred_element_type=F32)
        gs_ref[o, :] = jnp.dot(per_step, p3[...], preferred_element_type=F32)
        sum_c = jnp.dot(p4[...], ones, preferred_element_type=F32)
        sum_b = jnp.dot(p5[...], ones, preferred_element_type=F32)
        picked = (sum_b * pick_b + sum_c * pick_c).astype(BF16)
        gbc_ref[o, :] = jnp.dot(per_step, picked, preferred_element_type=F32)
        return carry, ga

    zero = jnp.zeros((states, width), F32)
    _, ga = lax.fori_loop(0, length // CHUNK, backward, (last_ref[...], zero))
    ga_ref[...] = ga


def scan_all(dt, u, gy, b, c, rate, begin, last):
    lanes, length, width = dt.shape
    states = rate.shape[0]
    token = pl.BlockSpec((None, length, width), lambda l: (l, 0, 0))
    column = pl.BlockSpec((None, length, states, LANE), lambda l: (l, 0, 0, 0))
    whole = pl.BlockSpec((states, width), lambda l: (0, 0))
    state = pl.BlockSpec((None, states, width), lambda l: (l, 0, 0))
    narrow = pl.BlockSpec((None, length, LANE), lambda l: (l, 0, 0))
    shape = jax.ShapeDtypeStruct
    return pl.pallas_call(
        scan_kernel,
        grid=(lanes,),
        in_specs=[token, token, token, column, column, whole, state, state],
        out_specs=[token, token, token, state, narrow],
        out_shape=[shape((lanes, length, width), F32)] * 3
        + [shape((lanes, states, width), F32), shape((lanes, length, LANE), F32)],
        scratch_shapes=[pltpu.VMEM(((length + 1) * states, width), BF16)]
        + [pltpu.VMEM((CHUNK * states, width), BF16)] * 5,
        compiler_params=pltpu.CompilerParams(vmem_limit_bytes=40 << 20),
        name="scan_all",
    )(dt, u, gy, b, c, rate, begin, last)


def entering(end, pulled, reach, rate):
    index, count = lax.axis_index("seq"), lax.axis_size("seq")
    own = (end.astype(BF16), pulled.astype(BF16))
    got = {}
    for k in range(1, count):
        to_later = (index ^ k) > index
        sent = jnp.where(to_later, own[0], own[1])
        got[k] = (swap(sent, "seq", k), swap(reach, "seq", k))
    states = jnp.stack([jnp.zeros_like(own[0])] + [got[k][0] for k in range(1, count)])
    spans = jnp.stack([jnp.zeros_like(reach)] + [got[k][1] for k in range(1, count)])
    order = jnp.arange(count) ^ index
    states, spans = states[order], spans[order]
    begin = jnp.zeros(end.shape, F32)
    last = jnp.zeros(end.shape, F32)
    for g in range(count):
        factor = jnp.exp(spans[g][:, None, :] * rate)
        begin = jnp.where(g < index, begin * factor + states[g].astype(F32), begin)
        h = count - 1 - g
        factor = jnp.exp(spans[h][:, None, :] * rate)
        last = jnp.where(h > index, last * factor + states[h].astype(F32), last)
    return begin, last


def per_device(
    inputs,
    row_starts,
    norm_gain,
    in_weight,
    conv_weight,
    conv_bias,
    xproj_weight,
    dtproj_weight,
    dt_bias,
    decay_log,
    skip_gain,
    out_weight,
    output_grad,
):
    lane_count, length, shard_width = inputs.shape
    low_rank = dtproj_weight.shape[0]
    state_count = decay_log.shape[0]
    tap_count = conv_weight.shape[0]
    inner_width = conv_bias.shape[0]
    model_width = norm_gain.shape[0]
    starts = row_starts.astype(F32)
    carry_mask = (1.0 - starts)[:, :, None]
    mp_index = lax.axis_index("mp")
    gathered = gather_last(inputs.astype(BF16), "mp").astype(F32)
    inv_rms = lax.rsqrt(jnp.mean(gathered * gathered, axis=2, keepdims=True) + 1e-05)
    normed = (gathered * inv_rms * norm_gain).astype(BF16)
    grad_whole = gather_last(output_grad.astype(BF16), "mp")
    w_in = in_weight.astype(BF16)
    inner_act = jnp.einsum("ltd,de->lte", normed, w_in[0], preferred_element_type=F32).astype(BF16)
    rim_rows = from_behind(inner_act[:, length - (tap_count - 1) :, :], "seq", 1)
    gate_in = jnp.einsum("ltd,de->lte", normed, w_in[1], preferred_element_type=F32)
    rim_rows = rim_rows.astype(F32) * carry_mask
    padded = jnp.concatenate([rim_rows, inner_act.astype(F32)], axis=1)
    conv_sum = conv_bias + conv_weight[0] * padded[:, 0:length]
    for tap in range(1, tap_count):
        conv_sum = conv_sum + conv_weight[tap] * padded[:, tap : tap + length]
    mixed = jax.nn.silu(conv_sum)
    mixed_low = mixed.astype(BF16)
    w_x = xproj_weight.astype(BF16)
    projected = sum_all(
        jnp.einsum("lte,er->ltr", mixed_low, w_x, preferred_element_type=F32), "mp"
    )
    dt_low = projected[:, :, :low_rank].astype(BF16)
    input_mat = projected[:, :, low_rank : low_rank + state_count]
    read_mat = projected[:, :, low_rank + state_count :]
    w_dt = dtproj_weight.astype(BF16)
    dt_pre = jnp.einsum("ltr,re->lte", dt_low, w_dt, preferred_element_type=F32) + dt_bias
    step_size = jax.nn.softplus(dt_pre)
    decay_rate = -jnp.exp(decay_log)
    w_out = out_weight.astype(BF16)
    gate_act = jax.nn.silu(gate_in)
    grad_gated = jnp.einsum("ltd,ed->lte", grad_whole, w_out, preferred_element_type=F32)
    grad_scan = grad_gated * gate_act
    source = step_size * mixed
    wide = input_mat.shape + (LANE,)
    b_wide = jnp.broadcast_to(input_mat[..., None], wide)
    c_wide = jnp.broadcast_to(read_mat[..., None], wide)
    end_state, pulled = scan_ends(step_size, source, grad_scan, b_wide, c_wide, decay_rate)
    reach = jnp.sum(step_size, axis=1) + FAR * starts
    begin, last = entering(end_state, pulled * carry_mask, reach, decay_rate)
    y, turn_sum, pull_sum, grad_rate, grad_bc = scan_all(
        step_size, source, grad_scan, b_wide, c_wide, decay_rate, begin * carry_mask, last
    )
    scan_out = y + skip_gain * mixed
    gated = (scan_out * gate_act).astype(BF16)
    out_part = jnp.einsum("lte,ed->ltd", gated, w_out, preferred_element_type=F32)
    blocks = jnp.moveaxis(
        out_part.reshape(lane_count, length, -1, shard_width), 2, 0
    )
    mp_bits = bits_of("mp")
    branch = scatter_sum(blocks, "mp", mp_bits[::-1])[0]
    output = inputs + branch
    grad_out_w = jnp.einsum("lte,ltd->ed", gated, grad_whole, preferred_element_type=F32)
    grad_gate = grad_gated * scan_out * silu_slope(gate_in)
    grad_skip = jnp.sum(grad_scan * mixed, axis=(0, 1))
    grad_step = turn_sum + pull_sum * mixed
    grad_mixed = pull_sum * step_size + grad_scan * skip_gain
    grad_log = jnp.sum(grad_rate, axis=0) * decay_rate
    slope_pre = grad_step * jax.nn.sigmoid(dt_pre)
    grad_bias_dt = jnp.sum(slope_pre, axis=(0, 1))
    grad_pre = slope_pre.astype(BF16)
    grad_dt_w = jnp.einsum("ltr,lte->re", dt_low, grad_pre, preferred_element_type=F32)
    grad_dt_low = jnp.einsum("lte,re->ltr", grad_pre, w_dt, preferred_element_type=F32)
    narrow = low_rank + 2 * state_count
    grad_proj_part = jnp.concatenate([grad_dt_low, grad_bc[:, :, low_rank:narrow]], axis=2)
    grad_projected = sum_all(grad_proj_part, "mp").astype(BF16)
    grad_x_w = jnp.einsum("ltr,lte->re", grad_projected, mixed_low, preferred_element_type=F32)
    grad_mixed = grad_mixed + jnp.einsum(
        "ltr,er->lte", grad_projected, w_x, preferred_element_type=F32
    )
    grad_conv = grad_mixed * silu_slope(conv_sum)
    grad_conv_b = jnp.sum(grad_conv, axis=(0, 1))
    grad_conv_w = jnp.stack(
        [
            jnp.sum(grad_conv * padded[:, tap : tap + length], axis=(0, 1))
            for tap in range(tap_count)
        ]
    )
    grad_padded = jnp.pad(conv_weight[0] * grad_conv, ((0, 0), (0, tap_count - 1), (0, 0)))
    for tap in range(1, tap_count):
        grad_padded = grad_padded + jnp.pad(
            conv_weight[tap] * grad_conv, ((0, 0), (tap, tap_count - 1 - tap), (0, 0))
        )
    rim_back = from_behind(grad_padded[:, : tap_count - 1] * carry_mask, "seq", -1)
    tail_zeros = jnp.zeros((lane_count, length - (tap_count - 1), inner_width), F32)
    grad_inner = grad_padded[:, tap_count - 1 :] + jnp.concatenate([tail_zeros, rim_back], axis=1)
    grad_inner_low = grad_inner.astype(BF16)
    grad_gate_low = grad_gate.astype(BF16)
    grad_in_w = [
        jnp.einsum("ltd,lte->de", normed, part, preferred_element_type=F32)
        for part in (grad_inner_low, grad_gate_low)
    ]
    grad_normed = jnp.einsum(
        "lte,de->ltd", grad_inner_low, w_in[0], preferred_element_type=F32
    ) + jnp.einsum("lte,de->ltd", grad_gate_low, w_in[1], preferred_element_type=F32)
    row_part = jnp.sum(
        grad_inner_low.astype(F32) * inner_act.astype(F32)
        + grad_gate_low.astype(F32) * gate_in,
        axis=2,
    )
    row_dot = row_part
    for bit in mp_bits:
        row_dot = row_dot + swap(row_dot, "mp", bit)
    blocks = jnp.moveaxis(grad_normed.reshape(lane_count, length, -1, shard_width), 2, 0)
    grad_own = scatter_sum(blocks, "mp", mp_bits[::-1])[0]
    own_gain = lax.dynamic_slice_in_dim(norm_gain, mp_index * shard_width, shard_width, 0)
    unit_own = inputs * inv_rms
    grad_gain = jnp.sum(grad_own * unit_own, axis=(0, 1))
    input_grad = output_grad + inv_rms * (
        grad_own * own_gain - unit_own * (row_dot[:, :, None] / model_width)
    )
    gain_rows = jnp.pad(grad_gain, (0, -shard_width % inner_width)).reshape(-1, inner_width)
    small = jnp.concatenate(
        [
            grad_conv_w,
            grad_conv_b[None],
            grad_bias_dt[None],
            grad_skip[None],
            grad_log,
            grad_dt_w,
            grad_x_w,
            gain_rows,
        ],
        axis=0,
    )
    sum_out_w = sum_rows(grad_out_w, "seq").astype(F32)
    sum_gate_w = sum_rows(grad_in_w[1], "seq").astype(F32)
    sum_inner_w = sum_rows(grad_in_w[0], "seq").astype(F32)
    small = sum_rows(small, "seq").astype(F32)
    cuts = [tap_count, 1, 1, 1, state_count, low_rank, narrow, gain_rows.shape[0]]
    parts, at = [], 0
    for size in cuts:
        parts.append(small[at : at + size])
        at += size
    return (
        output,
        input_grad,
        parts[7].reshape(-1)[:shard_width],
        jnp.stack([sum_inner_w, sum_gate_w]),
        parts[0],
        parts[1][0],
        parts[6].T,
        parts[5],
        parts[2][0],
        parts[4],
        parts[3][0],
        sum_out_w,
    )


def solution(mesh):
    in_specs = (
        P(None, "seq", "mp"),
        P(None, "seq"),
        P(),
        P(None, None, "mp"),
        P(None, "mp"),
        P("mp"),
        P("mp", None),
        P(None, "mp"),
        P("mp"),
        P(None, "mp"),
        P("mp"),
        P("mp", None),
        P(None, "seq", "mp"),
    )
    out_specs = (
        P(None, "seq", "mp"),
        P(None, "seq", "mp"),
        P("mp"),
        P(None, None, "mp"),
        P(None, "mp"),
        P("mp"),
        P("mp", None),
        P(None, "mp"),
        P("mp"),
        P(None, "mp"),
        P("mp"),
        P("mp", None),
    )
    return jax.shard_map(
        per_device, mesh=mesh, in_specs=in_specs, out_specs=out_specs, check_vma=False
    )
```

```python
import functools

import jax
import jax.numpy as jnp
from jax import lax
from jax.experimental import pallas as pl
from jax.experimental.pallas import tpu as pltpu
from jax.sharding import PartitionSpec as P

F32 = jnp.float32
BF16 = jnp.bfloat16
LOG2E = 1.4426950408889634
CHUNK = 32
LANE = 128
FAR = 1.0e4
VMEM = pl.BlockSpec(memory_space=pltpu.VMEM)


def swap(block, axis, bit):
    devices = lax.axis_size(axis)
    return lax.ppermute(block, axis, [(i, i ^ bit) for i in range(devices)])


def from_behind(block, axis, distance):
    devices = range(lax.axis_size(axis))
    route = [(i - distance, i) for i in devices if i - distance in devices]
    return lax.ppermute(block, axis, route)


def bits_of(axis):
    count = lax.axis_size(axis)
    bits = []
    while (1 << len(bits)) < count:
        bits.append(1 << len(bits))
    return bits


def after(array, *others):
    return lax.optimization_barrier((array, *others))[0]


def hop(kept, sent, axis, bit):
    total = kept.astype(F32) + swap(sent, axis, bit).astype(F32)
    half = total.shape[-1] // 2
    return total[..., :half], total[..., half:].astype(BF16)


class Reduction:
    def __init__(self):
        self.bits = bits_of("seq")
        self.orders = [list(self.bits), list(self.bits)]
        if len(self.bits) > 1:
            self.orders[1][:2] = self.bits[1], self.bits[0]
        self.index = lax.axis_index("seq")
        self.odd = lax.axis_index("mp") % 2
        self.mp = lax.axis_size("mp")
        self.count = lax.axis_size("seq")

    def own(self, step):
        even = (self.index & self.orders[0][step]) != 0
        odd = (self.index & self.orders[1][step]) != 0
        return jnp.where(self.odd == 1, odd, even).astype(jnp.int32)

    def swap(self, block, step):
        route = []
        for s in range(self.count):
            for m in range(self.mp):
                route.append((s * self.mp + m, (s ^ self.orders[m % 2][step]) * self.mp + m))
        return lax.ppermute(block, ("seq", "mp"), route)

    def halves(self, block, step):
        half = block.shape[0] // 2
        up = self.own(step)
        kept = lax.dynamic_slice_in_dim(block, up * half, half, 0)
        sent = lax.dynamic_slice_in_dim(block, (1 - up) * half, half, 0)
        return kept, sent

    def part(self, left, right, up):
        half = left.shape[2] // 2
        cut = lax.dynamic_slice_in_dim(left, up * half, half, 2)
        return jnp.einsum("lta,ltb->ab", cut, right, preferred_element_type=F32)

    def sent(self, left, right):
        return self.part(left, right, 1 - self.own(0)).astype(BF16)

    def kept(self, left, right):
        return self.part(left, right, self.own(0))

    def place(self):
        place = jnp.int32(0)
        for step in range(1, len(self.bits)):
            place = place * 2 + self.own(step)
        return place

    def order(self, per, turn):
        blocks = self.count // 2
        pieces = blocks // per
        at = jnp.arange(blocks)
        low, high = turn % pieces, turn // pieces
        source = (((at // per) ^ low) * per + at % per) ^ self.place()
        up = self.own(0) ^ high
        return jnp.concatenate([jnp.stack([up * blocks, (1 - up) * blocks]), source]).astype(jnp.int32)


class Sum:
    def __init__(self, over, sent, count):
        self.over, self.count, self.kept = over, count, None
        self.step, self.down = 0, False
        self.sent = sent
        self.got = over.swap(sent, 0)

    def split(self, block):
        rows = block.shape[0] // self.count
        return [block[k * rows : (k + 1) * rows] for k in range(self.count)]

    def over_now(self):
        return self.down and self.step == 0

    def next(self, *earlier):
        over, steps = self.over, len(self.over.bits)
        if earlier:
            self.got = after(self.got, *earlier)
        got = self.split(self.got)
        if not self.down:
            self.step += 1
            if self.step < steps:
                sent = []
                for k in range(self.count):
                    own, other = over.halves(self.kept[k], self.step), over.halves(got[k], self.step)
                    self.kept[k] = own[0].astype(F32) + other[0].astype(F32)
                    sent.append((own[1].astype(F32) + other[1].astype(F32)).astype(BF16))
                self.sent = jnp.concatenate(sent, axis=0)
            else:
                self.down = True
                self.whole = [(a.astype(F32) + b.astype(F32)).astype(BF16) for a, b in zip(self.kept, got, strict=True)]
                self.step -= 1
        else:
            self.whole = [jnp.concatenate(pair, axis=0) for pair in zip(self.whole, got, strict=True)]
            self.step -= 1
        if self.down:
            self.sent = jnp.concatenate(self.whole, axis=0)
        self.got = over.swap(self.sent, self.step)
        return self.sent

    def finish(self):
        while not self.over_now():
            self.next()
        return self.whole, self.split(self.got)


def silu_slope(values):
    logistic = jax.nn.sigmoid(values)
    return logistic * (1.0 + values * (1.0 - logistic))


def cost(ops, lanes, length, width, states):
    work = lanes * length * width * states
    return pl.CostEstimate(flops=ops * work * 16, bytes_accessed=work * 2, transcendentals=work)


def settle_kernel(names, layout, order_ref, *refs):
    parts, outs = refs[: len(layout)], refs[-2 - names : -2]
    wide, sems = refs[-2:]
    copies, at = [], 0
    for part, (out, lead, which, first, blocks, turned) in zip(parts, layout, strict=True):
        size = part.shape[0] // blocks
        for b in range(blocks):
            source = order_ref[which + 2 + b]
            rows = part[pl.ds(pl.multiple_of(source * size, size), size), :].astype(F32)
            goal = pl.multiple_of((order_ref[which + first] + b) * size, size)
            ref = outs[out] if lead is None else outs[out].at[lead]
            if turned:
                rows = jnp.transpose(rows)
                spot = wide.at[at : at + rows.shape[0], 0:size]
                target = ref.at[:, pl.ds(goal, size)]
            else:
                spot = wide.at[at : at + size, 0 : part.shape[1]]
                target = ref.at[pl.ds(goal, size), :]
            spot[...] = rows
            at += rows.shape[0]
            copies.append(pltpu.make_async_copy(spot, target, sems.at[len(copies)]))
            copies[-1].start()
    for copy in copies:
        copy.wait()


def settle(orders, parts, layout, shapes, into=()):
    any_space = pl.BlockSpec(memory_space=pl.ANY)
    rows = sum(p.shape[1] * l[4] if l[5] else p.shape[0] for p, l in zip(parts, layout, strict=True))
    width = max(p.shape[0] // l[4] if l[5] else p.shape[1] for p, l in zip(parts, layout, strict=True))
    count = sum(l[4] for l in layout)
    return pl.pallas_call(
        functools.partial(settle_kernel, len(shapes), layout),
        in_specs=[pl.BlockSpec(memory_space=pltpu.SMEM)] + [VMEM] * len(parts) + [any_space] * len(into),
        out_specs=[any_space] * len(shapes),
        out_shape=[jax.ShapeDtypeStruct(s, F32) for s in shapes],
        input_output_aliases={1 + len(parts) + k: k for k in range(len(into))},
        scratch_shapes=[pltpu.VMEM((rows, width), F32), pltpu.SemaphoreType.DMA((count,))],
        compiler_params=pltpu.CompilerParams(vmem_limit_bytes=16 << 20),
        name="settle",
    )(orders, *parts, *into)


def iota(shape, dim):
    return lax.broadcasted_iota(jnp.int32, shape, dim)


def widen(part, width):
    return jnp.concatenate([part] * (width // part.shape[1]), axis=1)


def dot(a, b):
    return jnp.dot(a, b, preferred_element_type=F32)


def dot_t(a, b):
    return lax.dot_general(a, b, (((1,), (1,)), ((), ())), preferred_element_type=F32)


def row_of(ref, t, count):
    return jnp.broadcast_to(ref[pl.ds(t, 1), :], (count, ref.shape[1]))


def rows_of(i, count):
    return pl.ds(pl.multiple_of(i * count, count), count)


def chunk_columns(ref, i):
    per = LANE // CHUNK
    tile = ref[:, rows_of(i // per, LANE)]
    return pltpu.roll(tile, LANE - (i % per) * CHUNK, 1)


def spread_column(tile, j, width):
    part = jnp.broadcast_to(tile[:, j : j + 1], (tile.shape[0], LANE))
    return widen(part, width)


def selectors(states):
    wide = CHUNK * states
    per_state = iota((states, wide), 1) % states == iota((states, wide), 0)
    per_step = iota((CHUNK, wide), 1) // states == iota((CHUNK, wide), 0)
    return per_state.astype(F32), per_step.astype(F32)


def from_lanes(first, states):
    shape = (LANE, CHUNK * states)
    return (iota(shape, 0) == first + iota(shape, 1) % states).astype(BF16)


def to_lanes(first, states):
    shape = (CHUNK * states, LANE)
    return (iota(shape, 1) == first + iota(shape, 0) % states).astype(BF16)


def by_step(proj, lanes, per_step):
    spread = dot(proj, lanes)
    return spread * jnp.concatenate([per_step] * (spread.shape[0] // CHUNK), axis=0)


def ends_kernel(
    low_rank, sent_ref, got_ref, wdt_ref, bias_ref, log_ref, mixed_ref, gy_ref,
    end_ref, pull_ref, span_ref, dt_ref, u_ref, sig_ref, proj_ref,
    ahead, behind, left_b, left_c, xa, xb, ya, yb,
):
    length, width = dt_ref.shape
    states = log_ref.shape[0]
    rate = -jnp.exp(log_ref[...]) * LOG2E
    per_state, per_step = selectors(states)
    chunks = length // CHUNK
    upto = (iota((length, length), 1) <= iota((length, length), 0)).astype(BF16)
    after = (iota((length, length), 1) > iota((length, length), 0)).astype(BF16)
    proj = sent_ref[...].astype(F32) + got_ref[...].astype(F32)
    proj_ref[...] = proj
    proj = proj.astype(BF16)
    for first, left in ((low_rank, left_b), (low_rank + states, left_c)):
        spread = by_step(proj, from_lanes(first, states), per_step)
        for i in range(chunks):
            flat = jnp.sum(spread[i * CHUNK : (i + 1) * CHUNK], axis=0, keepdims=True)
            left[i * states : (i + 1) * states, :] = (flat * per_state).astype(BF16)
    block = min(128, length)
    for i in range(length // block):
        o = slice(i * block, (i + 1) * block)
        pre = dot(proj[o], wdt_ref[...]) + bias_ref[...]
        small = jnp.exp(-jnp.abs(pre))
        one = 1.0 + small
        series = small * (1.0 - small * (0.5 - small * (1.0 / 3.0)))
        dt = jnp.maximum(pre, 0.0) + jnp.where(small < 1e-3, series, jnp.log(one))
        dt_ref[o, :] = dt
        u_ref[o, :] = dt * mixed_ref[o, :]
        sig_ref[o, :] = jnp.where(pre >= 0.0, 1.0, small) / one
    dt = dt_ref[...]
    high = dt.astype(BF16)
    low = (dt - high.astype(F32)).astype(BF16)
    ahead[...] = dot(upto, high) + dot(upto, low)
    behind[...] = dot(after, high) + dot(after, low)
    span_ref[...] = ahead[length - 1 : length, :]
    xb[...] = jnp.zeros(xb.shape, BF16)
    yb[...] = jnp.zeros(yb.shape, BF16)

    def flush(i, x, y, sums):
        o = rows_of(jnp.maximum(i, 0), states)
        return sums[0] + dot(left_b[o, :], x[...]), sums[1] + dot(left_c[o, :], y[...])

    def fill(i, x, y):
        for j in range(CHUNK):
            t = i * CHUNK + j
            s = slice(j * states, (j + 1) * states)
            to_end = jnp.exp2(row_of(behind, t, states) * rate)
            x[s, :] = (to_end * row_of(u_ref, t, states)).astype(BF16)
            to_here = jnp.exp2(row_of(ahead, t, states) * rate)
            y[s, :] = (to_here * row_of(gy_ref, t, states)).astype(BF16)

    def body(k, sums):
        sums = flush(2 * k - 1, xb, yb, sums)
        fill(2 * k, xa, ya)
        sums = flush(2 * k, xa, ya, sums)
        fill(2 * k + 1, xb, yb)
        return sums

    zero = jnp.zeros((states, width), F32)
    sums = lax.fori_loop(0, chunks // 2, body, (zero, zero))
    sums = flush(chunks - 1, xb, yb, sums)
    end_ref[...] = sums[0]
    pull_ref[...] = sums[1]


def lane_spec(*shape):
    return pl.BlockSpec((None, *shape), lambda l: (l,) + (0,) * len(shape))


def whole_spec(*shape):
    return pl.BlockSpec(shape, lambda l: (0,) * len(shape))


def scan_ends(low_rank, sent, got, w_dt, bias, log, mixed, gy):
    lanes, length, width = mixed.shape
    states = log.shape[0]
    shape = jax.ShapeDtypeStruct
    token = shape((lanes, length, width), F32)
    state = shape((lanes, states, width), F32)
    tokens, state_spec, narrow = lane_spec(length, width), lane_spec(states, width), lane_spec(length, LANE)
    return pl.pallas_call(
        functools.partial(ends_kernel, low_rank),
        grid=(lanes,),
        in_specs=[
            narrow,
            narrow,
            whole_spec(*w_dt.shape),
            whole_spec(1, width),
            whole_spec(states, width),
            tokens,
            tokens,
        ],
        out_specs=[state_spec, state_spec, lane_spec(1, width), tokens, tokens, tokens, narrow],
        out_shape=[state, state, shape((lanes, 1, width), F32), token, token, token, shape(sent.shape, F32)],
        scratch_shapes=[pltpu.VMEM((length, width), F32)] * 2
        + [pltpu.VMEM((length // CHUNK * states, CHUNK * states), BF16)] * 2
        + [pltpu.VMEM((CHUNK * states, width), BF16)] * 4,
        compiler_params=pltpu.CompilerParams(vmem_limit_bytes=24 << 20),
        cost_estimate=cost(8, lanes, length, width, states),
        name="scan_ends",
    )(sent, got, w_dt, bias, log, mixed, gy)


def forward_kernel(
    low_rank, lanes, place_ref, proj_ref, log_ref, dt_ref, u_ref, gy_ref, got_ref,
    y_ref, gc_ref, last_ref, hs_ref,
    pa, pb, p0, cols, left_c, masked, sems,
):
    length, width = dt_ref.shape
    states = log_ref.shape[0]
    l = pl.program_id(0)
    rate = -jnp.exp(log_ref[...]) * LOG2E
    _, per_step = selectors(states)
    wide = CHUNK * states
    chunks = length // CHUNK
    groups = got_ref.shape[0]
    place = place_ref[0]

    def leave(i, p, at):
        rows = pl.ds(pl.multiple_of((i * CHUNK + 1) * states, states), wide)
        return pltpu.make_async_copy(p, hs_ref.at[l, rows, :], sems.at[at])

    zero = jnp.zeros((states, width), F32)

    def join(g, total, use):
        at = lanes * states
        spans = got_ref[g, at : at + lanes, :].astype(F32)
        span = jnp.sum(jnp.where(iota(spans.shape, 0) == l, spans, 0.0), axis=0, keepdims=True)
        factor = jnp.exp2(span * rate)
        return jnp.where(use, total * factor + got_ref[g, rows_of(l, states), :].astype(F32), total)

    begin = last = zero
    for g in range(groups):
        begin = join(g, begin, g < place)
        h = groups - 1 - g
        last = join(h, last, h > place)
    last_ref[...] = last
    begin = jnp.where(place_ref[1 + l] != 0, 0.0, begin)
    p0[...] = begin.astype(BF16)
    first = pltpu.make_async_copy(p0, hs_ref.at[l, pl.ds(0, states), :], sems.at[2])
    first.start()
    proj = proj_ref[...]
    cols[...] = jnp.transpose(proj)[low_rank : low_rank + states]
    spread = by_step(proj.astype(BF16), from_lanes(low_rank + states, states), per_step)
    left_c[...] = spread.astype(BF16)

    def flush(i, p):
        o = rows_of(jnp.maximum(i, 0), CHUNK)
        h = p[...]
        y_ref[o, :] = dot(left_c[o, :], h)
        masked[o, :] = (dot_t(gy_ref[o, :].astype(BF16), h) * per_step).astype(BF16)

    def fill(i, state, p):
        b_tile = chunk_columns(cols, i)
        for j in range(CHUNK):
            t = i * CHUNK + j
            b = spread_column(b_tile, j, width)
            decay = jnp.exp2(row_of(dt_ref, t, states) * rate)
            state = decay * state + row_of(u_ref, t, states) * b
            p[j * states : (j + 1) * states, :] = state.astype(BF16)
        return state

    def body(k, state):
        @pl.when(k > 0)
        def _():
            leave(2 * k - 2, pa, 0).wait()

        flush(2 * k - 1, pb)
        state = fill(2 * k, state, pa)
        leave(2 * k, pa, 0).start()

        @pl.when(k > 0)
        def _():
            leave(2 * k - 1, pb, 1).wait()

        flush(2 * k, pa)
        state = fill(2 * k + 1, state, pb)
        leave(2 * k + 1, pb, 1).start()
        return state

    lax.fori_loop(0, chunks // 2, body, begin)
    flush(chunks - 1, pb)
    gc_ref[...] = dot(masked[...], to_lanes(low_rank + states, states))
    leave(chunks - 2, pa, 0).wait()
    leave(chunks - 1, pb, 1).wait()
    first.wait()


def scan_forward(low_rank, place, proj, log, dt, u, gy, got):
    lanes, length, width = dt.shape
    states = log.shape[0]
    shape = jax.ShapeDtypeStruct
    tokens, state_spec, narrow = lane_spec(length, width), lane_spec(states, width), lane_spec(length, LANE)
    return pl.pallas_call(
        functools.partial(forward_kernel, low_rank, lanes),
        grid=(lanes,),
        in_specs=[
            pl.BlockSpec(memory_space=pltpu.SMEM),
            narrow,
            whole_spec(states, width),
            tokens,
            tokens,
            tokens,
            whole_spec(*got.shape),
        ],
        out_specs=[tokens, narrow, state_spec, pl.BlockSpec(memory_space=pltpu.HBM)],
        out_shape=[
            shape((lanes, length, width), F32),
            shape(proj.shape, F32),
            shape((lanes, states, width), F32),
            shape((lanes, (length + 1) * states, width), BF16),
        ],
        scratch_shapes=[pltpu.VMEM((CHUNK * states, width), BF16)] * 2
        + [
            pltpu.VMEM((states, width), BF16),
            pltpu.VMEM((states, length), F32),
            pltpu.VMEM((length, CHUNK * states), BF16),
            pltpu.VMEM((length, CHUNK * states), BF16),
            pltpu.SemaphoreType.DMA((3,)),
        ],
        compiler_params=pltpu.CompilerParams(vmem_limit_bytes=24 << 20),
        cost_estimate=cost(8, lanes, length, width, states),
        name="scan_forward",
    )(place, proj, log, dt, u, gy, got)


def backward_kernel(
    low_rank, proj_ref, log_ref, dt_ref, u_ref, gy_ref, last_ref, gc_ref, hs_ref, *refs
):
    (turn_ref, pull_ref, gbc_ref, ga_ref,
     ha, hb, pa, pb, qa, qb, ra, rb, cols, left_b, masked, sems) = refs[-16:]
    length, width = dt_ref.shape
    states = log_ref.shape[0]
    l = pl.program_id(0)
    plain = -jnp.exp(log_ref[...])
    rate = plain * LOG2E
    rate_low = plain.astype(BF16)
    per_state, per_step = selectors(states)
    per_state_low, per_step_low = per_state.astype(BF16), per_step.astype(BF16)
    chunks = length // CHUNK
    wide = CHUNK * states

    def enter(i, h, at):
        return pltpu.make_async_copy(hs_ref.at[l, rows_of(i, wide), :], h, sems.at[at])

    enter(chunks - 1, ha, 0).start()
    for ref in (pb, qb, rb):
        ref[...] = jnp.zeros(ref.shape, BF16)
    proj = proj_ref[...]
    cols[...] = jnp.transpose(proj)[low_rank + states : low_rank + 2 * states]
    left_b[...] = by_step(proj.astype(BF16), from_lanes(low_rank, states), per_step).astype(BF16)

    def flush(i, p, q, r, ga):
        o = rows_of(jnp.minimum(i, chunks - 1), CHUNK)
        grad = p[...]
        pull_ref[o, :] = dot(left_b[o, :], grad)
        masked[o, :] = (dot_t(u_ref[o, :].astype(BF16), grad) * per_step).astype(BF16)
        turn_ref[o, :] = dot(per_step_low, q[...])
        return ga + dot(per_state_low, r[...])

    def fill(i, carry, h, p, q, r):
        c_tile = chunk_columns(cols, i)
        for j in reversed(range(CHUNK)):
            t = i * CHUNK + j
            s = slice(j * states, (j + 1) * states)
            c = spread_column(c_tile, j, width)
            dt = row_of(dt_ref, t, states)
            grad = carry + row_of(gy_ref, t, states) * c
            carry = jnp.exp2(dt * rate) * grad
            p[s, :] = grad.astype(BF16)
            turn = carry.astype(BF16) * h[s, :] * rate_low
            q[s, :] = turn
            r[s, :] = turn * dt.astype(BF16)
        return carry

    def body(k, carried):
        carry, ga = carried
        i = chunks - 1 - 2 * k
        enter(i, ha, 0).wait()
        enter(i - 1, hb, 1).start()
        ga = flush(i + 1, pb, qb, rb, ga)
        carry = fill(i, carry, ha, pa, qa, ra)
        enter(i - 1, hb, 1).wait()

        @pl.when(i > 1)
        def _():
            enter(i - 2, ha, 0).start()

        ga = flush(i, pa, qa, ra, ga)
        carry = fill(i - 1, carry, hb, pb, qb, rb)
        return carry, ga

    zero = jnp.zeros((states, width), F32)
    _, ga = lax.fori_loop(0, chunks // 2, body, (last_ref[...], zero))
    ga_ref[...] = flush(0, pb, qb, rb, ga)
    gbc_ref[...] = gc_ref[...] + dot(masked[...], to_lanes(low_rank, states))


def scan_backward(low_rank, proj, log, dt, u, gy, last, gc, hs, *earlier):
    lanes, length, width = dt.shape
    states = log.shape[0]
    shape = jax.ShapeDtypeStruct
    tokens, state_spec, narrow = lane_spec(length, width), lane_spec(states, width), lane_spec(length, LANE)
    token = shape((lanes, length, width), F32)
    return pl.pallas_call(
        functools.partial(backward_kernel, low_rank),
        grid=(lanes,),
        in_specs=[narrow, whole_spec(states, width), tokens, tokens, tokens, state_spec, narrow]
        + [pl.BlockSpec(memory_space=pltpu.HBM)]
        + [pl.BlockSpec(memory_space=pl.ANY)] * len(earlier),
        out_specs=[tokens, tokens, narrow, state_spec],
        out_shape=[token, token, shape(proj.shape, F32), shape((lanes, states, width), F32)],
        scratch_shapes=[pltpu.VMEM((CHUNK * states, width), BF16)] * 8
        + [
            pltpu.VMEM((states, length), F32),
            pltpu.VMEM((length, CHUNK * states), BF16),
            pltpu.VMEM((length, CHUNK * states), BF16),
            pltpu.SemaphoreType.DMA((2,)),
        ],
        compiler_params=pltpu.CompilerParams(vmem_limit_bytes=24 << 20),
        cost_estimate=cost(12, lanes, length, width, states),
        name="scan_backward",
    )(proj, log, dt, u, gy, last, gc, hs, *earlier)


def per_device(
    inputs,
    row_starts,
    norm_gain,
    in_weight,
    conv_weight,
    conv_bias,
    xproj_weight,
    dtproj_weight,
    dt_bias,
    decay_log,
    skip_gain,
    out_weight,
    output_grad,
):
    lane_count, length, shard_width = inputs.shape
    low_rank = dtproj_weight.shape[0]
    state_count = decay_log.shape[0]
    tap_count = conv_weight.shape[0]
    inner_width = conv_bias.shape[0]
    model_width = norm_gain.shape[0]
    starts = row_starts.astype(F32)
    carry_mask = (1.0 - starts)[:, :, None]
    mp_index, mp_size = lax.axis_index("mp"), lax.axis_size("mp")
    seq_index, seq_size = lax.axis_index("seq"), lax.axis_size("seq")
    mp_bits, seq_bits = bits_of("mp"), bits_of("seq")
    near_first = [int(format(k, "0%db" % len(mp_bits))[::-1], 2) for k in range(mp_size)]

    def blocks(array, axis, order):
        parts = [
            lax.dynamic_slice_in_dim(array, (mp_index ^ k) * shard_width, shard_width, axis) for k in order
        ]
        return jnp.concatenate(parts, axis=axis)

    x_parts, grad_parts = {0: inputs.astype(BF16)}, {}
    square = jnp.sum(jnp.square(inputs), axis=2)
    for bit in reversed(mp_bits):
        for k in list(x_parts):
            x_parts[k | bit] = swap(x_parts[k], "mp", bit)
        square = square + swap(square, "mp", bit)
    grad_parts[0] = after(output_grad.astype(BF16), x_parts[mp_bits[-1]])
    for bit in reversed(mp_bits):
        for k in list(grad_parts):
            grad_parts[k | bit] = swap(grad_parts[k], "mp", bit)
    near = list(range(mp_size))
    w_in = blocks(in_weight, 1, near).astype(BF16)
    w_back = blocks(in_weight, 1, near_first).astype(BF16)
    w_out = out_weight.astype(BF16)
    w_spread = blocks(out_weight, 1, near_first).astype(BF16)
    gain = blocks(norm_gain, 0, near)
    w_x = jnp.pad(xproj_weight.astype(BF16), ((0, 0), (0, -xproj_weight.shape[1] % LANE)))
    w_dt = jnp.pad(dtproj_weight.astype(BF16), ((0, -low_rank % LANE), (0, 0)))
    inv_rms = lax.rsqrt(square[:, :, None] / model_width + 1e-05)
    x_whole = jnp.concatenate([x_parts[k] for k in near], axis=2)
    normed = (x_whole.astype(F32) * inv_rms * gain).astype(BF16)
    inner_act = jnp.einsum("ltd,de->lte", normed, w_in[0], preferred_element_type=F32).astype(BF16)
    rim_rows = from_behind(inner_act[:, length - (tap_count - 1) :, :], "seq", 1)
    gate_in = jnp.einsum("ltd,de->lte", normed, w_in[1], preferred_element_type=F32)
    rim_rows = rim_rows.astype(F32) * carry_mask
    padded = jnp.concatenate([rim_rows, inner_act.astype(F32)], axis=1)
    conv_sum = conv_bias + conv_weight[0] * padded[:, 0:length]
    for tap in range(1, tap_count):
        conv_sum = conv_sum + conv_weight[tap] * padded[:, tap : tap + length]
    mixed = jax.nn.silu(conv_sum)
    mixed_low = mixed.astype(BF16)
    sent = jnp.einsum("lte,er->ltr", mixed_low, w_x, preferred_element_type=F32).astype(BF16)
    for bit in mp_bits[:-1]:
        sent = (sent.astype(F32) + swap(sent, "mp", bit).astype(F32)).astype(BF16)
    got = swap(sent, "mp", mp_bits[-1])
    grad_whole = jnp.concatenate(
        [
            sum(jnp.where(k == (mp_index ^ block), grad_parts[k], 0) for k in range(mp_size))
            for block in range(mp_size)
        ],
        axis=2,
    )
    grad_gated = jnp.einsum("ltd,ed->lte", grad_whole, w_out, preferred_element_type=F32)
    grad_scan = grad_gated * jax.nn.silu(gate_in)
    end_state, pulled, span, dt, source, slope_dt, projected = scan_ends(
        low_rank, sent, got, w_dt, dt_bias[None], decay_log, mixed, grad_scan
    )
    span = span + FAR * starts[:, :, None]
    to_later = (jnp.arange(seq_size) > seq_index)[:, None, None]
    flat = (1, lane_count * state_count, inner_width)
    edge = jnp.where(to_later, end_state.reshape(flat), (pulled * carry_mask).reshape(flat))
    spans = jnp.broadcast_to(
        span.reshape(1, lane_count, inner_width), (seq_size, lane_count, inner_width)
    )
    message = jnp.concatenate([edge, spans], axis=1).astype(BF16)
    message = jnp.pad(message, ((0, 0), (0, -message.shape[1] % 8), (0, 0)))
    groups = lax.all_to_all(message, "seq", 0, 0, tiled=True)
    place = jnp.concatenate([seq_index[None].astype(jnp.int32), row_starts[:, 0]])
    y, grad_read, last, states_all = scan_forward(
        low_rank, place, projected, decay_log, dt, source, grad_scan, groups
    )
    scan_out = y + skip_gain * mixed
    gated = (scan_out * jax.nn.silu(gate_in)).astype(BF16)
    grad_gate = (grad_gated * scan_out * silu_slope(gate_in)).astype(BF16)
    over = Reduction()
    half_width = model_width // 2
    first_sent = over.sent(normed, grad_gate)
    sum_first = Sum(over, jnp.concatenate([first_sent, over.sent(grad_whole, gated)], axis=0), 2)
    out_sent = jnp.einsum(
        "lte,ed->ltd", after(gated, sum_first.sent), w_spread[:, half_width:], preferred_element_type=F32
    ).astype(BF16)
    turn, pull, part, grad_log = scan_backward(
        low_rank, projected, decay_log, dt, source, grad_scan, last, grad_read, states_all,
        sum_first.sent, out_sent,
    )
    grad_slope = (turn + pull * mixed) * slope_dt
    grad_pre = grad_slope.astype(BF16)
    part = part + jnp.einsum("lte,re->ltr", grad_pre, w_dt, preferred_element_type=F32)
    sent = part.astype(BF16)
    for bit in mp_bits[:-1]:
        got = swap(sent, "mp", bit)
        if bit == 1:
            kept = over.kept(after(normed, sent), grad_gate)
            sent = after(sent, kept)
        sent = (sent.astype(F32) + got.astype(F32)).astype(BF16)
    got = swap(sent, "mp", mp_bits[-1])
    sum_first.kept = [kept, over.kept(after(grad_whole, sent), gated)]
    step = sum_first.next(sent)
    grad_dt_w = jnp.einsum(
        "ltr,lte->re", projected.astype(BF16), after(grad_pre, step), preferred_element_type=F32
    )[:low_rank]
    grad_projected = after(sent, grad_dt_w).astype(F32) + got.astype(F32)
    grad_projected = grad_projected.astype(BF16)
    grad_mixed = pull * dt + grad_scan * skip_gain + jnp.einsum(
        "ltr,er->lte", grad_projected, w_x, preferred_element_type=F32
    )
    grad_conv = grad_mixed * silu_slope(conv_sum)
    grad_conv_b = jnp.sum(grad_conv, axis=(0, 1))
    grad_conv_w = jnp.stack(
        [
            jnp.sum(grad_conv * padded[:, tap : tap + length], axis=(0, 1))
            for tap in range(tap_count)
        ]
    )
    grad_padded = jnp.pad(conv_weight[0] * grad_conv, ((0, 0), (0, tap_count - 1), (0, 0)))
    for tap in range(1, tap_count):
        grad_padded = grad_padded + jnp.pad(
            conv_weight[tap] * grad_conv, ((0, 0), (tap, tap_count - 1 - tap), (0, 0))
        )
    rim_sent = grad_padded[:, : tap_count - 1] * carry_mask
    rim_back = from_behind(rim_sent, "seq", -1)
    grad_x_w = jnp.einsum(
        "ltr,lte->re", grad_projected, after(mixed_low, rim_sent), preferred_element_type=F32
    )[: low_rank + 2 * state_count]
    step = grad_x_w
    tail_zeros = jnp.zeros((lane_count, length - (tap_count - 1), inner_width), F32)
    grad_inner = after(grad_padded, step)[:, tap_count - 1 :] + jnp.concatenate(
        [tail_zeros, rim_back], axis=1
    )
    grad_inner = grad_inner.astype(BF16)
    sum_inner = Sum(over, over.sent(normed, grad_inner), 1)
    sum_inner.kept = [over.kept(normed, after(grad_inner, sum_inner.sent))]
    step = sum_first.next(sum_inner.kept[0])

    def back(part, cut):
        return jnp.einsum("lte,de->ltd", part[0], w_back[0, cut], preferred_element_type=F32) + jnp.einsum(
            "lte,de->ltd", part[1], w_back[1, cut], preferred_element_type=F32
        )

    grads = (after(grad_inner, step), grad_gate)
    back_sent = back(grads, slice(half_width, None)).astype(BF16)
    back_kept = back((after(grad_inner, back_sent), grad_gate), slice(0, half_width))
    step = sum_inner.next(back_sent)
    row_dot = jnp.sum(
        after(grad_inner, step).astype(F32) * inner_act.astype(F32) + grad_gate.astype(F32) * gate_in,
        axis=2,
    )
    for bit in mp_bits:
        row_dot = row_dot + swap(row_dot, "mp", bit)
    for bit in mp_bits[:-1]:
        back_kept, back_sent = hop(back_kept, back_sent, "mp", bit)
    grad_own = back_kept + swap(back_sent, "mp", mp_bits[-1]).astype(F32)
    step = sum_first.next(back_sent)
    out_kept = jnp.einsum(
        "lte,ed->ltd", after(gated, step), w_spread[:, :half_width], preferred_element_type=F32
    )
    for bit in mp_bits[:-1]:
        out_kept, out_sent = hop(out_kept, out_sent, "mp", bit)
    output = inputs + (out_kept + swap(out_sent, "mp", mp_bits[-1]).astype(F32))
    step = sum_inner.next(out_sent)
    unit_own = inputs * inv_rms
    grad_gain = jnp.sum(grad_own * unit_own, axis=(0, 1))
    input_grad = output_grad + inv_rms * (
        grad_own * gain[:shard_width] - unit_own * (row_dot[:, :, None] / model_width)
    )
    gain_rows = jnp.pad(grad_gain, (0, -shard_width % inner_width)).reshape(-1, inner_width)
    small = jnp.concatenate(
        [
            grad_conv_w,
            grad_conv_b[None],
            jnp.sum(grad_slope, axis=(0, 1))[None],
            jnp.sum(grad_scan * mixed, axis=(0, 1))[None],
            jnp.sum(grad_log, axis=0),
            grad_dt_w,
            grad_x_w,
            gain_rows,
        ],
        axis=0,
    )
    small = jnp.pad(small, ((0, -small.shape[0] % 16), (0, 0)))
    step = sum_first.next(step)
    step = sum_inner.next(step)
    for bit in seq_bits:
        low = after(small, step).astype(BF16)
        small = low.astype(F32) + swap(low, "seq", bit).astype(F32)
        step = sum_first.next(step) if not sum_first.over_now() else step
        step = sum_inner.next(step) if not sum_inner.over_now() else step
    per = shard_width * seq_size // model_width
    blocks = seq_size // 2
    orders = jnp.concatenate([over.order(per, mp_index), over.order(1, 0)])
    second = 2 + blocks
    in_shape, out_shape = (2, model_width, inner_width), out_weight.shape
    early, late = sum_first.finish()
    layout = [(0, 1, 0, 0, blocks, False), (0, 1, 0, 1, blocks, False)]
    shapes, pieces = [in_shape], [early[0], late[0]]
    aligned = model_width // seq_size % LANE == 0
    if aligned:
        layout += [(1, None, second, 0, blocks, True), (1, None, second, 1, blocks, True)]
        shapes, pieces = [in_shape, out_shape], [*pieces, early[1], late[1]]
    in_w, *out_w = settle(orders, pieces, layout, shapes)
    if not aligned:
        source = orders[second + 2 :]
        halves = [p.reshape(blocks, -1, inner_width)[source].reshape(-1, inner_width) for p in (early[1], late[1])]
        up = over.own(0) == 1
        halves = [jnp.where(up, halves[1], halves[0]), jnp.where(up, halves[0], halves[1])]
        out_w = [jnp.concatenate(halves, axis=0).astype(F32).T]
    early, late = sum_inner.finish()
    (in_w,) = settle(orders, early, [(0, 0, 0, 0, blocks, False)], [in_shape], [in_w])
    (in_w,) = settle(orders, late, [(0, 0, 0, 1, blocks, False)], [in_shape], [in_w])
    (out_w,) = out_w
    sizes = [tap_count, 1, 1, 1, state_count, low_rank, low_rank + 2 * state_count, gain_rows.shape[0]]
    parts, at = [], 0
    for size in sizes:
        parts.append(small[at : at + size])
        at += size
    return (
        output,
        input_grad,
        parts[7].reshape(-1)[:shard_width],
        in_w,
        parts[0],
        parts[1][0],
        parts[6].T,
        parts[5],
        parts[2][0],
        parts[4],
        parts[3][0],
        out_w,
    )


def solution(mesh):
    in_specs = (
        P(None, "seq", "mp"),
        P(None, "seq"),
        P(),
        P(None, None, "mp"),
        P(None, "mp"),
        P("mp"),
        P("mp", None),
        P(None, "mp"),
        P("mp"),
        P(None, "mp"),
        P("mp"),
        P("mp", None),
        P(None, "seq", "mp"),
    )
    out_specs = (
        P(None, "seq", "mp"),
        P(None, "seq", "mp"),
        P("mp"),
        P(None, None, "mp"),
        P(None, "mp"),
        P("mp"),
        P("mp", None),
        P(None, "mp"),
        P("mp"),
        P(None, "mp"),
        P("mp"),
        P("mp", None),
    )
    return jax.shard_map(
        per_device, mesh=mesh, in_specs=in_specs, out_specs=out_specs, check_vma=False
    )
```

```python
import functools

import jax
import jax.numpy as jnp
from jax import lax
from jax.experimental import pallas as pl
from jax.experimental.pallas import tpu as pltpu
from jax.sharding import PartitionSpec as P

F32 = jnp.float32
BF16 = jnp.bfloat16
LOG2E = 1.4426950408889634
CHUNK = 32
ROUND = 4
LANE = 128
FAR = 1.0e4
VMEM = pl.BlockSpec(memory_space=pltpu.VMEM)


def swap(block, axis, bit):
    devices = lax.axis_size(axis)
    return lax.ppermute(block, axis, [(i, i ^ bit) for i in range(devices)])


def from_behind(block, axis, distance):
    devices = range(lax.axis_size(axis))
    route = [(i - distance, i) for i in devices if i - distance in devices]
    return lax.ppermute(block, axis, route)


def bits_of(axis):
    count = lax.axis_size(axis)
    bits = []
    while (1 << len(bits)) < count:
        bits.append(1 << len(bits))
    return bits


def after(array, *others):
    return lax.optimization_barrier((array, *others))[0]


class Reduction:
    def __init__(self):
        self.bits = bits_of("seq")
        self.orders = [list(self.bits), list(self.bits)]
        if len(self.bits) > 1:
            self.orders[1][:2] = self.bits[1], self.bits[0]
        self.index = lax.axis_index("seq")
        self.odd = lax.axis_index("mp") % 2
        self.mp = lax.axis_size("mp")
        self.count = lax.axis_size("seq")

    def own(self, step):
        even = (self.index & self.orders[0][step]) != 0
        odd = (self.index & self.orders[1][step]) != 0
        return jnp.where(self.odd == 1, odd, even).astype(jnp.int32)

    def swap(self, block, step):
        route = []
        for s in range(self.count):
            for m in range(self.mp):
                route.append((s * self.mp + m, (s ^ self.orders[m % 2][step]) * self.mp + m))
        return lax.ppermute(block, ("seq", "mp"), route)

    def halves(self, block, step):
        half = block.shape[0] // 2
        up = self.own(step)
        kept = lax.dynamic_slice_in_dim(block, up * half, half, 0)
        sent = lax.dynamic_slice_in_dim(block, (1 - up) * half, half, 0)
        return kept, sent

    def part(self, left, right, up):
        half = left.shape[2] // 2
        cut = lax.dynamic_slice_in_dim(left, up * half, half, 2)
        return jnp.einsum("lta,ltb->ab", cut, right, preferred_element_type=F32)

    def sent(self, left, right):
        return self.part(left, right, 1 - self.own(0)).astype(BF16)

    def kept(self, left, right):
        return self.part(left, right, self.own(0))

    def place(self):
        place = jnp.int32(0)
        for step in range(1, len(self.bits)):
            place = place * 2 + self.own(step)
        return place

    def order(self, per, turn):
        blocks = self.count // 2
        pieces = blocks // per
        at = jnp.arange(blocks)
        low, high = turn % pieces, turn // pieces
        source = (((at // per) ^ low) * per + at % per) ^ self.place()
        up = self.own(0) ^ high
        return jnp.concatenate([jnp.stack([up * blocks, (1 - up) * blocks]), source]).astype(jnp.int32)

    def flat_order(self):
        blocks = self.count // 2
        place = jnp.int32(0)
        for step in range(len(self.bits) - 1):
            place = place * 2 + self.own(step)
        return (jnp.arange(blocks) ^ place).astype(jnp.int32)


def advance_kernel(plan, flag_ref, *refs):
    refs = list(refs)
    sent_ref, got_ref = refs.pop(0), refs.pop(0)
    inputs, outputs = refs[: plan["inputs"]], refs[plan["inputs"] :]
    message = outputs.pop(0)
    up = flag_ref[0]
    at = 0
    for mode, rows, first in plan["blocks"]:
        if mode == "half":
            kept, new = inputs.pop(0), outputs.pop(0)
            half = rows // 2
            own = pl.multiple_of(up * half, half)
            other = pl.multiple_of((1 - up) * half, half)
            new[...] = kept[pl.ds(own, half), :].astype(F32) + got_ref[pl.ds(first + own, half), :].astype(F32)
            send = kept[pl.ds(other, half), :].astype(F32) + got_ref[pl.ds(first + other, half), :].astype(F32)
            message[at : at + half, :] = send.astype(BF16)
            at += half
        elif mode in ("flat", "sum", "hold"):
            kept = inputs.pop(0)
            total = (kept[...].astype(F32) + got_ref[first : first + rows, :].astype(F32)).astype(BF16)
            if mode != "sum":
                outputs.pop(0)[...] = total
            if mode != "hold":
                message[at : at + rows, :] = total
                at += rows
        elif mode == "enter":
            message[at : at + rows, :] = inputs.pop(0)[...].astype(BF16)
            at += rows
        elif mode == "grow":
            message[at : at + rows, :] = sent_ref[first : first + rows, :]
            message[at + rows : at + 2 * rows, :] = got_ref[first : first + rows, :]
            at += 2 * rows
        else:
            total = sent_ref[first : first + rows, :].astype(F32) + got_ref[first : first + rows, :].astype(F32)
            message[at : at + rows, :] = total.astype(BF16)
            at += rows


def advance(flag, sent, got, blocks, inputs):
    width = sent.shape[1]
    grown = {"half": 0.5, "hold": 0, "grow": 2}
    total = int(sum(rows * grown.get(mode, 1) for mode, rows, _ in blocks))
    shapes = [jax.ShapeDtypeStruct((total, width), BF16)]
    for mode, rows, _ in blocks:
        if mode == "half":
            shapes.append(jax.ShapeDtypeStruct((rows // 2, width), F32))
        elif mode in ("flat", "hold"):
            shapes.append(jax.ShapeDtypeStruct((rows, width), BF16))
    return pl.pallas_call(
        functools.partial(advance_kernel, {"inputs": len(inputs), "blocks": blocks}),
        in_specs=[pl.BlockSpec(memory_space=pltpu.SMEM)] + [VMEM] * (2 + len(inputs)),
        out_specs=[VMEM] * len(shapes),
        out_shape=shapes,
        compiler_params=pltpu.CompilerParams(vmem_limit_bytes=12 << 20),
        name="advance",
    )(flag, sent, got, *inputs)


class Sum:
    def __init__(self, over, sent, flat, flags):
        self.over, self.flat, self.flags = over, flat, flags
        self.kept, self.rider, self.count = None, None, 0
        self.rows = [block.shape[0] for block in sent]
        self.message = jnp.concatenate([block.astype(BF16) for block in sent], axis=0)
        self.got = over.swap(self.message, 0)

    def next(self, *earlier):
        steps = len(self.over.bits)
        k = self.count
        got = after(self.got, *earlier) if earlier else self.got
        blocks, inputs, rows, kept, first = [], [], [], [], 0
        for m, size in enumerate(self.rows):
            mode = "half" if k < steps - 1 else "sum" if k == steps - 1 else "grow"
            if self.flat[m]:
                mode = {steps - 2: "flat", steps - 1: "hold", steps: "enter"}.get(k, mode)
            if mode == "enter":
                size = self.kept[m].shape[0]
            blocks.append((mode, size, first))
            if mode != "grow":
                inputs.append(self.kept[m])
            first += 0 if mode == "enter" else size
            rows.append({"half": size // 2, "hold": 0, "grow": 2 * size}.get(mode, size))
        if self.rider is not None and k == steps - 1:
            blocks.append(("enter", self.rider.shape[0], 0))
            inputs.append(self.rider)
        elif self.rider is not None and k >= steps:
            blocks.append(("ride", self.rider.shape[0], first))
        flag = self.flags[min(k + 1, steps - 1)]
        self.message, *kept = advance(flag, self.message, got, blocks, inputs)
        for m, (mode, _, _) in enumerate(blocks[: len(rows)]):
            if mode in ("half", "flat", "hold"):
                self.kept[m] = kept.pop(0)
        self.rows = rows
        self.count = k + 1
        step = self.count if self.count < steps else 2 * steps - 1 - self.count
        self.got = self.over.swap(self.message, step)
        return self.message

    def run_out(self):
        while self.count < 2 * len(self.over.bits) - 1:
            self.next()


def silu_slope(values):
    logistic = jax.nn.sigmoid(values)
    return logistic * (1.0 + values * (1.0 - logistic))


def cost(ops, lanes, length, width, states):
    work = lanes * length * width * states
    return pl.CostEstimate(flops=ops * work * 16, bytes_accessed=work * 2, transcendentals=work)


def settle_kernel(names, layout, order_ref, *refs):
    parts, outs = refs[: len(layout)], refs[-2 - names : -2]
    wide, sems = refs[-2:]
    copies, at = [], 0
    for part, (out, lead, which, first, blocks, turned, offset, count) in zip(parts, layout, strict=True):
        size = count // blocks
        for b in range(blocks):
            source = order_ref[which + 2 + b]
            rows = part[pl.ds(pl.multiple_of(offset + source * size, size), size), :].astype(F32)
            goal = pl.multiple_of((order_ref[which + first] + b) * size, size)
            ref = outs[out] if lead is None else outs[out].at[lead]
            if turned:
                rows = jnp.transpose(rows)
                spot = wide.at[at : at + rows.shape[0], 0:size]
                target = ref.at[:, pl.ds(goal, size)]
            else:
                spot = wide.at[at : at + size, 0 : part.shape[1]]
                target = ref.at[pl.ds(goal, size), :]
            spot[...] = rows
            at += rows.shape[0]
            copies.append(pltpu.make_async_copy(spot, target, sems.at[len(copies)]))
            copies[-1].start()
    for copy in copies:
        copy.wait()


def settle(orders, parts, layout, shapes, into=()):
    any_space = pl.BlockSpec(memory_space=pl.ANY)
    rows = sum(p.shape[1] * l[4] if l[5] else l[7] for p, l in zip(parts, layout, strict=True))
    width = max(l[7] // l[4] if l[5] else p.shape[1] for p, l in zip(parts, layout, strict=True))
    count = sum(l[4] for l in layout)
    return pl.pallas_call(
        functools.partial(settle_kernel, len(shapes), layout),
        in_specs=[pl.BlockSpec(memory_space=pltpu.SMEM)] + [VMEM] * len(parts) + [any_space] * len(into),
        out_specs=[any_space] * len(shapes),
        out_shape=[jax.ShapeDtypeStruct(s, F32) for s in shapes],
        input_output_aliases={1 + len(parts) + k: k for k in range(len(into))},
        scratch_shapes=[pltpu.VMEM((rows, width), F32), pltpu.SemaphoreType.DMA((count,))],
        compiler_params=pltpu.CompilerParams(vmem_limit_bytes=16 << 20),
        name="settle",
    )(orders, *parts, *into)


def deal_kernel(sizes, offset, order_ref, own_ref, late_ref, *refs):
    outs, rows = refs[:-1], refs[-1]
    blocks = order_ref.shape[0]
    size = rows.shape[0] // blocks
    for b in range(blocks):
        source = order_ref[b]
        for part, first in ((own_ref, 0), (late_ref, blocks // 2)):

            @pl.when(jnp.logical_and(source >= first, source < first + blocks // 2))
            def _():
                at = pl.ds(pl.multiple_of(offset + (source - first) * size, size), size)
                rows[b * size : (b + 1) * size, :] = part[at, :].astype(F32)

    at = 0
    for out, count in zip(outs, sizes, strict=True):
        out[...] = rows[at : at + count, :]
        at += count


def deal(order, own, late, offset, count, sizes):
    width = own.shape[1]
    return pl.pallas_call(
        functools.partial(deal_kernel, sizes, offset),
        in_specs=[pl.BlockSpec(memory_space=pltpu.SMEM), VMEM, VMEM],
        out_shape=[jax.ShapeDtypeStruct((count, width), F32) for count in sizes],
        scratch_shapes=[pltpu.VMEM((2 * count, width), F32)],
        compiler_params=pltpu.CompilerParams(vmem_limit_bytes=8 << 20),
        name="deal",
    )(order, own, late)


def hop_kernel(got_ref, *refs):
    kept, (row_ref, message), outs = refs[:2], refs[2:4], refs[4:]
    lanes, length, width = kept[0].shape
    half = width // 2
    for l in range(lanes):
        for m in range(2):
            o = slice(m * length, (m + 1) * length)
            outs[m][l] = kept[m][l, :, :half] + got_ref[l, o, :half].astype(F32)
            send = kept[m][l, :, half:] + got_ref[l, o, half:].astype(F32)
            message[l, o, :] = send.astype(BF16)
        rows = got_ref[l, 2 * length :, :].astype(F32)
        came = jnp.concatenate([rows[r : r + 1] for r in range(2 * length // width)], axis=1)
        total = row_ref[l : l + 1, :] + came[:, :length] + came[:, length:]
        outs[2][l : l + 1, :] = total
        high = total.astype(BF16).astype(F32)
        both = jnp.concatenate([high, total - high], axis=1)
        pieces = [both[:, at : at + half] for at in range(0, 2 * length, half)]
        pieces.append(jnp.zeros((message.shape[1] - 2 * length - len(pieces), half), F32))
        message[l, 2 * length :, :] = jnp.concatenate(pieces, axis=0).astype(BF16)


def hop(got, out_kept, back_kept, row_dot):
    lanes, length, width = out_kept.shape
    shape = jax.ShapeDtypeStruct
    half = shape((lanes, length, width // 2), F32)
    rows = 2 * length - (-(4 * length // width) // 16) * 16
    return pl.pallas_call(
        hop_kernel_entry,
        in_specs=[VMEM] * 4,
        out_specs=[VMEM] * 4,
        out_shape=[shape((lanes, rows, width // 2), BF16), half, half, shape(row_dot.shape, F32)],
        compiler_params=pltpu.CompilerParams(vmem_limit_bytes=12 << 20),
        name="hop",
    )(got, out_kept, back_kept, row_dot)


def hop_kernel_entry(got_ref, out_ref, back_ref, row_ref, message, *outs):
    hop_kernel(got_ref, out_ref, back_ref, row_ref, message, *outs)


def iota(shape, dim):
    return lax.broadcasted_iota(jnp.int32, shape, dim)


def widen(part, width):
    return jnp.concatenate([part] * (width // part.shape[1]), axis=1)


def dot(a, b):
    return jnp.dot(a, b, preferred_element_type=F32)


def dot_t(a, b):
    return lax.dot_general(a, b, (((1,), (1,)), ((), ())), preferred_element_type=F32)


def row_of(ref, t, count):
    return jnp.broadcast_to(ref[pl.ds(t, 1), :], (count, ref.shape[1]))


def rows_of(i, count):
    return pl.ds(pl.multiple_of(i * count, count), count)


def chunk_columns(ref, i):
    per = LANE // CHUNK
    tile = ref[:, rows_of(i // per, LANE)]
    return pltpu.roll(tile, LANE - (i % per) * CHUNK, 1)


def spread_column(tile, j, width):
    part = jnp.broadcast_to(tile[:, j : j + 1], (tile.shape[0], LANE))
    return widen(part, width)


def selectors(states):
    wide = CHUNK * states
    per_state = iota((states, wide), 1) % states == iota((states, wide), 0)
    per_step = iota((CHUNK, wide), 1) // states == iota((CHUNK, wide), 0)
    return per_state.astype(F32), per_step.astype(F32)


def from_lanes(first, states):
    shape = (LANE, CHUNK * states)
    return (iota(shape, 0) == first + iota(shape, 1) % states).astype(BF16)


def to_lanes(first, states):
    shape = (CHUNK * states, LANE)
    return (iota(shape, 1) == first + iota(shape, 0) % states).astype(BF16)


def by_step(proj, lanes, per_step):
    spread = dot(proj, lanes)
    return spread * jnp.concatenate([per_step] * (spread.shape[0] // CHUNK), axis=0)


def ends_kernel(
    low_rank, sent_ref, got_ref, wdt_ref, bias_ref, log_ref, mixed_ref, gy_ref,
    end_ref, pull_ref, span_ref, dt_ref, u_ref, sig_ref, proj_ref,
    ahead, behind, left_b, left_c, xa, xb, ya, yb,
):
    length, width = dt_ref.shape
    states = log_ref.shape[0]
    rate = -jnp.exp(log_ref[...]) * LOG2E
    per_state, per_step = selectors(states)
    chunks = length // CHUNK
    upto = (iota((length, length), 1) <= iota((length, length), 0)).astype(BF16)
    after = (iota((length, length), 1) > iota((length, length), 0)).astype(BF16)
    proj = sent_ref[...].astype(F32) + got_ref[...].astype(F32)
    proj_ref[...] = proj
    proj = proj.astype(BF16)
    for first, left in ((low_rank, left_b), (low_rank + states, left_c)):
        spread = by_step(proj, from_lanes(first, states), per_step)
        for i in range(chunks):
            flat = jnp.sum(spread[i * CHUNK : (i + 1) * CHUNK], axis=0, keepdims=True)
            left[i * states : (i + 1) * states, :] = (flat * per_state).astype(BF16)
    block = min(128, length)
    for i in range(length // block):
        o = slice(i * block, (i + 1) * block)
        pre = dot(proj[o], wdt_ref[...]) + bias_ref[...]
        small = jnp.exp(-jnp.abs(pre))
        one = 1.0 + small
        series = small * (1.0 - small * (0.5 - small * (1.0 / 3.0)))
        dt = jnp.maximum(pre, 0.0) + jnp.where(small < 1e-3, series, jnp.log(one))
        dt_ref[o, :] = dt
        u_ref[o, :] = dt * mixed_ref[o, :]
        sig_ref[o, :] = jnp.where(pre >= 0.0, 1.0, small) / one
    dt = dt_ref[...]
    high = dt.astype(BF16)
    low = (dt - high.astype(F32)).astype(BF16)
    ahead[...] = dot(upto, high) + dot(upto, low)
    behind[...] = dot(after, high) + dot(after, low)
    span_ref[...] = ahead[length - 1 : length, :]
    xb[...] = jnp.zeros(xb.shape, BF16)
    yb[...] = jnp.zeros(yb.shape, BF16)

    def flush(i, x, y, sums):
        o = rows_of(jnp.maximum(i, 0), states)
        return sums[0] + dot(left_b[o, :], x[...]), sums[1] + dot(left_c[o, :], y[...])

    def fill(i, x, y):
        for j in range(CHUNK):
            t = i * CHUNK + j
            s = slice(j * states, (j + 1) * states)
            to_end = jnp.exp2(row_of(behind, t, states) * rate)
            x[s, :] = (to_end * row_of(u_ref, t, states)).astype(BF16)
            to_here = jnp.exp2(row_of(ahead, t, states) * rate)
            y[s, :] = (to_here * row_of(gy_ref, t, states)).astype(BF16)

    def body(k, sums):
        for i in range(0, ROUND, 2):
            at = ROUND * k + i
            sums = flush(at - 1, xb, yb, sums)
            fill(at, xa, ya)
            sums = flush(at, xa, ya, sums)
            fill(at + 1, xb, yb)
        return sums

    zero = jnp.zeros((states, width), F32)
    sums = lax.fori_loop(0, chunks // ROUND, body, (zero, zero))
    sums = flush(chunks - 1, xb, yb, sums)
    end_ref[...] = sums[0]
    pull_ref[...] = sums[1]


def lane_spec(*shape):
    return pl.BlockSpec((None, *shape), lambda l: (l,) + (0,) * len(shape))


def whole_spec(*shape):
    return pl.BlockSpec(shape, lambda l: (0,) * len(shape))


def scan_ends(low_rank, sent, got, w_dt, bias, log, mixed, gy):
    lanes, length, width = mixed.shape
    states = log.shape[0]
    shape = jax.ShapeDtypeStruct
    token = shape((lanes, length, width), F32)
    state = shape((lanes, states, width), F32)
    tokens, state_spec, narrow = lane_spec(length, width), lane_spec(states, width), lane_spec(length, LANE)
    return pl.pallas_call(
        functools.partial(ends_kernel, low_rank),
        grid=(lanes,),
        in_specs=[
            narrow,
            narrow,
            whole_spec(*w_dt.shape),
            whole_spec(1, width),
            whole_spec(states, width),
            tokens,
            tokens,
        ],
        out_specs=[state_spec, state_spec, lane_spec(1, width), tokens, tokens, tokens, narrow],
        out_shape=[state, state, shape((lanes, 1, width), F32)]
        + [pltpu.HBM((lanes, length, width), F32)] * 3
        + [shape(sent.shape, F32)],
        scratch_shapes=[pltpu.VMEM((length, width), F32)] * 2
        + [pltpu.VMEM((length // CHUNK * states, CHUNK * states), BF16)] * 2
        + [pltpu.VMEM((CHUNK * states, width), BF16)] * 4,
        compiler_params=pltpu.CompilerParams(vmem_limit_bytes=14 << 20),
        cost_estimate=cost(8, lanes, length, width, states),
        name="scan_ends",
    )(sent, got, w_dt, bias, log, mixed, gy)


def forward_kernel(
    low_rank, lanes, place_ref, proj_ref, log_ref, dt_ref, u_ref, gy_ref, got_ref,
    y_ref, gc_ref, last_ref, hs_ref,
    kept, pa, pb, cols, left_c, masked, sems,
):
    length, width = dt_ref.shape
    states = log_ref.shape[0]
    l = pl.program_id(0)
    rate = -jnp.exp(log_ref[...]) * LOG2E
    _, per_step = selectors(states)
    wide = CHUNK * states
    chunks = length // CHUNK
    groups = got_ref.shape[0]
    place = place_ref[0]

    half = chunks // 2 * wide

    def leave(slot, part):
        rows = pl.ds(part * half, half)
        return pltpu.make_async_copy(kept.at[slot, rows, :], hs_ref.at[slot, rows, :], sems.at[slot, part])

    zero = jnp.zeros((states, width), F32)

    def join(g, total, use):
        at = lanes * states
        spans = got_ref[g, at : at + lanes, :].astype(F32)
        span = jnp.sum(jnp.where(iota(spans.shape, 0) == l, spans, 0.0), axis=0, keepdims=True)
        factor = jnp.exp2(span * rate)
        return jnp.where(use, total * factor + got_ref[g, rows_of(l, states), :].astype(F32), total)

    begin = last = zero
    for g in range(groups):
        begin = join(g, begin, g < place)
        h = groups - 1 - g
        last = join(h, last, h > place)
    last_ref[...] = last
    begin = jnp.where(place_ref[1 + l] != 0, 0.0, begin)
    proj = proj_ref[...]
    cols[...] = jnp.transpose(proj)[low_rank : low_rank + states]
    spread = by_step(proj.astype(BF16), from_lanes(low_rank + states, states), per_step)
    left_c[...] = spread.astype(BF16)

    def flush(i, p):
        o = rows_of(jnp.maximum(i, 0), CHUNK)
        h = p[...]
        y_ref[o, :] = dot(left_c[o, :], h)
        masked[o, :] = (dot_t(gy_ref[o, :].astype(BF16), h) * per_step).astype(BF16)

    def fill(i, state, p):
        b_tile = chunk_columns(cols, i)
        low = state.astype(BF16)
        for j in range(CHUNK):
            t = i * CHUNK + j
            b = spread_column(b_tile, j, width)
            decay = jnp.exp2(row_of(dt_ref, t, states) * rate)
            state = decay * state + row_of(u_ref, t, states) * b
            kept[l, rows_of(t, states), :] = low
            low = state.astype(BF16)
            p[j * states : (j + 1) * states, :] = low
        return state

    def body(k, state):
        for i in range(0, ROUND, 2):
            at = ROUND * k + i
            flush(at - 1, pb)
            state = fill(at, state, pa)
            flush(at, pa)
            state = fill(at + 1, state, pb)
        return state

    rounds = chunks // ROUND
    state = lax.fori_loop(0, rounds // 2, body, begin)
    leave(l, 0).start()
    lax.fori_loop(rounds // 2, rounds, body, state)
    leave(l, 1).start()
    flush(chunks - 1, pb)
    gc_ref[...] = dot(masked[...], to_lanes(low_rank + states, states))

    @pl.when(l == lanes - 1)
    def _():
        for slot in range(lanes):
            for part in range(2):
                leave(slot, part).wait()


def scan_forward(low_rank, place, proj, log, dt, u, gy, got):
    lanes, length, width = dt.shape
    states = log.shape[0]
    shape = jax.ShapeDtypeStruct
    tokens, state_spec, narrow = lane_spec(length, width), lane_spec(states, width), lane_spec(length, LANE)
    return pl.pallas_call(
        functools.partial(forward_kernel, low_rank, lanes),
        grid=(lanes,),
        in_specs=[
            pl.BlockSpec(memory_space=pltpu.SMEM),
            narrow,
            whole_spec(states, width),
            tokens,
            tokens,
            tokens,
            whole_spec(*got.shape),
        ],
        out_specs=[tokens, narrow, state_spec, pl.BlockSpec(memory_space=pltpu.HBM)],
        out_shape=[
            shape((lanes, length, width), F32),
            shape(proj.shape, F32),
            shape((lanes, states, width), F32),
            shape((lanes, length * states, width), BF16),
        ],
        scratch_shapes=[pltpu.VMEM((lanes, length * states, width), BF16)]
        + [pltpu.VMEM((CHUNK * states, width), BF16)] * 2
        + [
            pltpu.VMEM((states, length), F32),
            pltpu.VMEM((length, CHUNK * states), BF16),
            pltpu.VMEM((length, CHUNK * states), BF16),
            pltpu.SemaphoreType.DMA((lanes, 2)),
        ],
        compiler_params=pltpu.CompilerParams(vmem_limit_bytes=20 << 20),
        cost_estimate=cost(8, lanes, length, width, states),
        name="scan_forward",
    )(place, proj, log, dt, u, gy, got)


def backward_kernel(
    low_rank, lanes, proj_ref, log_ref, dt_ref, u_ref, gy_ref, last_ref, gc_ref, hs_ref, *refs
):
    (turn_ref, pull_ref, gbc_ref, ga_ref,
     kept, pa, pb, qa, qb, ra, rb, cols, left_b, masked, sems) = refs[-15:]
    length, width = dt_ref.shape
    states = log_ref.shape[0]
    l = pl.program_id(0)
    plain = -jnp.exp(log_ref[...])
    rate = plain * LOG2E
    rate_low = plain.astype(BF16)
    per_state, per_step = selectors(states)
    per_state_low, per_step_low = per_state.astype(BF16), per_step.astype(BF16)
    chunks = length // CHUNK

    half = length // 2 * states

    def enter(slot, part):
        rows = pl.ds(part * half, half)
        return pltpu.make_async_copy(hs_ref.at[slot, rows, :], kept.at[slot, rows, :], sems.at[slot, part])

    @pl.when(l == 0)
    def _():
        for slot in range(lanes):
            for part in (1, 0):
                enter(slot, part).start()

    for ref in (pb, qb, rb):
        ref[...] = jnp.zeros(ref.shape, BF16)
    proj = proj_ref[...]
    cols[...] = jnp.transpose(proj)[low_rank + states : low_rank + 2 * states]
    left_b[...] = by_step(proj.astype(BF16), from_lanes(low_rank, states), per_step).astype(BF16)

    def flush(i, p, q, r, ga):
        o = rows_of(jnp.minimum(i, chunks - 1), CHUNK)
        grad = p[...]
        pull_ref[o, :] = dot(left_b[o, :], grad)
        masked[o, :] = (dot_t(u_ref[o, :].astype(BF16), grad) * per_step).astype(BF16)
        turn_ref[o, :] = dot(per_step_low, q[...])
        return ga + dot(per_state_low, r[...])

    def fill(i, carry, p, q, r):
        c_tile = chunk_columns(cols, i)
        for j in reversed(range(CHUNK)):
            t = i * CHUNK + j
            s = slice(j * states, (j + 1) * states)
            c = spread_column(c_tile, j, width)
            dt = row_of(dt_ref, t, states)
            grad = carry + row_of(gy_ref, t, states) * c
            carry = jnp.exp2(dt * rate) * grad
            p[s, :] = grad.astype(BF16)
            turn = carry.astype(BF16) * kept[l, rows_of(t, states), :] * rate_low
            q[s, :] = turn
            r[s, :] = turn * dt.astype(BF16)
        return carry

    def body(k, carried):
        carry, ga = carried
        for i in range(0, ROUND, 2):
            at = chunks - 1 - ROUND * k - i
            ga = flush(at + 1, pb, qb, rb, ga)
            carry = fill(at, carry, pa, qa, ra)
            ga = flush(at, pa, qa, ra, ga)
            carry = fill(at - 1, carry, pb, qb, rb)
        return carry, ga

    rounds = chunks // ROUND
    carried = (last_ref[...], jnp.zeros((states, width), F32))
    enter(l, 1).wait()
    carried = lax.fori_loop(0, rounds // 2, body, carried)
    enter(l, 0).wait()
    _, ga = lax.fori_loop(rounds // 2, rounds, body, carried)
    ga_ref[...] = flush(0, pb, qb, rb, ga)
    gbc_ref[...] = gc_ref[...] + dot(masked[...], to_lanes(low_rank, states))


def scan_backward(low_rank, proj, log, dt, u, gy, last, gc, hs, *earlier):
    lanes, length, width = dt.shape
    states = log.shape[0]
    shape = jax.ShapeDtypeStruct
    tokens, state_spec, narrow = lane_spec(length, width), lane_spec(states, width), lane_spec(length, LANE)
    token = shape((lanes, length, width), F32)
    return pl.pallas_call(
        functools.partial(backward_kernel, low_rank, lanes),
        grid=(lanes,),
        in_specs=[narrow, whole_spec(states, width), tokens, tokens, tokens, state_spec, narrow]
        + [pl.BlockSpec(memory_space=pltpu.HBM)]
        + [pl.BlockSpec(memory_space=pl.ANY)] * len(earlier),
        out_specs=[tokens, tokens, narrow, state_spec],
        out_shape=[token, token, shape(proj.shape, F32), shape((lanes, states, width), F32)],
        scratch_shapes=[pltpu.VMEM((lanes, length * states, width), BF16)]
        + [pltpu.VMEM((CHUNK * states, width), BF16)] * 6
        + [
            pltpu.VMEM((states, length), F32),
            pltpu.VMEM((length, CHUNK * states), BF16),
            pltpu.VMEM((length, CHUNK * states), BF16),
            pltpu.SemaphoreType.DMA((lanes, 2)),
        ],
        compiler_params=pltpu.CompilerParams(vmem_limit_bytes=22 << 20),
        cost_estimate=cost(12, lanes, length, width, states),
        name="scan_backward",
    )(proj, log, dt, u, gy, last, gc, hs, *earlier)


def per_device(
    inputs,
    row_starts,
    norm_gain,
    in_weight,
    conv_weight,
    conv_bias,
    xproj_weight,
    dtproj_weight,
    dt_bias,
    decay_log,
    skip_gain,
    out_weight,
    output_grad,
):
    lane_count, length, shard_width = inputs.shape
    low_rank = dtproj_weight.shape[0]
    state_count = decay_log.shape[0]
    tap_count = conv_weight.shape[0]
    inner_width = conv_bias.shape[0]
    model_width = norm_gain.shape[0]
    starts = row_starts.astype(F32)
    carry_mask = (1.0 - starts)[:, :, None]
    mp_index, mp_size = lax.axis_index("mp"), lax.axis_size("mp")
    seq_index, seq_size = lax.axis_index("seq"), lax.axis_size("seq")
    mp_bits, seq_bits = bits_of("mp"), bits_of("seq")
    near_first = [int(format(k, "0%db" % len(mp_bits))[::-1], 2) for k in range(mp_size)]

    def blocks(array, axis, order):
        parts = [
            lax.dynamic_slice_in_dim(array, (mp_index ^ k) * shard_width, shard_width, axis) for k in order
        ]
        return jnp.concatenate(parts, axis=axis)

    x_parts, grad_parts = {0: inputs.astype(BF16)}, {}
    square = jnp.sum(jnp.square(inputs), axis=2)
    for bit in reversed(mp_bits):
        for k in list(x_parts):
            x_parts[k | bit] = swap(x_parts[k], "mp", bit)
        square = square + swap(square, "mp", bit)
    grad_parts[0] = after(output_grad.astype(BF16), x_parts[mp_bits[-1]])
    for bit in reversed(mp_bits[1:]):
        for k in list(grad_parts):
            grad_parts[k | bit] = swap(grad_parts[k], "mp", bit)
    near = list(range(mp_size))
    over = Reduction()
    per = shard_width * seq_size // model_width
    halves = seq_size // 2
    place = jnp.concatenate([seq_index[None].astype(jnp.int32), row_starts[:, 0]])
    orders = jnp.concatenate([over.order(per, mp_index), over.order(1, 0)])
    flat_order = over.flat_order()
    flags = [over.own(step)[None] for step in range(len(seq_bits))]
    span_more = FAR * starts[:, :, None]
    to_later = (jnp.arange(seq_size) > seq_index)[:, None, None]
    w_in = blocks(in_weight, 1, near).astype(BF16)
    w_back = blocks(in_weight, 1, near_first).astype(BF16)
    w_out = out_weight.astype(BF16)
    w_spread = blocks(out_weight, 1, near_first).astype(BF16)
    gain = blocks(norm_gain, 0, near)
    w_x = jnp.pad(xproj_weight.astype(BF16), ((0, 0), (0, -xproj_weight.shape[1] % LANE)))
    w_dt = jnp.pad(dtproj_weight.astype(BF16), ((0, -low_rank % LANE), (0, 0)))
    inv_rms = lax.rsqrt(square[:, :, None] / model_width + 1e-05)
    x_parts[near[-1]] = after(x_parts[near[-1]], place, orders, flat_order, span_more, *flags)
    x_whole = jnp.concatenate([x_parts[k] for k in near], axis=2)
    normed = (x_whole.astype(F32) * inv_rms * gain).astype(BF16)
    rim_count = 8
    rim_normed = from_behind(normed[:, length - rim_count :, :], "seq", 1)
    inner_act = jnp.einsum("ltd,de->lte", normed, w_in[0], preferred_element_type=F32).astype(BF16)
    gate_in = jnp.einsum("ltd,de->lte", normed, w_in[1], preferred_element_type=F32)
    rim_rows = jnp.einsum("ltd,de->lte", rim_normed, w_in[0], preferred_element_type=F32).astype(BF16)
    rim_rows = after(rim_rows, *grad_parts.values())
    rim_rows = (rim_rows.astype(F32) * carry_mask)[:, rim_count - (tap_count - 1) :]
    padded = jnp.concatenate([rim_rows, inner_act.astype(F32)], axis=1)
    conv_sum = conv_bias + conv_weight[0] * padded[:, 0:length]
    for tap in range(1, tap_count):
        conv_sum = conv_sum + conv_weight[tap] * padded[:, tap : tap + length]
    mixed = jax.nn.silu(conv_sum)
    mixed_low = mixed.astype(BF16)
    sent = jnp.einsum("lte,er->ltr", mixed_low, w_x, preferred_element_type=F32).astype(BF16)
    for bit in mp_bits[:-1]:
        sent = (sent.astype(F32) + swap(sent, "mp", bit).astype(F32)).astype(BF16)
    got = swap(sent, "mp", mp_bits[-1])
    for k in list(grad_parts):
        grad_parts[k] = after(grad_parts[k], sent)
        grad_parts[k | 1] = swap(grad_parts[k], "mp", 1)
    rim_pad = jnp.zeros((lane_count, rim_count, model_width), BF16)
    normed_more = jnp.concatenate([after(normed, sent), rim_normed, rim_pad], axis=1)
    grad_whole = jnp.concatenate(
        [
            sum(jnp.where(k == (mp_index ^ block), grad_parts[k], 0) for k in range(mp_size))
            for block in range(mp_size)
        ],
        axis=2,
    )
    grad_gated = jnp.einsum("ltd,ed->lte", grad_whole, w_out, preferred_element_type=F32)
    grad_scan = grad_gated * jax.nn.silu(gate_in)
    end_state, pulled, span, dt, source, slope_dt, projected = scan_ends(
        low_rank, sent, got, w_dt, dt_bias[None], decay_log, mixed, grad_scan
    )
    span = span + span_more
    flat = (1, lane_count * state_count, inner_width)
    edge = jnp.where(to_later, end_state.reshape(flat), (pulled * carry_mask).reshape(flat))
    spans = jnp.broadcast_to(
        span.reshape(1, lane_count, inner_width), (seq_size, lane_count, inner_width)
    )
    message = jnp.concatenate([edge, spans], axis=1).astype(BF16)
    message = jnp.pad(message, ((0, 0), (0, -message.shape[1] % 8), (0, 0)))
    groups = lax.all_to_all(message, "seq", 0, 0, tiled=True)
    y, grad_read, last, states_all = scan_forward(
        low_rank, place, projected, decay_log, dt, source, grad_scan, groups
    )
    scan_out = y + skip_gain * mixed
    gated = (scan_out * jax.nn.silu(gate_in)).astype(BF16)
    grad_gate = (grad_gated * scan_out * silu_slope(gate_in)).astype(BF16)
    half_width = model_width // 2
    first = [over.sent(normed, grad_gate)]
    first.append(over.sent(grad_whole, after(gated, first[0])))
    sum_first = Sum(over, first, (False, False), flags)
    sum_first.kept = [over.kept(after(normed, sum_first.message), grad_gate)]
    sum_first.kept.append(over.kept(grad_whole, after(gated, sum_first.kept[0])))
    turn, pull, part, grad_log = scan_backward(
        low_rank, projected, decay_log, dt, source, grad_scan, last, grad_read, states_all, *sum_first.kept
    )
    grad_slope = (turn + pull * mixed) * slope_dt
    grad_pre = grad_slope.astype(BF16)
    part = part + jnp.einsum("lte,re->ltr", grad_pre, w_dt, preferred_element_type=F32)
    sent = part.astype(BF16)
    for bit in mp_bits[:-1]:
        got = swap(sent, "mp", bit)
        if bit == 1:
            got = after(got, sum_first.next(sent))
        sent = (sent.astype(F32) + got.astype(F32)).astype(BF16)
    got = swap(sent, "mp", mp_bits[-1])
    grad_dt_w = jnp.einsum(
        "ltr,lte->re", projected.astype(BF16), after(grad_pre, sent), preferred_element_type=F32
    )[:low_rank]
    grad_projected = after(sent, grad_dt_w).astype(F32) + got.astype(F32)
    grad_projected = grad_projected.astype(BF16)
    grad_mixed = pull * dt + grad_scan * skip_gain + jnp.einsum(
        "ltr,er->lte", grad_projected, w_x, preferred_element_type=F32
    )
    grad_conv = grad_mixed * silu_slope(conv_sum)
    grad_conv_b = jnp.sum(grad_conv, axis=(0, 1))
    grad_conv_w = jnp.stack(
        [
            jnp.sum(grad_conv * padded[:, tap : tap + length], axis=(0, 1))
            for tap in range(tap_count)
        ]
    )
    grad_padded = jnp.pad(conv_weight[0] * grad_conv, ((0, 0), (0, tap_count - 1), (0, 0)))
    for tap in range(1, tap_count):
        grad_padded = grad_padded + jnp.pad(
            conv_weight[tap] * grad_conv, ((0, 0), (tap, tap_count - 1 - tap), (0, 0))
        )
    rim_sent = grad_padded[:, : tap_count - 1] * carry_mask
    rim_fill = jnp.zeros((lane_count, rim_count - (tap_count - 1), inner_width), F32)
    rim_tail = jnp.zeros((lane_count, rim_count, inner_width), F32)
    grad_more = jnp.concatenate(
        [grad_padded[:, tap_count - 1 :], rim_fill, rim_sent, rim_tail], axis=1
    ).astype(BF16)
    grad_x_w = jnp.einsum("ltr,lte->re", grad_projected, after(mixed_low, rim_sent), preferred_element_type=F32)
    small = jnp.concatenate(
        [
            grad_conv_w,
            grad_conv_b[None],
            jnp.sum(grad_slope, axis=(0, 1))[None],
            jnp.sum(grad_scan * mixed, axis=(0, 1))[None],
            jnp.sum(grad_log, axis=0),
            grad_dt_w,
            grad_x_w[: low_rank + 2 * state_count],
        ],
        axis=0,
    )
    small = jnp.pad(small, ((0, -small.shape[0] % (8 * seq_size)), (0, 0)))
    small_kept, small_sent = over.halves(small, 0)
    inner_sent = over.sent(normed_more, after(grad_more, grad_x_w))
    sum_inner = Sum(over, [inner_sent, small_sent], (False, True), flags)
    step = sum_first.next(sum_inner.message)
    sum_inner.kept = [over.kept(normed_more, after(grad_more, step)), small_kept]
    rim_back = from_behind(after(rim_sent, step), "seq", -1)
    out_sent = jnp.einsum(
        "lte,ed->ltd", after(gated, sum_inner.kept[0]), w_spread[:, half_width:], preferred_element_type=F32
    ).astype(BF16)
    out_kept = jnp.einsum(
        "lte,ed->ltd", after(gated, out_sent), w_spread[:, :half_width], preferred_element_type=F32
    )
    tail_zeros = jnp.zeros((lane_count, length - (tap_count - 1), inner_width), F32)
    grad_inner = grad_padded[:, tap_count - 1 :] + jnp.concatenate(
        [tail_zeros, after(rim_back, out_kept)], axis=1
    )
    grad_inner = grad_inner.astype(BF16)

    def back(part, cut):
        return jnp.einsum("lte,de->ltd", part[0], w_back[0, cut], preferred_element_type=F32) + jnp.einsum(
            "lte,de->ltd", part[1], w_back[1, cut], preferred_element_type=F32
        )

    back_sent = back((grad_inner, grad_gate), slice(half_width, None)).astype(BF16)
    back_kept = back((after(grad_inner, back_sent), grad_gate), slice(0, half_width))
    row_dot = jnp.sum(
        after(grad_inner, back_kept).astype(F32) * inner_act.astype(F32) + grad_gate.astype(F32) * gate_in,
        axis=2,
    )

    def as_rows(values, width):
        high = values.astype(BF16)
        low = (values - high.astype(F32)).astype(BF16)
        rows = jnp.concatenate([high, low], axis=1).reshape(lane_count, -1, width)
        return jnp.pad(rows, ((0, 0), (0, -rows.shape[1] % 16), (0, 0)))

    message = jnp.concatenate([out_sent, back_sent, as_rows(row_dot, half_width)], axis=1)
    step = sum_inner.next(message)
    step = sum_first.next(step)
    got = swap(after(message, step), "mp", 1)
    for bit in mp_bits[:-1]:
        if bit == 1:
            step = sum_inner.next(message)
            step = sum_first.next(step)
        message, out_kept, back_kept, row_dot = hop(after(got, step), out_kept, back_kept, row_dot)
        got = swap(message, "mp", 2 * bit)
    got = after(got, message)
    rows = got[:, 2 * length :][:, : 2 * length // shard_width].reshape(lane_count, 2 * length).astype(F32)
    row_dot = row_dot + rows[:, :length] + rows[:, length:]
    grad_own = back_kept + got[:, length : 2 * length].astype(F32)
    output = inputs + (out_kept + got[:, :length].astype(F32))
    unit_own = inputs * inv_rms
    grad_gain = jnp.sum(grad_own * unit_own, axis=(0, 1))
    input_grad = output_grad + inv_rms * (
        grad_own * gain[:shard_width] - unit_own * (row_dot[:, :, None] / model_width)
    )
    grad_gain = jnp.pad(grad_gain, (0, -shard_width % inner_width)).reshape(-1, inner_width)
    sum_inner.rider = jnp.pad(grad_gain, ((0, -grad_gain.shape[0] % 16), (0, 0)))
    step = sum_inner.next(grad_gain)
    step = sum_first.next(step)
    output, input_grad = after(output, step), after(input_grad, step)
    step = sum_inner.next(step)
    step = sum_inner.next(step)
    sum_first.run_out()
    second = 2 + halves
    in_shape, out_shape = (2, model_width, inner_width), out_weight.shape
    half = model_width // 2
    layout = [(0, 1, 0, 0, halves, False, 0, half), (0, 1, 0, 1, halves, False, 0, half)]
    ends = (sum_first.message, after(sum_first.got, step))
    if model_width // seq_size % LANE == 0:
        layout += [(1, None, second, 0, halves, True, half, half), (1, None, second, 1, halves, True, half, half)]
        in_w, out_w = settle(orders, [*ends, *ends], layout, [in_shape, out_shape])
    else:
        (in_w,) = settle(orders, [*ends], layout, [in_shape])
        rows = [p[half:].reshape(halves, -1, inner_width)[orders[second + 2 :]].reshape(half, -1) for p in ends]
        up = over.own(0) == 1
        rows = [jnp.where(up, rows[1], rows[0]), jnp.where(up, rows[0], rows[1])]
        out_w = jnp.concatenate(rows, axis=0).astype(F32).T
    sizes = [tap_count, 1, 1, 1, state_count, low_rank, low_rank + 2 * state_count]
    sum_inner.run_out()
    ends = (sum_inner.message, sum_inner.got)
    in_w = settle(orders, ends[:1], [(0, 0, 0, 0, halves, False, 0, half)], [in_shape], [in_w])
    parts = deal(flat_order, *ends, half, small.shape[0] // 2, sizes)
    (in_w,) = settle(orders, ends[1:], [(0, 0, 0, 1, halves, False, 0, half)], [in_shape], in_w)
    last = half + small.shape[0] // 2
    grad_gain = ends[0][last : last + 1].astype(F32) + ends[1][last : last + 1].astype(F32)
    return (
        output,
        input_grad,
        grad_gain.reshape(-1)[:shard_width],
        in_w,
        parts[0],
        parts[1][0],
        parts[6].T,
        parts[5],
        parts[2][0],
        parts[4],
        parts[3][0],
        out_w,
    )


def solution(mesh):
    in_specs = (
        P(None, "seq", "mp"),
        P(None, "seq"),
        P(),
        P(None, None, "mp"),
        P(None, "mp"),
        P("mp"),
        P("mp", None),
        P(None, "mp"),
        P("mp"),
        P(None, "mp"),
        P("mp"),
        P("mp", None),
        P(None, "seq", "mp"),
    )
    out_specs = (
        P(None, "seq", "mp"),
        P(None, "seq", "mp"),
        P("mp"),
        P(None, None, "mp"),
        P(None, "mp"),
        P("mp"),
        P("mp", None),
        P(None, "mp"),
        P("mp"),
        P(None, "mp"),
        P("mp"),
        P("mp", None),
    )
    return jax.shard_map(
        per_device, mesh=mesh, in_specs=in_specs, out_specs=out_specs, check_vma=False
    )
```

```python
import functools

import jax
import jax.numpy as jnp
from jax import lax
from jax.experimental import pallas as pl
from jax.experimental.pallas import tpu as pltpu
from jax.sharding import PartitionSpec as P

F32 = jnp.float32
BF16 = jnp.bfloat16
LOG2E = 1.4426950408889634
CHUNK = 32
ROUND = 4
LANE = 128
FAR = 1.0e4
VMEM = pl.BlockSpec(memory_space=pltpu.VMEM)


def swap(block, axis, bit):
    devices = lax.axis_size(axis)
    return lax.ppermute(block, axis, [(i, i ^ bit) for i in range(devices)])


def from_behind(block, axis, distance):
    devices = range(lax.axis_size(axis))
    route = [(i - distance, i) for i in devices if i - distance in devices]
    return lax.ppermute(block, axis, route)


def bits_of(axis):
    count = lax.axis_size(axis)
    bits = []
    while (1 << len(bits)) < count:
        bits.append(1 << len(bits))
    return bits


def after(array, *others):
    return lax.optimization_barrier((array, *others))[0]


class Reduction:
    def __init__(self):
        self.bits = bits_of("seq")
        self.orders = [list(self.bits), list(self.bits)]
        if len(self.bits) > 1:
            self.orders[1][:2] = self.bits[1], self.bits[0]
        self.index = lax.axis_index("seq")
        self.odd = lax.axis_index("mp") % 2
        self.mp = lax.axis_size("mp")
        self.count = lax.axis_size("seq")

    def own(self, step):
        even = (self.index & self.orders[0][step]) != 0
        odd = (self.index & self.orders[1][step]) != 0
        return jnp.where(self.odd == 1, odd, even).astype(jnp.int32)

    def swap(self, block, step):
        route = []
        for s in range(self.count):
            for m in range(self.mp):
                route.append((s * self.mp + m, (s ^ self.orders[m % 2][step]) * self.mp + m))
        return lax.ppermute(block, ("seq", "mp"), route)

    def halves(self, block, step):
        half = block.shape[0] // 2
        up = self.own(step)
        kept = lax.dynamic_slice_in_dim(block, up * half, half, 0)
        sent = lax.dynamic_slice_in_dim(block, (1 - up) * half, half, 0)
        return kept, sent

    def part(self, left, right, up):
        half = left.shape[2] // 2
        cut = lax.dynamic_slice_in_dim(left, up * half, half, 2)
        return jnp.einsum("lta,ltb->ab", cut, right, preferred_element_type=F32)

    def sent(self, left, right):
        return self.part(left, right, 1 - self.own(0)).astype(BF16)

    def kept(self, left, right):
        return self.part(left, right, self.own(0))

    def place(self):
        place = jnp.int32(0)
        for step in range(1, len(self.bits)):
            place = place * 2 + self.own(step)
        return place

    def order(self, per, turn):
        blocks = self.count // 2
        pieces = blocks // per
        at = jnp.arange(blocks)
        low, high = turn % pieces, turn // pieces
        source = (((at // per) ^ low) * per + at % per) ^ self.place()
        up = self.own(0) ^ high
        return jnp.concatenate([jnp.stack([up * blocks, (1 - up) * blocks]), source]).astype(jnp.int32)

    def flat_order(self):
        blocks = self.count // 2
        place = jnp.int32(0)
        for step in range(len(self.bits) - 1):
            place = place * 2 + self.own(step)
        return (jnp.arange(blocks) ^ place).astype(jnp.int32)


def advance_kernel(plan, flag_ref, *refs):
    refs = list(refs)
    sent_ref, got_ref = refs.pop(0), refs.pop(0)
    inputs, outputs = refs[: plan["inputs"]], refs[plan["inputs"] :]
    message = outputs.pop(0)
    up = flag_ref[0]
    at = 0
    for mode, rows, first in plan["blocks"]:
        if mode == "half":
            kept, new = inputs.pop(0), outputs.pop(0)
            half = rows // 2
            own = pl.multiple_of(up * half, half)
            other = pl.multiple_of((1 - up) * half, half)
            new[...] = kept[pl.ds(own, half), :].astype(F32) + got_ref[pl.ds(first + own, half), :].astype(F32)
            send = kept[pl.ds(other, half), :].astype(F32) + got_ref[pl.ds(first + other, half), :].astype(F32)
            message[at : at + half, :] = send.astype(BF16)
            at += half
        elif mode in ("flat", "sum", "hold"):
            kept = inputs.pop(0)
            total = (kept[...].astype(F32) + got_ref[first : first + rows, :].astype(F32)).astype(BF16)
            if mode != "sum":
                outputs.pop(0)[...] = total
            if mode != "hold":
                message[at : at + rows, :] = total
                at += rows
        elif mode == "enter":
            message[at : at + rows, :] = inputs.pop(0)[...].astype(BF16)
            at += rows
        elif mode == "grow":
            message[at : at + rows, :] = sent_ref[first : first + rows, :]
            message[at + rows : at + 2 * rows, :] = got_ref[first : first + rows, :]
            at += 2 * rows
        else:
            total = sent_ref[first : first + rows, :].astype(F32) + got_ref[first : first + rows, :].astype(F32)
            message[at : at + rows, :] = total.astype(BF16)
            at += rows


def advance(flag, sent, got, blocks, inputs):
    width = sent.shape[1]
    grown = {"half": 0.5, "hold": 0, "grow": 2}
    total = int(sum(rows * grown.get(mode, 1) for mode, rows, _ in blocks))
    shapes = [jax.ShapeDtypeStruct((total, width), BF16)]
    for mode, rows, _ in blocks:
        if mode == "half":
            shapes.append(jax.ShapeDtypeStruct((rows // 2, width), F32))
        elif mode in ("flat", "hold"):
            shapes.append(jax.ShapeDtypeStruct((rows, width), BF16))
    return pl.pallas_call(
        functools.partial(advance_kernel, {"inputs": len(inputs), "blocks": blocks}),
        in_specs=[pl.BlockSpec(memory_space=pltpu.SMEM)] + [VMEM] * (2 + len(inputs)),
        out_specs=[VMEM] * len(shapes),
        out_shape=shapes,
        compiler_params=pltpu.CompilerParams(vmem_limit_bytes=12 << 20),
        name="advance",
    )(flag, sent, got, *inputs)


class Sum:
    def __init__(self, over, sent, flat, flags, rows=None):
        self.over, self.flat, self.flags = over, flat, flags
        self.kept, self.rider, self.count = None, None, 0
        self.rows = rows or [block.shape[0] for block in sent]
        self.message = sent[0] if rows else jnp.concatenate([block.astype(BF16) for block in sent], axis=0)
        self.got = over.swap(self.message, 0)

    def next(self, *earlier):
        steps = len(self.over.bits)
        k = self.count
        got = after(self.got, *earlier) if earlier else self.got
        blocks, inputs, rows, kept, first = [], [], [], [], 0
        for m, size in enumerate(self.rows):
            mode = "half" if k < steps - 1 else "sum" if k == steps - 1 else "grow"
            if self.flat[m]:
                mode = {steps - 2: "flat", steps - 1: "hold", steps: "enter"}.get(k, mode)
            if mode == "enter":
                size = self.kept[m].shape[0]
            blocks.append((mode, size, first))
            if mode != "grow":
                inputs.append(self.kept[m])
            first += 0 if mode == "enter" else size
            rows.append({"half": size // 2, "hold": 0, "grow": 2 * size}.get(mode, size))
        if self.rider is not None and k == steps - 1:
            blocks.append(("enter", self.rider.shape[0], 0))
            inputs.append(self.rider)
        elif self.rider is not None and k >= steps:
            blocks.append(("ride", self.rider.shape[0], first))
        flag = self.flags[min(k + 1, steps - 1)]
        self.message, *kept = advance(flag, self.message, got, blocks, inputs)
        for m, (mode, _, _) in enumerate(blocks[: len(rows)]):
            if mode in ("half", "flat", "hold"):
                self.kept[m] = kept.pop(0)
        self.rows = rows
        self.count = k + 1
        step = self.count if self.count < steps else 2 * steps - 1 - self.count
        self.got = self.over.swap(self.message, step)
        return self.message

    def run_out(self):
        while self.count < 2 * len(self.over.bits) - 1:
            self.next()


def silu_slope(values):
    logistic = jax.nn.sigmoid(values)
    return logistic * (1.0 + values * (1.0 - logistic))


def cost(ops, lanes, length, width, states):
    work = lanes * length * width * states
    return pl.CostEstimate(flops=ops * work * 16, bytes_accessed=work * 2, transcendentals=work)


def settle_kernel(names, layout, order_ref, *refs, starts=True, waits=True):
    parts, outs = refs[: len(layout)], refs[-2 - names : -2]
    wide, sems = refs[-2:]
    copies, at = [], 0
    for part, (out, lead, which, first, blocks, turned, offset, count) in zip(parts, layout, strict=True):
        size = count // blocks
        for b in range(blocks):
            source = order_ref[which + 2 + b]
            goal = pl.multiple_of((order_ref[which + first] + b) * size, size)
            ref = outs[out] if lead is None else outs[out].at[lead]
            if turned:
                spot = wide.at[at : at + part.shape[1], 0:size]
                target = ref.at[:, pl.ds(goal, size)]
            else:
                spot = wide.at[at : at + size, 0 : part.shape[1]]
                target = ref.at[pl.ds(goal, size), :]
            at += part.shape[1] if turned else size
            copies.append(pltpu.make_async_copy(spot, target, sems.at[len(copies)]))
            if starts:
                rows = part[pl.ds(pl.multiple_of(offset + source * size, size), size), :].astype(F32)
                spot[...] = jnp.transpose(rows) if turned else rows
                copies[-1].start()
    for copy in copies:
        if waits:
            copy.wait()


def settle(orders, parts, layout, shapes, into=()):
    any_space = pl.BlockSpec(memory_space=pl.ANY)
    rows = sum(p.shape[1] * l[4] if l[5] else l[7] for p, l in zip(parts, layout, strict=True))
    width = max(l[7] // l[4] if l[5] else p.shape[1] for p, l in zip(parts, layout, strict=True))
    count = sum(l[4] for l in layout)
    return pl.pallas_call(
        functools.partial(settle_kernel, len(shapes), layout),
        in_specs=[pl.BlockSpec(memory_space=pltpu.SMEM)] + [VMEM] * len(parts) + [any_space] * len(into),
        out_specs=[any_space] * len(shapes),
        out_shape=[jax.ShapeDtypeStruct(s, F32) for s in shapes],
        input_output_aliases={1 + len(parts) + k: k for k in range(len(into))},
        scratch_shapes=[pltpu.VMEM((rows, width), F32), pltpu.SemaphoreType.DMA((count,))],
        compiler_params=pltpu.CompilerParams(vmem_limit_bytes=16 << 20),
        name="settle",
    )(orders, *parts, *into)


def deal_rows(sizes, offset, order_ref, own_ref, late_ref, outs, rows):
    blocks = order_ref.shape[0]
    size = rows.shape[0] // blocks
    for b in range(blocks):
        source = order_ref[b]
        for part, first in ((own_ref, 0), (late_ref, blocks // 2)):

            @pl.when(jnp.logical_and(source >= first, source < first + blocks // 2))
            def _():
                at = pl.ds(pl.multiple_of(offset + (source - first) * size, size), size)
                rows[b * size : (b + 1) * size, :] = part[at, :].astype(F32)

    at = 0
    for out, count in zip(outs, sizes, strict=True):
        out[...] = rows[at : at + count, :]
        at += count


def finish_kernel(sizes, layout, offset, last, order_ref, flat_ref, own_ref, late_ref, into_ref, *refs):
    out, small, (total, rows, wide, sems) = refs[0], refs[1:-4], refs[-4:]
    settle_kernel(1, layout, order_ref, late_ref, out, wide, sems, waits=False)
    deal_rows(sizes, offset, flat_ref, own_ref, late_ref, small, rows)
    total[...] = own_ref[last : last + 16, :].astype(F32) + late_ref[last : last + 16, :].astype(F32)
    settle_kernel(1, layout, order_ref, late_ref, out, wide, sems, starts=False)


def finish(orders, flat_order, own, late, layout, offset, count, sizes, into):
    width = own.shape[1]
    any_space, smem = pl.BlockSpec(memory_space=pl.ANY), pl.BlockSpec(memory_space=pltpu.SMEM)
    shape = jax.ShapeDtypeStruct
    return pl.pallas_call(
        functools.partial(finish_kernel, sizes, layout, offset, offset + count),
        in_specs=[smem, smem, VMEM, VMEM, any_space],
        out_specs=[any_space] + [VMEM] * (len(sizes) + 1),
        out_shape=[shape(into.shape, F32)] + [shape((n, width), F32) for n in sizes] + [shape((16, width), F32)],
        input_output_aliases={4: 0},
        scratch_shapes=[
            pltpu.VMEM((2 * count, width), F32),
            pltpu.VMEM((layout[0][7], width), F32),
            pltpu.SemaphoreType.DMA((layout[0][4],)),
        ],
        compiler_params=pltpu.CompilerParams(vmem_limit_bytes=16 << 20),
        name="finish",
    )(orders, flat_order, own, late, into)


def hop_kernel(got_ref, out_ref, back_ref, row_ref, message, other, out_new, back_new, row_new):
    lanes, length, width = out_ref.shape
    half = width // 2
    for l in range(lanes):
        for m, (kept, new, sent) in enumerate(((out_ref, out_new, other), (back_ref, back_new, message))):
            o = slice(m * length, (m + 1) * length)
            new[l] = kept[l, :, :half] + got_ref[l, o, :half].astype(F32)
            send = kept[l, :, half:] + got_ref[l, o, half:].astype(F32)
            sent[l, :length, :] = send.astype(BF16)
        rows = got_ref[l, 2 * length :, :].astype(F32)
        came = jnp.concatenate([rows[r : r + 1] for r in range(2 * length // width)], axis=1)
        total = row_ref[l : l + 1, :] + came[:, :length] + came[:, length:]
        row_new[l : l + 1, :] = total
        high = total.astype(BF16).astype(F32)
        both = jnp.concatenate([high, total - high], axis=1)
        pieces = [both[:, at : at + half] for at in range(0, 2 * length, half)]
        pieces.append(jnp.zeros((message.shape[1] - length - len(pieces), half), F32))
        message[l, length:, :] = jnp.concatenate(pieces, axis=0).astype(BF16)


def hop(got, out_kept, back_kept, row_dot):
    lanes, length, width = out_kept.shape
    shape = jax.ShapeDtypeStruct
    half = shape((lanes, length, width // 2), F32)
    rows = length - (-(4 * length // width) // 16) * 16
    return pl.pallas_call(
        hop_kernel,
        in_specs=[VMEM] * 4,
        out_specs=[VMEM] * 5,
        out_shape=[
            shape((lanes, rows, width // 2), BF16),
            shape((lanes, length, width // 2), BF16),
            half,
            half,
            shape(row_dot.shape, F32),
        ],
        compiler_params=pltpu.CompilerParams(vmem_limit_bytes=12 << 20),
        name="hop",
    )(got, out_kept, back_kept, row_dot)


def product_kernel(flag_ref, left_ref, right_ref, more_ref, message):
    half = message.shape[0] - more_ref.shape[0]
    at = pl.multiple_of((1 - flag_ref[0]) * half, half)
    for block in range(0, half, min(half, 256)):
        size = min(half, 256)
        cut = left_ref[:, pl.ds(pl.multiple_of(at + block, size), size)]
        total = lax.dot_general(cut, right_ref[...], (((0,), (0,)), ((), ())), preferred_element_type=F32)
        message[block : block + size, :] = total.astype(BF16)
    message[half:, :] = more_ref[...].astype(BF16)


def sent_product(flag, left, right, more):
    half, width = left.shape[1] // 2, right.shape[1]
    return pl.pallas_call(
        product_kernel,
        in_specs=[pl.BlockSpec(memory_space=pltpu.SMEM)] + [VMEM] * 3,
        out_specs=VMEM,
        out_shape=jax.ShapeDtypeStruct((half + more.shape[0], width), BF16),
        compiler_params=pltpu.CompilerParams(vmem_limit_bytes=16 << 20),
        name="sent_product",
    )(flag, left, right, more)


def pack_kernel(sizes, flag_ref, sent_ref, *refs):
    parts, (message, kept, rows) = refs[:-3], refs[-3:]
    at = 0
    for part, size in zip(parts, sizes, strict=True):
        if part.ndim == 3:
            total = part[0]
            for l in range(1, part.shape[0]):
                total = total + part[l]
            rows[at : at + size, :] = total
        else:
            rows[at : at + size, :] = part[0:size, :]
        at += size
    rows[at:, :] = jnp.zeros((rows.shape[0] - at, rows.shape[1]), F32)
    half, first = kept.shape[0], sent_ref.shape[0]
    up = flag_ref[0]
    kept[...] = rows[pl.ds(pl.multiple_of(up * half, half), half), :]
    message[0:first, :] = sent_ref[...]
    message[first:, :] = rows[pl.ds(pl.multiple_of((1 - up) * half, half), half), :].astype(BF16)


def pack(flag, sent, parts, sizes, half):
    width = sent.shape[1]
    shape = jax.ShapeDtypeStruct
    return pl.pallas_call(
        functools.partial(pack_kernel, sizes),
        in_specs=[pl.BlockSpec(memory_space=pltpu.SMEM)] + [VMEM] * (1 + len(parts)),
        out_specs=[VMEM] * 2,
        out_shape=[shape((sent.shape[0] + half, width), BF16), shape((half, width), F32)],
        scratch_shapes=[pltpu.VMEM((2 * half, width), F32)],
        compiler_params=pltpu.CompilerParams(vmem_limit_bytes=8 << 20),
        name="pack",
    )(flag, sent, *parts)


def iota(shape, dim):
    return lax.broadcasted_iota(jnp.int32, shape, dim)


def widen(part, width):
    return jnp.concatenate([part] * (width // part.shape[1]), axis=1)


def dot(a, b):
    return jnp.dot(a, b, preferred_element_type=F32)


def dot_t(a, b):
    return lax.dot_general(a, b, (((1,), (1,)), ((), ())), preferred_element_type=F32)


def row_of(ref, t, count):
    return jnp.broadcast_to(ref[pl.ds(t, 1), :], (count, ref.shape[1]))


def rows_of(i, count):
    return pl.ds(pl.multiple_of(i * count, count), count)


def chunk_columns(ref, i):
    per = LANE // CHUNK
    tile = ref[:, rows_of(i // per, LANE)]
    return pltpu.roll(tile, LANE - (i % per) * CHUNK, 1)


def spread_column(tile, j, width):
    part = jnp.broadcast_to(tile[:, j : j + 1], (tile.shape[0], LANE))
    return widen(part, width)


def selectors(states):
    wide = CHUNK * states
    per_state = iota((states, wide), 1) % states == iota((states, wide), 0)
    per_step = iota((CHUNK, wide), 1) // states == iota((CHUNK, wide), 0)
    return per_state.astype(F32), per_step.astype(F32)


def from_lanes(first, states):
    shape = (LANE, CHUNK * states)
    return (iota(shape, 0) == first + iota(shape, 1) % states).astype(BF16)


def to_lanes(first, states):
    shape = (CHUNK * states, LANE)
    return (iota(shape, 1) == first + iota(shape, 0) % states).astype(BF16)


def by_step(proj, lanes, per_step):
    spread = dot(proj, lanes)
    return spread * jnp.concatenate([per_step] * (spread.shape[0] // CHUNK), axis=0)


def ends_kernel(
    low_rank, sent_ref, got_ref, wdt_ref, bias_ref, log_ref, mixed_ref, gy_ref,
    end_ref, pull_ref, span_ref, dt_ref, u_ref, sig_ref, proj_ref,
    ahead, behind, left_b, left_c, xa, xb, ya, yb,
):
    length, width = dt_ref.shape
    states = log_ref.shape[0]
    rate = -jnp.exp(log_ref[...]) * LOG2E
    per_state, per_step = selectors(states)
    chunks = length // CHUNK
    upto = (iota((length, length), 1) <= iota((length, length), 0)).astype(BF16)
    after = (iota((length, length), 1) > iota((length, length), 0)).astype(BF16)
    proj = sent_ref[...].astype(F32) + got_ref[...].astype(F32)
    proj_ref[...] = proj
    proj = proj.astype(BF16)
    for first, left in ((low_rank, left_b), (low_rank + states, left_c)):
        spread = by_step(proj, from_lanes(first, states), per_step)
        for i in range(chunks):
            flat = jnp.sum(spread[i * CHUNK : (i + 1) * CHUNK], axis=0, keepdims=True)
            left[i * states : (i + 1) * states, :] = (flat * per_state).astype(BF16)
    block = min(128, length)
    for i in range(length // block):
        o = slice(i * block, (i + 1) * block)
        pre = dot(proj[o], wdt_ref[...]) + bias_ref[...]
        small = jnp.exp(-jnp.abs(pre))
        one = 1.0 + small
        series = small * (1.0 - small * (0.5 - small * (1.0 / 3.0)))
        dt = jnp.maximum(pre, 0.0) + jnp.where(small < 1e-3, series, jnp.log(one))
        dt_ref[o, :] = dt
        u_ref[o, :] = dt * mixed_ref[o, :]
        sig_ref[o, :] = jnp.where(pre >= 0.0, 1.0, small) / one
    dt = dt_ref[...]
    high = dt.astype(BF16)
    low = (dt - high.astype(F32)).astype(BF16)
    ahead[...] = dot(upto, high) + dot(upto, low)
    behind[...] = dot(after, high) + dot(after, low)
    span_ref[...] = ahead[length - 1 : length, :]
    xb[...] = jnp.zeros(xb.shape, BF16)
    yb[...] = jnp.zeros(yb.shape, BF16)

    def flush(i, x, y, sums):
        o = rows_of(jnp.maximum(i, 0), states)
        return sums[0] + dot(left_b[o, :], x[...]), sums[1] + dot(left_c[o, :], y[...])

    def fill(i, x, y):
        for j in range(CHUNK):
            t = i * CHUNK + j
            s = slice(j * states, (j + 1) * states)
            to_end = jnp.exp2(row_of(behind, t, states) * rate)
            x[s, :] = (to_end * row_of(u_ref, t, states)).astype(BF16)
            to_here = jnp.exp2(row_of(ahead, t, states) * rate)
            y[s, :] = (to_here * row_of(gy_ref, t, states)).astype(BF16)

    def body(k, sums):
        for i in range(0, ROUND, 2):
            at = ROUND * k + i
            sums = flush(at - 1, xb, yb, sums)
            fill(at, xa, ya)
            sums = flush(at, xa, ya, sums)
            fill(at + 1, xb, yb)
        return sums

    zero = jnp.zeros((states, width), F32)
    sums = lax.fori_loop(0, chunks // ROUND, body, (zero, zero))
    sums = flush(chunks - 1, xb, yb, sums)
    end_ref[...] = sums[0]
    pull_ref[...] = sums[1]


def lane_spec(*shape):
    return pl.BlockSpec((None, *shape), lambda l: (l,) + (0,) * len(shape))


def whole_spec(*shape):
    return pl.BlockSpec(shape, lambda l: (0,) * len(shape))


def scan_ends(low_rank, sent, got, w_dt, bias, log, mixed, gy):
    lanes, length, width = mixed.shape
    states = log.shape[0]
    shape = jax.ShapeDtypeStruct
    token = shape((lanes, length, width), F32)
    state = shape((lanes, states, width), F32)
    tokens, state_spec, narrow = lane_spec(length, width), lane_spec(states, width), lane_spec(length, LANE)
    return pl.pallas_call(
        functools.partial(ends_kernel, low_rank),
        grid=(lanes,),
        in_specs=[
            narrow,
            narrow,
            whole_spec(*w_dt.shape),
            whole_spec(1, width),
            whole_spec(states, width),
            tokens,
            tokens,
        ],
        out_specs=[state_spec, state_spec, lane_spec(1, width), tokens, tokens, tokens, narrow],
        out_shape=[state, state, shape((lanes, 1, width), F32)]
        + [pltpu.HBM((lanes, length, width), F32)] * 3
        + [shape(sent.shape, F32)],
        scratch_shapes=[pltpu.VMEM((length, width), F32)] * 2
        + [pltpu.VMEM((length // CHUNK * states, CHUNK * states), BF16)] * 2
        + [pltpu.VMEM((CHUNK * states, width), BF16)] * 4,
        compiler_params=pltpu.CompilerParams(vmem_limit_bytes=14 << 20),
        cost_estimate=cost(8, lanes, length, width, states),
        name="scan_ends",
    )(sent, got, w_dt, bias, log, mixed, gy)


def forward_kernel(
    low_rank, lanes, place_ref, proj_ref, log_ref, dt_ref, u_ref, gy_ref, got_ref,
    y_ref, gc_ref, last_ref, hs_ref,
    kept, pa, pb, cols, left_c, masked, sems,
):
    length, width = dt_ref.shape
    states = log_ref.shape[0]
    l = pl.program_id(0)
    rate = -jnp.exp(log_ref[...]) * LOG2E
    _, per_step = selectors(states)
    wide = CHUNK * states
    chunks = length // CHUNK
    groups = got_ref.shape[0]
    place = place_ref[0]

    half = chunks // 2 * wide

    def leave(slot, part):
        rows = pl.ds(part * half, half)
        return pltpu.make_async_copy(kept.at[slot, rows, :], hs_ref.at[slot, rows, :], sems.at[slot, part])

    zero = jnp.zeros((states, width), F32)

    def join(g, total, use):
        at = lanes * states
        spans = got_ref[g, at : at + lanes, :].astype(F32)
        span = jnp.sum(jnp.where(iota(spans.shape, 0) == l, spans, 0.0), axis=0, keepdims=True)
        factor = jnp.exp2(span * rate)
        return jnp.where(use, total * factor + got_ref[g, rows_of(l, states), :].astype(F32), total)

    begin = last = zero
    for g in range(groups):
        begin = join(g, begin, g < place)
        h = groups - 1 - g
        last = join(h, last, h > place)
    last_ref[...] = last
    begin = jnp.where(place_ref[1 + l] != 0, 0.0, begin)
    proj = proj_ref[...]
    cols[...] = jnp.transpose(proj)[low_rank : low_rank + states]
    spread = by_step(proj.astype(BF16), from_lanes(low_rank + states, states), per_step)
    left_c[...] = spread.astype(BF16)

    def flush(i, p):
        o = rows_of(jnp.maximum(i, 0), CHUNK)
        h = p[...]
        y_ref[o, :] = dot(left_c[o, :], h)
        masked[o, :] = (dot_t(gy_ref[o, :].astype(BF16), h) * per_step).astype(BF16)

    def fill(i, state, p):
        b_tile = chunk_columns(cols, i)
        low = state.astype(BF16)
        for j in range(CHUNK):
            t = i * CHUNK + j
            b = spread_column(b_tile, j, width)
            decay = jnp.exp2(row_of(dt_ref, t, states) * rate)
            state = decay * state + row_of(u_ref, t, states) * b
            kept[l, rows_of(t, states), :] = low
            low = state.astype(BF16)
            p[j * states : (j + 1) * states, :] = low
        return state

    def body(k, state):
        for i in range(0, ROUND, 2):
            at = ROUND * k + i
            flush(at - 1, pb)
            state = fill(at, state, pa)
            flush(at, pa)
            state = fill(at + 1, state, pb)
        return state

    rounds = chunks // ROUND
    state = lax.fori_loop(0, rounds // 2, body, begin)
    leave(l, 0).start()
    lax.fori_loop(rounds // 2, rounds, body, state)
    leave(l, 1).start()
    flush(chunks - 1, pb)
    gc_ref[...] = dot(masked[...], to_lanes(low_rank + states, states))

    @pl.when(l == lanes - 1)
    def _():
        for slot in range(lanes):
            for part in range(2):
                leave(slot, part).wait()


def scan_forward(low_rank, place, proj, log, dt, u, gy, got):
    lanes, length, width = dt.shape
    states = log.shape[0]
    shape = jax.ShapeDtypeStruct
    tokens, state_spec, narrow = lane_spec(length, width), lane_spec(states, width), lane_spec(length, LANE)
    return pl.pallas_call(
        functools.partial(forward_kernel, low_rank, lanes),
        grid=(lanes,),
        in_specs=[
            pl.BlockSpec(memory_space=pltpu.SMEM),
            narrow,
            whole_spec(states, width),
            tokens,
            tokens,
            tokens,
            whole_spec(*got.shape),
        ],
        out_specs=[tokens, narrow, state_spec, pl.BlockSpec(memory_space=pltpu.HBM)],
        out_shape=[
            shape((lanes, length, width), F32),
            shape(proj.shape, F32),
            shape((lanes, states, width), F32),
            shape((lanes, length * states, width), BF16),
        ],
        scratch_shapes=[pltpu.VMEM((lanes, length * states, width), BF16)]
        + [pltpu.VMEM((CHUNK * states, width), BF16)] * 2
        + [
            pltpu.VMEM((states, length), F32),
            pltpu.VMEM((length, CHUNK * states), BF16),
            pltpu.VMEM((length, CHUNK * states), BF16),
            pltpu.SemaphoreType.DMA((lanes, 2)),
        ],
        compiler_params=pltpu.CompilerParams(vmem_limit_bytes=20 << 20),
        cost_estimate=cost(8, lanes, length, width, states),
        name="scan_forward",
    )(place, proj, log, dt, u, gy, got)


def backward_kernel(
    low_rank, lanes, proj_ref, log_ref, dt_ref, u_ref, gy_ref, last_ref, gc_ref, hs_ref, *refs
):
    (turn_ref, pull_ref, gbc_ref, ga_ref,
     kept, pa, pb, qa, qb, ra, rb, cols, left_b, masked, sems) = refs[-15:]
    length, width = dt_ref.shape
    states = log_ref.shape[0]
    l = pl.program_id(0)
    plain = -jnp.exp(log_ref[...])
    rate = plain * LOG2E
    rate_low = plain.astype(BF16)
    per_state, per_step = selectors(states)
    per_state_low, per_step_low = per_state.astype(BF16), per_step.astype(BF16)
    chunks = length // CHUNK

    half = length // 2 * states

    def enter(slot, part):
        rows = pl.ds(part * half, half)
        return pltpu.make_async_copy(hs_ref.at[slot, rows, :], kept.at[slot, rows, :], sems.at[slot, part])

    @pl.when(l == 0)
    def _():
        for slot in range(lanes):
            for part in (1, 0):
                enter(slot, part).start()

    for ref in (pb, qb, rb):
        ref[...] = jnp.zeros(ref.shape, BF16)
    proj = proj_ref[...]
    cols[...] = jnp.transpose(proj)[low_rank + states : low_rank + 2 * states]
    left_b[...] = by_step(proj.astype(BF16), from_lanes(low_rank, states), per_step).astype(BF16)

    def flush(i, p, q, r, ga):
        o = rows_of(jnp.minimum(i, chunks - 1), CHUNK)
        grad = p[...]
        pull_ref[o, :] = dot(left_b[o, :], grad)
        masked[o, :] = (dot_t(u_ref[o, :].astype(BF16), grad) * per_step).astype(BF16)
        turn_ref[o, :] = dot(per_step_low, q[...])
        return ga + dot(per_state_low, r[...])

    def fill(i, carry, p, q, r):
        c_tile = chunk_columns(cols, i)
        for j in reversed(range(CHUNK)):
            t = i * CHUNK + j
            s = slice(j * states, (j + 1) * states)
            c = spread_column(c_tile, j, width)
            dt = row_of(dt_ref, t, states)
            grad = carry + row_of(gy_ref, t, states) * c
            carry = jnp.exp2(dt * rate) * grad
            p[s, :] = grad.astype(BF16)
            turn = carry.astype(BF16) * kept[l, rows_of(t, states), :] * rate_low
            q[s, :] = turn
            r[s, :] = turn * dt.astype(BF16)
        return carry

    def body(k, carried):
        carry, ga = carried
        for i in range(0, ROUND, 2):
            at = chunks - 1 - ROUND * k - i
            ga = flush(at + 1, pb, qb, rb, ga)
            carry = fill(at, carry, pa, qa, ra)
            ga = flush(at, pa, qa, ra, ga)
            carry = fill(at - 1, carry, pb, qb, rb)
        return carry, ga

    rounds = chunks // ROUND
    carried = (last_ref[...], jnp.zeros((states, width), F32))
    enter(l, 1).wait()
    carried = lax.fori_loop(0, rounds // 2, body, carried)
    enter(l, 0).wait()
    _, ga = lax.fori_loop(rounds // 2, rounds, body, carried)
    ga_ref[...] = flush(0, pb, qb, rb, ga)
    gbc_ref[...] = gc_ref[...] + dot(masked[...], to_lanes(low_rank, states))


def scan_backward(low_rank, proj, log, dt, u, gy, last, gc, hs, *earlier):
    lanes, length, width = dt.shape
    states = log.shape[0]
    shape = jax.ShapeDtypeStruct
    tokens, state_spec, narrow = lane_spec(length, width), lane_spec(states, width), lane_spec(length, LANE)
    token = shape((lanes, length, width), F32)
    return pl.pallas_call(
        functools.partial(backward_kernel, low_rank, lanes),
        grid=(lanes,),
        in_specs=[narrow, whole_spec(states, width), tokens, tokens, tokens, state_spec, narrow]
        + [pl.BlockSpec(memory_space=pltpu.HBM)]
        + [pl.BlockSpec(memory_space=pl.ANY)] * len(earlier),
        out_specs=[tokens, tokens, narrow, state_spec],
        out_shape=[token, token, shape(proj.shape, F32), shape((lanes, states, width), F32)],
        scratch_shapes=[pltpu.VMEM((lanes, length * states, width), BF16)]
        + [pltpu.VMEM((CHUNK * states, width), BF16)] * 6
        + [
            pltpu.VMEM((states, length), F32),
            pltpu.VMEM((length, CHUNK * states), BF16),
            pltpu.VMEM((length, CHUNK * states), BF16),
            pltpu.SemaphoreType.DMA((lanes, 2)),
        ],
        compiler_params=pltpu.CompilerParams(vmem_limit_bytes=22 << 20),
        cost_estimate=cost(12, lanes, length, width, states),
        name="scan_backward",
    )(proj, log, dt, u, gy, last, gc, hs, *earlier)


def per_device(
    inputs,
    row_starts,
    norm_gain,
    in_weight,
    conv_weight,
    conv_bias,
    xproj_weight,
    dtproj_weight,
    dt_bias,
    decay_log,
    skip_gain,
    out_weight,
    output_grad,
):
    lane_count, length, shard_width = inputs.shape
    low_rank = dtproj_weight.shape[0]
    state_count = decay_log.shape[0]
    tap_count = conv_weight.shape[0]
    inner_width = conv_bias.shape[0]
    model_width = norm_gain.shape[0]
    starts = row_starts.astype(F32)
    carry_mask = (1.0 - starts)[:, :, None]
    mp_index, mp_size = lax.axis_index("mp"), lax.axis_size("mp")
    seq_index, seq_size = lax.axis_index("seq"), lax.axis_size("seq")
    mp_bits, seq_bits = bits_of("mp"), bits_of("seq")
    near_first = [int(format(k, "0%db" % len(mp_bits))[::-1], 2) for k in range(mp_size)]

    def blocks(array, axis, order):
        parts = [
            lax.dynamic_slice_in_dim(array, (mp_index ^ k) * shard_width, shard_width, axis) for k in order
        ]
        return jnp.concatenate(parts, axis=axis)

    x_parts, grad_parts = {0: inputs.astype(BF16)}, {}
    square = jnp.sum(jnp.square(inputs), axis=2)
    for bit in reversed(mp_bits):
        for k in list(x_parts):
            x_parts[k | bit] = swap(x_parts[k], "mp", bit)
        square = square + swap(square, "mp", bit)
    grad_parts[0] = after(output_grad.astype(BF16), x_parts[mp_bits[-1]])
    for bit in reversed(mp_bits[1:]):
        for k in list(grad_parts):
            grad_parts[k | bit] = swap(grad_parts[k], "mp", bit)
    near = list(range(mp_size))
    over = Reduction()
    per = shard_width * seq_size // model_width
    halves = seq_size // 2
    place = jnp.concatenate([seq_index[None].astype(jnp.int32), row_starts[:, 0]])
    orders = jnp.concatenate([over.order(per, mp_index), over.order(1, 0)])
    flat_order = over.flat_order()
    flags = [over.own(step)[None] for step in range(len(seq_bits))]
    span_more = FAR * starts[:, :, None]
    to_later = (jnp.arange(seq_size) > seq_index)[:, None, None]
    w_in = blocks(in_weight, 1, near).astype(BF16)
    w_back = blocks(in_weight, 1, near_first).astype(BF16)
    w_out = out_weight.astype(BF16)
    w_spread = blocks(out_weight, 1, near_first).astype(BF16)
    gain = blocks(norm_gain, 0, near)
    w_x = jnp.pad(xproj_weight.astype(BF16), ((0, 0), (0, -xproj_weight.shape[1] % LANE)))
    w_dt = jnp.pad(dtproj_weight.astype(BF16), ((0, -low_rank % LANE), (0, 0)))
    inv_rms = lax.rsqrt(square[:, :, None] / model_width + 1e-05)
    x_parts[near[-1]] = after(x_parts[near[-1]], place, orders, flat_order, span_more, *flags)
    x_whole = jnp.concatenate([x_parts[k] for k in near], axis=2)
    normed = (x_whole.astype(F32) * inv_rms * gain).astype(BF16)
    rim_count = 8
    rim_normed = from_behind(normed[:, length - rim_count :, :], "seq", 1)
    inner_act = jnp.einsum("ltd,de->lte", normed, w_in[0], preferred_element_type=F32).astype(BF16)
    gate_in = jnp.einsum("ltd,de->lte", normed, w_in[1], preferred_element_type=F32)
    rim_rows = jnp.einsum("ltd,de->lte", rim_normed, w_in[0], preferred_element_type=F32).astype(BF16)
    rim_rows = after(rim_rows, *grad_parts.values())
    rim_rows = (rim_rows.astype(F32) * carry_mask)[:, rim_count - (tap_count - 1) :]
    padded = jnp.concatenate([rim_rows, inner_act.astype(F32)], axis=1)
    conv_sum = conv_bias + conv_weight[0] * padded[:, 0:length]
    for tap in range(1, tap_count):
        conv_sum = conv_sum + conv_weight[tap] * padded[:, tap : tap + length]
    mixed = jax.nn.silu(conv_sum)
    mixed_low = mixed.astype(BF16)
    sent = jnp.einsum("lte,er->ltr", mixed_low, w_x, preferred_element_type=F32).astype(BF16)
    for bit in mp_bits[:-1]:
        sent = (sent.astype(F32) + swap(sent, "mp", bit).astype(F32)).astype(BF16)
    got = swap(sent, "mp", mp_bits[-1])
    for k in list(grad_parts):
        grad_parts[k] = after(grad_parts[k], sent)
        grad_parts[k | 1] = swap(grad_parts[k], "mp", 1)
    normed_more = jnp.concatenate(
        [after(normed, sent).reshape(-1, model_width), rim_normed.reshape(-1, model_width)], axis=0
    )[None]
    grad_whole = jnp.concatenate(
        [
            sum(jnp.where(k == (mp_index ^ block), grad_parts[k], 0) for k in range(mp_size))
            for block in range(mp_size)
        ],
        axis=2,
    )
    grad_gated = jnp.einsum("ltd,ed->lte", grad_whole, w_out, preferred_element_type=F32)
    grad_scan = grad_gated * jax.nn.silu(gate_in)
    end_state, pulled, span, dt, source, slope_dt, projected = scan_ends(
        low_rank, sent, got, w_dt, dt_bias[None], decay_log, mixed, grad_scan
    )
    span = span + span_more
    flat = (1, lane_count * state_count, inner_width)
    edge = jnp.where(to_later, end_state.reshape(flat), (pulled * carry_mask).reshape(flat))
    spans = jnp.broadcast_to(
        span.reshape(1, lane_count, inner_width), (seq_size, lane_count, inner_width)
    )
    message = jnp.concatenate([edge, spans], axis=1).astype(BF16)
    message = jnp.pad(message, ((0, 0), (0, -message.shape[1] % 8), (0, 0)))
    groups = lax.all_to_all(message, "seq", 0, 0, tiled=True)
    projected, normed_more, w_back, w_spread = lax.optimization_barrier(
        (projected, normed_more, w_back, w_spread)
    )
    y, grad_read, last, states_all = scan_forward(
        low_rank, place, projected, decay_log, dt, source, grad_scan, groups
    )
    scan_out = y + skip_gain * mixed
    gated = (scan_out * jax.nn.silu(gate_in)).astype(BF16)
    grad_gate = (grad_gated * scan_out * silu_slope(gate_in)).astype(BF16)
    half_width = model_width // 2
    first = [over.sent(normed, grad_gate)]
    first.append(over.sent(grad_whole, after(gated, first[0])))
    sum_first = Sum(over, first, (False, False), flags)
    sum_first.kept = [over.kept(after(normed, sum_first.message), grad_gate)]
    sum_first.kept.append(over.kept(grad_whole, after(gated, sum_first.kept[0])))
    turn, pull, part, grad_log = scan_backward(
        low_rank, projected, decay_log, dt, source, grad_scan, last, grad_read, states_all, *sum_first.kept
    )
    grad_slope = (turn + pull * mixed) * slope_dt
    grad_pre = grad_slope.astype(BF16)
    part = part + jnp.einsum("lte,re->ltr", grad_pre, w_dt, preferred_element_type=F32)
    sent = part.astype(BF16)
    for bit in mp_bits[:-1]:
        got = swap(sent, "mp", bit)
        if bit == 1:
            got = after(got, sum_first.next(sent))
        sent = (sent.astype(F32) + got.astype(F32)).astype(BF16)
    got = swap(sent, "mp", mp_bits[-1])
    grad_dt_w = jnp.einsum(
        "ltr,lte->re", projected.astype(BF16), after(grad_pre, sent), preferred_element_type=F32
    )
    grad_projected = after(sent, grad_dt_w).astype(F32) + got.astype(F32)
    grad_projected = grad_projected.astype(BF16)
    grad_mixed = pull * dt + grad_scan * skip_gain + jnp.einsum(
        "ltr,er->lte", grad_projected, w_x, preferred_element_type=F32
    )
    grad_conv = grad_mixed * silu_slope(conv_sum)
    grad_conv_b = jnp.sum(grad_conv, axis=(0, 1))
    grad_conv_w = jnp.stack(
        [
            jnp.sum(grad_conv * padded[:, tap : tap + length], axis=(0, 1))
            for tap in range(tap_count)
        ]
    )
    grad_padded = jnp.pad(conv_weight[0] * grad_conv, ((0, 0), (0, tap_count - 1), (0, 0)))
    for tap in range(1, tap_count):
        grad_padded = grad_padded + jnp.pad(
            conv_weight[tap] * grad_conv, ((0, 0), (tap, tap_count - 1 - tap), (0, 0))
        )
    rim_sent = grad_padded[:, : tap_count - 1] * carry_mask
    rim_fill = jnp.zeros((lane_count, rim_count - (tap_count - 1), inner_width), F32)
    rim_rows = jnp.concatenate([rim_fill, rim_sent], axis=1).astype(BF16)
    grad_main = grad_padded[:, tap_count - 1 :].astype(BF16)
    grad_more = jnp.concatenate(
        [grad_main.reshape(-1, inner_width), rim_rows.reshape(-1, inner_width)], axis=0
    )[None]
    grad_x_w = jnp.einsum("ltr,lte->re", grad_projected, after(mixed_low, rim_sent), preferred_element_type=F32)
    small = [
        (grad_conv_w, tap_count),
        (grad_conv_b[None], 1),
        (jnp.sum(grad_slope, axis=(0, 1))[None], 1),
        (jnp.sum(grad_scan * mixed, axis=(0, 1))[None], 1),
        (grad_log, state_count),
        (grad_dt_w, low_rank),
        (grad_x_w, low_rank + 2 * state_count),
    ]
    sizes = [size for _, size in small]
    small_half = -(-sum(sizes) // (8 * seq_size)) * 4 * seq_size
    inner_sent = over.sent(normed_more, after(grad_more, grad_x_w))
    inner_sent, small_kept = pack(flags[0], inner_sent, [part for part, _ in small], sizes, small_half)
    sum_inner = Sum(over, [inner_sent], (False, True), flags, [half_width, small_half])
    step = sum_first.next(sum_inner.message)
    sum_inner.kept = [over.kept(normed_more, after(grad_more, step)), small_kept]
    rim_back = from_behind(after(rim_sent, step), "seq", -1)
    out_sent = jnp.einsum(
        "lte,ed->ltd", after(gated, sum_inner.kept[0]), w_spread[:, half_width:], preferred_element_type=F32
    ).astype(BF16)
    out_kept = jnp.einsum(
        "lte,ed->ltd", after(gated, out_sent), w_spread[:, :half_width], preferred_element_type=F32
    )
    tail_zeros = jnp.zeros((lane_count, length - (tap_count - 1), inner_width), F32)
    grad_inner = grad_padded[:, tap_count - 1 :] + jnp.concatenate(
        [tail_zeros, after(rim_back, out_kept)], axis=1
    )
    grad_inner = grad_inner.astype(BF16)

    def back(part, cut):
        return jnp.einsum("lte,de->ltd", part[0], w_back[0, cut], preferred_element_type=F32) + jnp.einsum(
            "lte,de->ltd", part[1], w_back[1, cut], preferred_element_type=F32
        )

    back_sent = back((grad_inner, grad_gate), slice(half_width, None)).astype(BF16)
    back_kept = back((after(grad_inner, back_sent), grad_gate), slice(0, half_width))
    row_dot = jnp.sum(
        after(grad_inner, back_kept).astype(F32) * inner_act.astype(F32) + grad_gate.astype(F32) * gate_in,
        axis=2,
    )

    def as_rows(values, width):
        high = values.astype(BF16)
        low = (values - high.astype(F32)).astype(BF16)
        rows = jnp.concatenate([high, low], axis=1).reshape(lane_count, -1, width)
        return jnp.pad(rows, ((0, 0), (0, -rows.shape[1] % 16), (0, 0)))

    message = jnp.concatenate([out_sent, back_sent, as_rows(row_dot, half_width)], axis=1)
    step = sum_inner.next(message)
    step = sum_first.next(step)
    got = swap(after(message, step), "mp", 1)
    far = mp_bits[-1]
    for bit in mp_bits[:-1]:
        if bit == 1:
            step = sum_inner.next(message)
            step = sum_first.next(step)
        message, other, out_kept, back_kept, row_dot = hop(after(got, step), out_kept, back_kept, row_dot)
        if 2 * bit == far:
            got = swap(message, "mp", far)
            out_got = swap(after(other, message), "mp", far)
        else:
            message = jnp.concatenate([other, message], axis=1)
            got = swap(message, "mp", 2 * bit)
    got = after(got, message)
    rows = got[:, length:][:, : 2 * length // shard_width].reshape(lane_count, 2 * length).astype(F32)
    row_dot = row_dot + rows[:, :length] + rows[:, length:]
    grad_own = back_kept + got[:, :length].astype(F32)
    unit_own = inputs * inv_rms
    grad_gain = jnp.sum(grad_own * unit_own, axis=(0, 1))
    input_grad = output_grad + inv_rms * (
        grad_own * gain[:shard_width] - unit_own * (row_dot[:, :, None] / model_width)
    )
    grad_gain = jnp.pad(grad_gain, (0, -shard_width % inner_width)).reshape(-1, inner_width)
    sum_inner.rider = jnp.pad(grad_gain, ((0, -grad_gain.shape[0] % 16), (0, 0)))
    step = sum_inner.next(grad_gain)
    step = sum_first.next(step)
    input_grad = after(input_grad, step)
    step = sum_inner.next(step)
    output = inputs + (out_kept + after(out_got, step).astype(F32))
    step = sum_inner.next(output)
    sum_first.run_out()
    second = 2 + halves
    in_shape, out_shape = (2, model_width, inner_width), out_weight.shape
    half = model_width // 2
    layout = [(0, 1, 0, 0, halves, False, 0, half), (0, 1, 0, 1, halves, False, 0, half)]
    ends = (sum_first.message, after(sum_first.got, step))
    if model_width // seq_size % LANE == 0:
        layout += [(1, None, second, 0, halves, True, half, half), (1, None, second, 1, halves, True, half, half)]
        in_w, out_w = settle(orders, [*ends, *ends], layout, [in_shape, out_shape])
    else:
        (in_w,) = settle(orders, [*ends], layout, [in_shape])
        rows = [p[half:].reshape(halves, -1, inner_width)[orders[second + 2 :]].reshape(half, -1) for p in ends]
        up = over.own(0) == 1
        rows = [jnp.where(up, rows[1], rows[0]), jnp.where(up, rows[0], rows[1])]
        out_w = jnp.concatenate(rows, axis=0).astype(F32).T
    sum_inner.run_out()
    ends = (sum_inner.message, sum_inner.got)
    in_w = settle(orders, ends[:1], [(0, 0, 0, 0, halves, False, 0, half)], [in_shape], [in_w])
    count = small_half
    in_w, *parts, grad_gain = finish(
        orders, flat_order, *ends, [(0, 0, 0, 1, halves, False, 0, half)], half, count, sizes, in_w[0]
    )
    return (
        output,
        input_grad,
        grad_gain[0, :shard_width],
        in_w,
        parts[0],
        parts[1][0],
        parts[6].T,
        parts[5],
        parts[2][0],
        parts[4],
        parts[3][0],
        out_w,
    )


def solution(mesh):
    in_specs = (
        P(None, "seq", "mp"),
        P(None, "seq"),
        P(),
        P(None, None, "mp"),
        P(None, "mp"),
        P("mp"),
        P("mp", None),
        P(None, "mp"),
        P("mp"),
        P(None, "mp"),
        P("mp"),
        P("mp", None),
        P(None, "seq", "mp"),
    )
    out_specs = (
        P(None, "seq", "mp"),
        P(None, "seq", "mp"),
        P("mp"),
        P(None, None, "mp"),
        P(None, "mp"),
        P("mp"),
        P("mp", None),
        P(None, "mp"),
        P("mp"),
        P(None, "mp"),
        P("mp"),
        P("mp", None),
    )
    return jax.shard_map(
        per_device, mesh=mesh, in_specs=in_specs, out_specs=out_specs, check_vma=False
    )
```

```python
import functools

import jax
import jax.numpy as jnp
from jax import lax
from jax.experimental import pallas as pl
from jax.experimental.pallas import tpu as pltpu
from jax.sharding import PartitionSpec as P

F32 = jnp.float32
BF16 = jnp.bfloat16
LOG2E = 1.4426950408889634
CHUNK = 32
ROUND = 4
LANE = 128
FAR = 1.0e4
VMEM = pl.BlockSpec(memory_space=pltpu.VMEM)


def swap(block, axis, bit):
    devices = lax.axis_size(axis)
    return lax.ppermute(block, axis, [(i, i ^ bit) for i in range(devices)])


def from_behind(block, axis, distance):
    devices = range(lax.axis_size(axis))
    route = [(i - distance, i) for i in devices if i - distance in devices]
    return lax.ppermute(block, axis, route)


def bits_of(axis):
    count = lax.axis_size(axis)
    bits = []
    while (1 << len(bits)) < count:
        bits.append(1 << len(bits))
    return bits


def after(array, *others):
    return lax.optimization_barrier((array, *others))[0]


class Reduction:
    def __init__(self):
        self.bits = bits_of("seq")
        self.orders = [list(self.bits), list(self.bits)]
        if len(self.bits) > 1:
            self.orders[1][:2] = self.bits[1], self.bits[0]
        self.index = lax.axis_index("seq")
        self.odd = lax.axis_index("mp") % 2
        self.mp = lax.axis_size("mp")
        self.count = lax.axis_size("seq")

    def own(self, step):
        even = (self.index & self.orders[0][step]) != 0
        odd = (self.index & self.orders[1][step]) != 0
        return jnp.where(self.odd == 1, odd, even).astype(jnp.int32)

    def swap(self, block, step):
        route = []
        for s in range(self.count):
            for m in range(self.mp):
                route.append((s * self.mp + m, (s ^ self.orders[m % 2][step]) * self.mp + m))
        return lax.ppermute(block, ("seq", "mp"), route)

    def halves(self, block, step):
        half = block.shape[0] // 2
        up = self.own(step)
        kept = lax.dynamic_slice_in_dim(block, up * half, half, 0)
        sent = lax.dynamic_slice_in_dim(block, (1 - up) * half, half, 0)
        return kept, sent

    def part(self, left, right, up):
        half = left.shape[2] // 2
        cut = lax.dynamic_slice_in_dim(left, up * half, half, 2)
        return jnp.einsum("lta,ltb->ab", cut, right, preferred_element_type=F32)

    def sent(self, left, right):
        return self.part(left, right, 1 - self.own(0)).astype(BF16)

    def kept(self, left, right):
        return self.part(left, right, self.own(0))

    def place(self):
        place = jnp.int32(0)
        for step in range(1, len(self.bits)):
            place = place * 2 + self.own(step)
        return place

    def order(self, per, turn):
        blocks = self.count // 2
        pieces = blocks // per
        at = jnp.arange(blocks)
        low, high = turn % pieces, turn // pieces
        source = (((at // per) ^ low) * per + at % per) ^ self.place()
        up = self.own(0) ^ high
        return jnp.concatenate([jnp.stack([up * blocks, (1 - up) * blocks]), source]).astype(jnp.int32)

    def flat_order(self):
        blocks = self.count // 2
        place = jnp.int32(0)
        for step in range(len(self.bits) - 1):
            place = place * 2 + self.own(step)
        return (jnp.arange(blocks) ^ place).astype(jnp.int32)


def advance_kernel(plan, flag_ref, *refs):
    refs = list(refs)
    sent_ref, got_ref = refs.pop(0), refs.pop(0)
    inputs, outputs = refs[: plan["inputs"]], refs[plan["inputs"] :]
    message = outputs.pop(0)
    up = flag_ref[0]
    at = 0
    for mode, rows, first in plan["blocks"]:
        if mode == "half":
            kept, new = inputs.pop(0), outputs.pop(0)
            half = rows // 2
            own = pl.multiple_of(up * half, half)
            other = pl.multiple_of((1 - up) * half, half)
            new[...] = kept[pl.ds(own, half), :].astype(F32) + got_ref[pl.ds(first + own, half), :].astype(F32)
            send = kept[pl.ds(other, half), :].astype(F32) + got_ref[pl.ds(first + other, half), :].astype(F32)
            message[at : at + half, :] = send.astype(BF16)
            at += half
        elif mode in ("flat", "sum", "hold"):
            kept = inputs.pop(0)
            total = (kept[...].astype(F32) + got_ref[first : first + rows, :].astype(F32)).astype(BF16)
            if mode != "sum":
                outputs.pop(0)[...] = total
            if mode != "hold":
                message[at : at + rows, :] = total
                at += rows
        elif mode == "enter":
            message[at : at + rows, :] = inputs.pop(0)[...].astype(BF16)
            at += rows
        elif mode == "grow":
            message[at : at + rows, :] = sent_ref[first : first + rows, :]
            message[at + rows : at + 2 * rows, :] = got_ref[first : first + rows, :]
            at += 2 * rows
        else:
            total = sent_ref[first : first + rows, :].astype(F32) + got_ref[first : first + rows, :].astype(F32)
            message[at : at + rows, :] = total.astype(BF16)
            at += rows


def advance(flag, sent, got, blocks, inputs):
    width = sent.shape[1]
    grown = {"half": 0.5, "hold": 0, "grow": 2}
    total = int(sum(rows * grown.get(mode, 1) for mode, rows, _ in blocks))
    shapes = [jax.ShapeDtypeStruct((total, width), BF16)]
    for mode, rows, _ in blocks:
        if mode == "half":
            shapes.append(jax.ShapeDtypeStruct((rows // 2, width), F32))
        elif mode in ("flat", "hold"):
            shapes.append(jax.ShapeDtypeStruct((rows, width), BF16))
    return pl.pallas_call(
        functools.partial(advance_kernel, {"inputs": len(inputs), "blocks": blocks}),
        in_specs=[pl.BlockSpec(memory_space=pltpu.SMEM)] + [VMEM] * (2 + len(inputs)),
        out_specs=[VMEM] * len(shapes),
        out_shape=shapes,
        compiler_params=pltpu.CompilerParams(vmem_limit_bytes=12 << 20),
        name="advance",
    )(flag, sent, got, *inputs)


class Sum:
    def __init__(self, over, sent, flat, flags, rows=None):
        self.over, self.flat, self.flags = over, flat, flags
        self.kept, self.rider, self.count = None, None, 0
        self.rows = rows or [block.shape[0] for block in sent]
        self.message = sent[0] if rows else jnp.concatenate([block.astype(BF16) for block in sent], axis=0)
        self.got = over.swap(self.message, 0)

    def next(self, *earlier):
        steps = len(self.over.bits)
        k = self.count
        got = after(self.got, *earlier) if earlier else self.got
        blocks, inputs, rows, kept, first = [], [], [], [], 0
        for m, size in enumerate(self.rows):
            mode = "half" if k < steps - 1 else "sum" if k == steps - 1 else "grow"
            if self.flat[m]:
                mode = {steps - 2: "flat", steps - 1: "hold", steps: "enter"}.get(k, mode)
            if mode == "enter":
                size = self.kept[m].shape[0]
            blocks.append((mode, size, first))
            if mode != "grow":
                inputs.append(self.kept[m])
            first += 0 if mode == "enter" else size
            rows.append({"half": size // 2, "hold": 0, "grow": 2 * size}.get(mode, size))
        if self.rider is not None and k == steps - 1:
            blocks.append(("enter", self.rider.shape[0], 0))
            inputs.append(self.rider)
        elif self.rider is not None and k >= steps:
            blocks.append(("ride", self.rider.shape[0], first))
        flag = self.flags[min(k + 1, steps - 1)]
        self.message, *kept = advance(flag, self.message, got, blocks, inputs)
        for m, (mode, _, _) in enumerate(blocks[: len(rows)]):
            if mode in ("half", "flat", "hold"):
                self.kept[m] = kept.pop(0)
        self.rows = rows
        self.count = k + 1
        step = self.count if self.count < steps else 2 * steps - 1 - self.count
        self.got = self.over.swap(self.message, step)
        return self.message

    def run_out(self):
        while self.count < 2 * len(self.over.bits) - 1:
            self.next()


def silu_slope(values):
    logistic = jax.nn.sigmoid(values)
    return logistic * (1.0 + values * (1.0 - logistic))


def cost(ops, lanes, length, width, states):
    work = lanes * length * width * states
    return pl.CostEstimate(flops=ops * work * 16, bytes_accessed=work * 2, transcendentals=work)


def settle_kernel(names, layout, order_ref, *refs, starts=True, waits=True):
    parts, outs = refs[: len(layout)], refs[-2 - names : -2]
    wide, sems = refs[-2:]
    copies, at = [], 0
    for part, (out, lead, which, first, blocks, turned, offset, count) in zip(parts, layout, strict=True):
        size = count // blocks
        for b in range(blocks):
            source = order_ref[which + 2 + b]
            goal = pl.multiple_of((order_ref[which + first] + b) * size, size)
            ref = outs[out] if lead is None else outs[out].at[lead]
            if turned:
                spot = wide.at[at : at + part.shape[1], 0:size]
                target = ref.at[:, pl.ds(goal, size)]
            else:
                spot = wide.at[at : at + size, 0 : part.shape[1]]
                target = ref.at[pl.ds(goal, size), :]
            at += part.shape[1] if turned else size
            copies.append(pltpu.make_async_copy(spot, target, sems.at[len(copies)]))
            if starts:
                rows = part[pl.ds(pl.multiple_of(offset + source * size, size), size), :].astype(F32)
                spot[...] = jnp.transpose(rows) if turned else rows
                copies[-1].start()
    for copy in copies:
        if waits:
            copy.wait()


def settle(orders, parts, layout, shapes, into=()):
    any_space = pl.BlockSpec(memory_space=pl.ANY)
    rows = sum(p.shape[1] * l[4] if l[5] else l[7] for p, l in zip(parts, layout, strict=True))
    width = max(l[7] // l[4] if l[5] else p.shape[1] for p, l in zip(parts, layout, strict=True))
    count = sum(l[4] for l in layout)
    return pl.pallas_call(
        functools.partial(settle_kernel, len(shapes), layout),
        in_specs=[pl.BlockSpec(memory_space=pltpu.SMEM)] + [VMEM] * len(parts) + [any_space] * len(into),
        out_specs=[any_space] * len(shapes),
        out_shape=[jax.ShapeDtypeStruct(s, F32) for s in shapes],
        input_output_aliases={1 + len(parts) + k: k for k in range(len(into))},
        scratch_shapes=[pltpu.VMEM((rows, width), F32), pltpu.SemaphoreType.DMA((count,))],
        compiler_params=pltpu.CompilerParams(vmem_limit_bytes=16 << 20),
        name="settle",
    )(orders, *parts, *into)


def deal_rows(sizes, offset, order_ref, own_ref, late_ref, outs, rows):
    blocks = order_ref.shape[0]
    size = rows.shape[0] // blocks
    for b in range(blocks):
        source = order_ref[b]
        for part, first in ((own_ref, 0), (late_ref, blocks // 2)):

            @pl.when(jnp.logical_and(source >= first, source < first + blocks // 2))
            def _():
                at = pl.ds(pl.multiple_of(offset + (source - first) * size, size), size)
                rows[b * size : (b + 1) * size, :] = part[at, :].astype(F32)

    at = 0
    for out, count in zip(outs, sizes, strict=True):
        out[...] = rows[at : at + count, :]
        at += count


def finish_kernel(sizes, layout, offset, last, order_ref, flat_ref, own_ref, late_ref, into_ref, *refs):
    out, small, (total, rows, wide, sems) = refs[0], refs[1:-4], refs[-4:]
    settle_kernel(1, layout, order_ref, late_ref, out, wide, sems, waits=False)
    deal_rows(sizes, offset, flat_ref, own_ref, late_ref, small, rows)
    total[...] = own_ref[last : last + 16, :].astype(F32) + late_ref[last : last + 16, :].astype(F32)
    settle_kernel(1, layout, order_ref, late_ref, out, wide, sems, starts=False)


def finish(orders, flat_order, own, late, layout, offset, count, sizes, into):
    width = own.shape[1]
    any_space, smem = pl.BlockSpec(memory_space=pl.ANY), pl.BlockSpec(memory_space=pltpu.SMEM)
    shape = jax.ShapeDtypeStruct
    return pl.pallas_call(
        functools.partial(finish_kernel, sizes, layout, offset, offset + count),
        in_specs=[smem, smem, VMEM, VMEM, any_space],
        out_specs=[any_space] + [VMEM] * (len(sizes) + 1),
        out_shape=[shape(into.shape, F32)] + [shape((n, width), F32) for n in sizes] + [shape((16, width), F32)],
        input_output_aliases={4: 0},
        scratch_shapes=[
            pltpu.VMEM((2 * count, width), F32),
            pltpu.VMEM((layout[0][7], width), F32),
            pltpu.SemaphoreType.DMA((layout[0][4],)),
        ],
        compiler_params=pltpu.CompilerParams(vmem_limit_bytes=16 << 20),
        name="finish",
    )(orders, flat_order, own, late, into)


def hop_kernel(got_ref, out_ref, back_ref, row_ref, message, other, out_new, back_new, row_new):
    lanes, length, width = out_ref.shape
    half = width // 2
    for l in range(lanes):
        for m, (kept, new, sent) in enumerate(((out_ref, out_new, other), (back_ref, back_new, message))):
            o = slice(m * length, (m + 1) * length)
            new[l] = kept[l, :, :half] + got_ref[l, o, :half].astype(F32)
            send = kept[l, :, half:] + got_ref[l, o, half:].astype(F32)
            sent[l, :length, :] = send.astype(BF16)
        rows = got_ref[l, 2 * length :, :].astype(F32)
        came = jnp.concatenate([rows[r : r + 1] for r in range(2 * length // width)], axis=1)
        total = row_ref[l : l + 1, :] + came[:, :length] + came[:, length:]
        row_new[l : l + 1, :] = total
        high = total.astype(BF16).astype(F32)
        both = jnp.concatenate([high, total - high], axis=1)
        pieces = [both[:, at : at + half] for at in range(0, 2 * length, half)]
        pieces.append(jnp.zeros((message.shape[1] - length - len(pieces), half), F32))
        message[l, length:, :] = jnp.concatenate(pieces, axis=0).astype(BF16)


def hop(got, out_kept, back_kept, row_dot):
    lanes, length, width = out_kept.shape
    shape = jax.ShapeDtypeStruct
    half = shape((lanes, length, width // 2), F32)
    rows = length - (-(4 * length // width) // 16) * 16
    return pl.pallas_call(
        hop_kernel,
        in_specs=[VMEM] * 4,
        out_specs=[VMEM] * 5,
        out_shape=[
            shape((lanes, rows, width // 2), BF16),
            shape((lanes, length, width // 2), BF16),
            half,
            half,
            shape(row_dot.shape, F32),
        ],
        compiler_params=pltpu.CompilerParams(vmem_limit_bytes=12 << 20),
        name="hop",
    )(got, out_kept, back_kept, row_dot)


def product_kernel(flag_ref, left_ref, right_ref, more_ref, message):
    half = message.shape[0] - more_ref.shape[0]
    at = pl.multiple_of((1 - flag_ref[0]) * half, half)
    for block in range(0, half, min(half, 256)):
        size = min(half, 256)
        cut = left_ref[:, pl.ds(pl.multiple_of(at + block, size), size)]
        total = lax.dot_general(cut, right_ref[...], (((0,), (0,)), ((), ())), preferred_element_type=F32)
        message[block : block + size, :] = total.astype(BF16)
    message[half:, :] = more_ref[...].astype(BF16)


def sent_product(flag, left, right, more):
    half, width = left.shape[1] // 2, right.shape[1]
    return pl.pallas_call(
        product_kernel,
        in_specs=[pl.BlockSpec(memory_space=pltpu.SMEM)] + [VMEM] * 3,
        out_specs=VMEM,
        out_shape=jax.ShapeDtypeStruct((half + more.shape[0], width), BF16),
        compiler_params=pltpu.CompilerParams(vmem_limit_bytes=16 << 20),
        name="sent_product",
    )(flag, left, right, more)


def pack_kernel(sizes, flag_ref, sent_ref, *refs):
    parts, (message, kept, rows) = refs[:-3], refs[-3:]
    at = 0
    for part, size in zip(parts, sizes, strict=True):
        if part.ndim == 3:
            total = part[0]
            for l in range(1, part.shape[0]):
                total = total + part[l]
            rows[at : at + size, :] = total
        else:
            rows[at : at + size, :] = part[0:size, :]
        at += size
    rows[at:, :] = jnp.zeros((rows.shape[0] - at, rows.shape[1]), F32)
    half, first = kept.shape[0], sent_ref.shape[0]
    up = flag_ref[0]
    kept[...] = rows[pl.ds(pl.multiple_of(up * half, half), half), :]
    message[0:first, :] = sent_ref[...]
    message[first:, :] = rows[pl.ds(pl.multiple_of((1 - up) * half, half), half), :].astype(BF16)


def pack(flag, sent, parts, sizes, half):
    width = sent.shape[1]
    shape = jax.ShapeDtypeStruct
    return pl.pallas_call(
        functools.partial(pack_kernel, sizes),
        in_specs=[pl.BlockSpec(memory_space=pltpu.SMEM)] + [VMEM] * (1 + len(parts)),
        out_specs=[VMEM] * 2,
        out_shape=[shape((sent.shape[0] + half, width), BF16), shape((half, width), F32)],
        scratch_shapes=[pltpu.VMEM((2 * half, width), F32)],
        compiler_params=pltpu.CompilerParams(vmem_limit_bytes=8 << 20),
        name="pack",
    )(flag, sent, *parts)


def join_kernel(lanes, short, up_ref, got_ref, log_ref, total_ref, window_ref, message, total, window):
    states, width = log_ref.shape
    rate = -jnp.exp(log_ref[...]) * LOG2E
    upper = up_ref[0] != 0
    count = lanes * states
    spans = got_ref[got_ref.shape[0] - 16 :, :].astype(F32)
    upper_next = up_ref[1] != 0
    sums, befores, behinds = [], [], []
    for l in range(lanes):
        s = slice(l * states, (l + 1) * states)
        g = slice(count + l * states, count + (l + 1) * states)
        span, came = total_ref[2 * count + l : 2 * count + l + 1, :], spans[l : l + 1]
        before = window_ref[2 * count + l : 2 * count + l + 1, :]
        behind = window_ref[2 * count + lanes + l : 2 * count + lanes + l + 1, :]
        through, through_came = jnp.exp2(span * rate), jnp.exp2(came * rate)
        end, pull = total_ref[s, :], total_ref[g, :]
        end_came = got_ref[s, :].astype(F32)
        pull_came = end_came if short[0] else got_ref[g, :].astype(F32)
        end_new = jnp.where(upper, end + through * end_came, end_came + through_came * end)
        pull_new = jnp.where(upper, pull_came + through_came * pull, pull + through * pull_came)
        total[s, :], total[g, :] = end_new, pull_new
        if short[1]:
            message[s, :] = jnp.where(upper_next, pull_new, end_new).astype(BF16)
        else:
            message[s, :], message[g, :] = end_new.astype(BF16), pull_new.astype(BF16)
        enter = window_ref[s, :] + jnp.exp2(before * rate) * end_came
        leave = window_ref[g, :] + jnp.exp2(behind * rate) * pull_came
        window[s, :] = jnp.where(upper, enter, window_ref[s, :])
        window[g, :] = jnp.where(upper, window_ref[g, :], leave)
        sums.append(span + came)
        befores.append(jnp.where(upper, before + came, before))
        behinds.append(jnp.where(upper, behind, behind + came))
    fill = jnp.zeros((8 - lanes, width), F32)
    rows = jnp.concatenate([*sums, fill], axis=0)
    total[2 * count :, :] = rows
    message[message.shape[0] - 16 :, :] = jnp.concatenate([rows, jnp.zeros((8, width), F32)], axis=0).astype(BF16)
    fill = jnp.zeros((8 - 2 * lanes, width), F32)
    window[2 * count :, :] = jnp.concatenate([*befores, *behinds, fill], axis=0)


def join(lanes, short, up, got, log, total, window):
    shape = jax.ShapeDtypeStruct
    rows = 16 + lanes * log.shape[0] * (1 if short[1] else 2)
    return pl.pallas_call(
        functools.partial(join_kernel, lanes, short),
        in_specs=[pl.BlockSpec(memory_space=pltpu.SMEM)] + [VMEM] * 4,
        out_specs=[VMEM] * 3,
        out_shape=[shape((rows, got.shape[1]), BF16), shape(total.shape, F32), shape(window.shape, F32)],
        compiler_params=pltpu.CompilerParams(vmem_limit_bytes=8 << 20),
        name="join",
    )(up, got, log, total, window)


def iota(shape, dim):
    return lax.broadcasted_iota(jnp.int32, shape, dim)


def widen(part, width):
    return jnp.concatenate([part] * (width // part.shape[1]), axis=1)


def dot(a, b):
    return jnp.dot(a, b, preferred_element_type=F32)


def dot_t(a, b):
    return lax.dot_general(a, b, (((1,), (1,)), ((), ())), preferred_element_type=F32)


def row_of(ref, t, count):
    return jnp.broadcast_to(ref[pl.ds(t, 1), :], (count, ref.shape[1]))


def rows_of(i, count):
    return pl.ds(pl.multiple_of(i * count, count), count)


def chunk_columns(ref, i):
    per = LANE // CHUNK
    tile = ref[:, rows_of(i // per, LANE)]
    return pltpu.roll(tile, LANE - (i % per) * CHUNK, 1)


def spread_column(tile, j, width):
    part = jnp.broadcast_to(tile[:, j : j + 1], (tile.shape[0], LANE))
    return widen(part, width)


def selectors(states):
    wide = CHUNK * states
    per_state = iota((states, wide), 1) % states == iota((states, wide), 0)
    per_step = iota((CHUNK, wide), 1) // states == iota((CHUNK, wide), 0)
    return per_state.astype(F32), per_step.astype(F32)


def from_lanes(first, states):
    shape = (LANE, CHUNK * states)
    return (iota(shape, 0) == first + iota(shape, 1) % states).astype(BF16)


def to_lanes(first, states):
    shape = (CHUNK * states, LANE)
    return (iota(shape, 1) == first + iota(shape, 0) % states).astype(BF16)


def by_step(proj, lanes, per_step):
    spread = dot(proj, lanes)
    return spread * jnp.concatenate([per_step] * (spread.shape[0] // CHUNK), axis=0)


def ends_kernel(
    low_rank, sent_ref, got_ref, wdt_ref, bias_ref, log_ref, mixed_ref, gy_ref,
    end_ref, pull_ref, span_ref, dt_ref, u_ref, sig_ref, proj_ref,
    ahead, behind, left_b, left_c, xa, xb, ya, yb,
):
    length, width = dt_ref.shape
    states = log_ref.shape[0]
    rate = -jnp.exp(log_ref[...]) * LOG2E
    per_state, per_step = selectors(states)
    chunks = length // CHUNK
    upto = (iota((length, length), 1) <= iota((length, length), 0)).astype(BF16)
    after = (iota((length, length), 1) > iota((length, length), 0)).astype(BF16)
    proj = sent_ref[...].astype(F32) + got_ref[...].astype(F32)
    proj_ref[...] = proj
    proj = proj.astype(BF16)
    for first, left in ((low_rank, left_b), (low_rank + states, left_c)):
        spread = by_step(proj, from_lanes(first, states), per_step)
        for i in range(chunks):
            flat = jnp.sum(spread[i * CHUNK : (i + 1) * CHUNK], axis=0, keepdims=True)
            left[i * states : (i + 1) * states, :] = (flat * per_state).astype(BF16)
    block = min(128, length)
    for i in range(length // block):
        o = slice(i * block, (i + 1) * block)
        pre = dot(proj[o], wdt_ref[...]) + bias_ref[...]
        small = jnp.exp(-jnp.abs(pre))
        one = 1.0 + small
        series = small * (1.0 - small * (0.5 - small * (1.0 / 3.0)))
        dt = jnp.maximum(pre, 0.0) + jnp.where(small < 1e-3, series, jnp.log(one))
        dt_ref[o, :] = dt
        u_ref[o, :] = dt * mixed_ref[o, :]
        sig_ref[o, :] = jnp.where(pre >= 0.0, 1.0, small) / one
    dt = dt_ref[...]
    high = dt.astype(BF16)
    low = (dt - high.astype(F32)).astype(BF16)
    ahead[...] = dot(upto, high) + dot(upto, low)
    behind[...] = dot(after, high) + dot(after, low)
    span_ref[...] = ahead[length - 1 : length, :]
    xb[...] = jnp.zeros(xb.shape, BF16)
    yb[...] = jnp.zeros(yb.shape, BF16)

    def flush(i, x, y, sums):
        o = rows_of(jnp.maximum(i, 0), states)
        return sums[0] + dot(left_b[o, :], x[...]), sums[1] + dot(left_c[o, :], y[...])

    def fill(i, x, y):
        for j in range(CHUNK):
            t = i * CHUNK + j
            s = slice(j * states, (j + 1) * states)
            to_end = jnp.exp2(row_of(behind, t, states) * rate)
            x[s, :] = (to_end * row_of(u_ref, t, states)).astype(BF16)
            to_here = jnp.exp2(row_of(ahead, t, states) * rate)
            y[s, :] = (to_here * row_of(gy_ref, t, states)).astype(BF16)

    def body(k, sums):
        for i in range(0, ROUND, 2):
            at = ROUND * k + i
            sums = flush(at - 1, xb, yb, sums)
            fill(at, xa, ya)
            sums = flush(at, xa, ya, sums)
            fill(at + 1, xb, yb)
        return sums

    zero = jnp.zeros((states, width), F32)
    sums = lax.fori_loop(0, chunks // ROUND, body, (zero, zero))
    sums = flush(chunks - 1, xb, yb, sums)
    end_ref[...] = sums[0]
    pull_ref[...] = sums[1]


def lane_spec(*shape):
    return pl.BlockSpec((None, *shape), lambda l: (l,) + (0,) * len(shape))


def whole_spec(*shape):
    return pl.BlockSpec(shape, lambda l: (0,) * len(shape))


def scan_ends(low_rank, sent, got, w_dt, bias, log, mixed, gy):
    lanes, length, width = mixed.shape
    states = log.shape[0]
    shape = jax.ShapeDtypeStruct
    token = shape((lanes, length, width), F32)
    state = shape((lanes, states, width), F32)
    tokens, state_spec, narrow = lane_spec(length, width), lane_spec(states, width), lane_spec(length, LANE)
    return pl.pallas_call(
        functools.partial(ends_kernel, low_rank),
        grid=(lanes,),
        in_specs=[
            narrow,
            narrow,
            whole_spec(*w_dt.shape),
            whole_spec(1, width),
            whole_spec(states, width),
            tokens,
            tokens,
        ],
        out_specs=[state_spec, state_spec, lane_spec(1, width), tokens, tokens, tokens, narrow],
        out_shape=[state, state, shape((lanes, 1, width), F32)]
        + [pltpu.HBM((lanes, length, width), F32)] * 3
        + [shape(sent.shape, F32)],
        scratch_shapes=[pltpu.VMEM((length, width), F32)] * 2
        + [pltpu.VMEM((length // CHUNK * states, CHUNK * states), BF16)] * 2
        + [pltpu.VMEM((CHUNK * states, width), BF16)] * 4,
        compiler_params=pltpu.CompilerParams(vmem_limit_bytes=14 << 20),
        cost_estimate=cost(8, lanes, length, width, states),
        name="scan_ends",
    )(sent, got, w_dt, bias, log, mixed, gy)


def forward_kernel(
    low_rank, lanes, starts_ref, proj_ref, log_ref, dt_ref, u_ref, gy_ref, begin_ref,
    y_ref, gc_ref, hs_ref,
    kept, pa, pb, cols, left_c, masked, sems,
):
    length, width = dt_ref.shape
    states = log_ref.shape[0]
    l = pl.program_id(0)
    rate = -jnp.exp(log_ref[...]) * LOG2E
    _, per_step = selectors(states)
    wide = CHUNK * states
    chunks = length // CHUNK

    half = chunks // 2 * wide

    def leave(slot, part):
        rows = pl.ds(part * half, half)
        return pltpu.make_async_copy(kept.at[slot, rows, :], hs_ref.at[slot, rows, :], sems.at[slot, part])

    begin = jnp.where(starts_ref[l] != 0, 0.0, begin_ref[...])
    proj = proj_ref[...]
    cols[...] = jnp.transpose(proj)[low_rank : low_rank + states]
    spread = by_step(proj.astype(BF16), from_lanes(low_rank + states, states), per_step)
    left_c[...] = spread.astype(BF16)

    def flush(i, p):
        o = rows_of(jnp.maximum(i, 0), CHUNK)
        h = p[...]
        y_ref[o, :] = dot(left_c[o, :], h)
        masked[o, :] = (dot_t(gy_ref[o, :].astype(BF16), h) * per_step).astype(BF16)

    def fill(i, state, p):
        b_tile = chunk_columns(cols, i)
        low = state.astype(BF16)
        for j in range(CHUNK):
            t = i * CHUNK + j
            b = spread_column(b_tile, j, width)
            decay = jnp.exp2(row_of(dt_ref, t, states) * rate)
            state = decay * state + row_of(u_ref, t, states) * b
            kept[l, rows_of(t, states), :] = low
            low = state.astype(BF16)
            p[j * states : (j + 1) * states, :] = low
        return state

    def body(k, state):
        for i in range(0, ROUND, 2):
            at = ROUND * k + i
            flush(at - 1, pb)
            state = fill(at, state, pa)
            flush(at, pa)
            state = fill(at + 1, state, pb)
        return state

    rounds = chunks // ROUND
    state = lax.fori_loop(0, rounds // 2, body, begin)
    leave(l, 0).start()
    lax.fori_loop(rounds // 2, rounds, body, state)
    leave(l, 1).start()
    flush(chunks - 1, pb)
    gc_ref[...] = dot(masked[...], to_lanes(low_rank + states, states))

    @pl.when(l == lanes - 1)
    def _():
        for slot in range(lanes):
            for part in range(2):
                leave(slot, part).wait()


def scan_forward(low_rank, starts, proj, log, dt, u, gy, begin):
    lanes, length, width = dt.shape
    states = log.shape[0]
    shape = jax.ShapeDtypeStruct
    tokens, state_spec, narrow = lane_spec(length, width), lane_spec(states, width), lane_spec(length, LANE)
    return pl.pallas_call(
        functools.partial(forward_kernel, low_rank, lanes),
        grid=(lanes,),
        in_specs=[
            pl.BlockSpec(memory_space=pltpu.SMEM),
            narrow,
            whole_spec(states, width),
            tokens,
            tokens,
            tokens,
            state_spec,
        ],
        out_specs=[tokens, narrow, pl.BlockSpec(memory_space=pltpu.HBM)],
        out_shape=[
            shape((lanes, length, width), F32),
            shape(proj.shape, F32),
            shape((lanes, length * states, width), BF16),
        ],
        scratch_shapes=[pltpu.VMEM((lanes, length * states, width), BF16)]
        + [pltpu.VMEM((CHUNK * states, width), BF16)] * 2
        + [
            pltpu.VMEM((states, length), F32),
            pltpu.VMEM((length, CHUNK * states), BF16),
            pltpu.VMEM((length, CHUNK * states), BF16),
            pltpu.SemaphoreType.DMA((lanes, 2)),
        ],
        compiler_params=pltpu.CompilerParams(vmem_limit_bytes=20 << 20),
        cost_estimate=cost(8, lanes, length, width, states),
        name="scan_forward",
    )(starts, proj, log, dt, u, gy, begin)


def backward_kernel(
    low_rank, lanes, proj_ref, log_ref, dt_ref, u_ref, gy_ref, last_ref, gc_ref, hs_ref, *refs
):
    (turn_ref, pull_ref, gbc_ref, ga_ref,
     kept, pa, pb, qa, qb, ra, rb, cols, left_b, masked, sems) = refs[-15:]
    length, width = dt_ref.shape
    states = log_ref.shape[0]
    l = pl.program_id(0)
    plain = -jnp.exp(log_ref[...])
    rate = plain * LOG2E
    rate_low = plain.astype(BF16)
    per_state, per_step = selectors(states)
    per_state_low, per_step_low = per_state.astype(BF16), per_step.astype(BF16)
    chunks = length // CHUNK

    half = length // 2 * states

    def enter(slot, part):
        rows = pl.ds(part * half, half)
        return pltpu.make_async_copy(hs_ref.at[slot, rows, :], kept.at[slot, rows, :], sems.at[slot, part])

    @pl.when(l == 0)
    def _():
        for slot in range(lanes):
            for part in (1, 0):
                enter(slot, part).start()

    for ref in (pb, qb, rb):
        ref[...] = jnp.zeros(ref.shape, BF16)
    proj = proj_ref[...]
    cols[...] = jnp.transpose(proj)[low_rank + states : low_rank + 2 * states]
    left_b[...] = by_step(proj.astype(BF16), from_lanes(low_rank, states), per_step).astype(BF16)

    def flush(i, p, q, r, ga):
        o = rows_of(jnp.minimum(i, chunks - 1), CHUNK)
        grad = p[...]
        pull_ref[o, :] = dot(left_b[o, :], grad)
        masked[o, :] = (dot_t(u_ref[o, :].astype(BF16), grad) * per_step).astype(BF16)
        turn_ref[o, :] = dot(per_step_low, q[...])
        return ga + dot(per_state_low, r[...])

    def fill(i, carry, p, q, r):
        c_tile = chunk_columns(cols, i)
        for j in reversed(range(CHUNK)):
            t = i * CHUNK + j
            s = slice(j * states, (j + 1) * states)
            c = spread_column(c_tile, j, width)
            dt = row_of(dt_ref, t, states)
            grad = carry + row_of(gy_ref, t, states) * c
            carry = jnp.exp2(dt * rate) * grad
            p[s, :] = grad.astype(BF16)
            turn = carry.astype(BF16) * kept[l, rows_of(t, states), :] * rate_low
            q[s, :] = turn
            r[s, :] = turn * dt.astype(BF16)
        return carry

    def body(k, carried):
        carry, ga = carried
        for i in range(0, ROUND, 2):
            at = chunks - 1 - ROUND * k - i
            ga = flush(at + 1, pb, qb, rb, ga)
            carry = fill(at, carry, pa, qa, ra)
            ga = flush(at, pa, qa, ra, ga)
            carry = fill(at - 1, carry, pb, qb, rb)
        return carry, ga

    rounds = chunks // ROUND
    carried = (last_ref[...], jnp.zeros((states, width), F32))
    enter(l, 1).wait()
    carried = lax.fori_loop(0, rounds // 2, body, carried)
    enter(l, 0).wait()
    _, ga = lax.fori_loop(rounds // 2, rounds, body, carried)
    ga_ref[...] = flush(0, pb, qb, rb, ga)
    gbc_ref[...] = gc_ref[...] + dot(masked[...], to_lanes(low_rank, states))


def scan_backward(low_rank, proj, log, dt, u, gy, last, gc, hs, *earlier):
    lanes, length, width = dt.shape
    states = log.shape[0]
    shape = jax.ShapeDtypeStruct
    tokens, state_spec, narrow = lane_spec(length, width), lane_spec(states, width), lane_spec(length, LANE)
    token = shape((lanes, length, width), F32)
    return pl.pallas_call(
        functools.partial(backward_kernel, low_rank, lanes),
        grid=(lanes,),
        in_specs=[narrow, whole_spec(states, width), tokens, tokens, tokens, state_spec, narrow]
        + [pl.BlockSpec(memory_space=pltpu.HBM)]
        + [pl.BlockSpec(memory_space=pl.ANY)] * len(earlier),
        out_specs=[tokens, tokens, narrow, state_spec],
        out_shape=[token, token, shape(proj.shape, F32), shape((lanes, states, width), F32)],
        scratch_shapes=[pltpu.VMEM((lanes, length * states, width), BF16)]
        + [pltpu.VMEM((CHUNK * states, width), BF16)] * 6
        + [
            pltpu.VMEM((states, length), F32),
            pltpu.VMEM((length, CHUNK * states), BF16),
            pltpu.VMEM((length, CHUNK * states), BF16),
            pltpu.SemaphoreType.DMA((lanes, 2)),
        ],
        compiler_params=pltpu.CompilerParams(vmem_limit_bytes=22 << 20),
        cost_estimate=cost(12, lanes, length, width, states),
        name="scan_backward",
    )(proj, log, dt, u, gy, last, gc, hs, *earlier)


def per_device(
    inputs,
    row_starts,
    norm_gain,
    in_weight,
    conv_weight,
    conv_bias,
    xproj_weight,
    dtproj_weight,
    dt_bias,
    decay_log,
    skip_gain,
    out_weight,
    output_grad,
):
    lane_count, length, shard_width = inputs.shape
    low_rank = dtproj_weight.shape[0]
    state_count = decay_log.shape[0]
    tap_count = conv_weight.shape[0]
    inner_width = conv_bias.shape[0]
    model_width = norm_gain.shape[0]
    starts = row_starts.astype(F32)
    carry_mask = (1.0 - starts)[:, :, None]
    mp_index, mp_size = lax.axis_index("mp"), lax.axis_size("mp")
    seq_index, seq_size = lax.axis_index("seq"), lax.axis_size("seq")
    mp_bits, seq_bits = bits_of("mp"), bits_of("seq")
    near_first = [int(format(k, "0%db" % len(mp_bits))[::-1], 2) for k in range(mp_size)]

    def blocks(array, axis, order):
        parts = [
            lax.dynamic_slice_in_dim(array, (mp_index ^ k) * shard_width, shard_width, axis) for k in order
        ]
        return jnp.concatenate(parts, axis=axis)

    x_parts, grad_parts = {0: inputs.astype(BF16)}, {}
    square = jnp.sum(jnp.square(inputs), axis=2)
    for bit in reversed(mp_bits):
        for k in list(x_parts):
            x_parts[k | bit] = swap(x_parts[k], "mp", bit)
        square = square + swap(square, "mp", bit)
    grad_parts[0] = after(output_grad.astype(BF16), x_parts[mp_bits[-1]])
    for bit in reversed(mp_bits[1:]):
        for k in list(grad_parts):
            grad_parts[k | bit] = swap(grad_parts[k], "mp", bit)
    near = list(range(mp_size))
    over = Reduction()
    per = shard_width * seq_size // model_width
    halves = seq_size // 2
    ups = ((seq_index & jnp.array([*seq_bits, 0])) != 0).astype(jnp.int32)
    ups = [ups[step : step + 2] for step in range(len(seq_bits))]
    orders = jnp.concatenate([over.order(per, mp_index), over.order(1, 0)])
    flat_order = over.flat_order()
    flags = [over.own(step)[None] for step in range(len(seq_bits))]
    span_more = FAR * starts[:, :, None]
    w_in = blocks(in_weight, 1, near).astype(BF16)
    w_out = lax.optimization_barrier(out_weight.astype(BF16))
    gain = blocks(norm_gain, 0, near)
    w_x = jnp.pad(xproj_weight.astype(BF16), ((0, 0), (0, -xproj_weight.shape[1] % LANE)))
    w_dt = jnp.pad(dtproj_weight.astype(BF16), ((0, -low_rank % LANE), (0, 0)))
    w_dt = lax.optimization_barrier(w_dt)
    inv_rms = lax.rsqrt(square[:, :, None] / model_width + 1e-05)
    x_parts[near[-1]] = after(x_parts[near[-1]], orders, flat_order, span_more, *flags, *ups, w_out, w_dt)
    x_whole = jnp.concatenate([x_parts[k] for k in near], axis=2)
    normed = (x_whole.astype(F32) * inv_rms * gain).astype(BF16)
    rim_count = 8
    rim_normed = from_behind(normed[:, length - rim_count :, :], "seq", 1)
    inner_act = jnp.einsum("ltd,de->lte", normed, w_in[0], preferred_element_type=F32).astype(BF16)
    rim_rows = jnp.einsum("ltd,de->lte", rim_normed, w_in[0], preferred_element_type=F32).astype(BF16)
    rim_rows = after(rim_rows, *grad_parts.values())
    rim_rows = (rim_rows.astype(F32) * carry_mask)[:, rim_count - (tap_count - 1) :]
    padded = jnp.concatenate([rim_rows, inner_act.astype(F32)], axis=1)
    conv_sum = conv_bias + conv_weight[0] * padded[:, 0:length]
    for tap in range(1, tap_count):
        conv_sum = conv_sum + conv_weight[tap] * padded[:, tap : tap + length]
    mixed = jax.nn.silu(conv_sum)
    mixed_low = mixed.astype(BF16)
    sent = jnp.einsum("lte,er->ltr", mixed_low, w_x, preferred_element_type=F32).astype(BF16)
    for bit in mp_bits[:-1]:
        sent = (sent.astype(F32) + swap(sent, "mp", bit).astype(F32)).astype(BF16)
    got = swap(sent, "mp", mp_bits[-1])
    gate_in = jnp.einsum("ltd,de->lte", after(normed, sent), w_in[1], preferred_element_type=F32)
    for k in list(grad_parts):
        grad_parts[k] = after(grad_parts[k], sent)
        grad_parts[k | 1] = swap(grad_parts[k], "mp", 1)
    normed_more = jnp.concatenate(
        [after(normed, sent).reshape(-1, model_width), rim_normed.reshape(-1, model_width)], axis=0
    )[None]
    grad_whole = jnp.concatenate(
        [
            sum(jnp.where(k == (mp_index ^ block), grad_parts[k], 0) for k in range(mp_size))
            for block in range(mp_size)
        ],
        axis=2,
    )
    grad_gated = jnp.einsum("ltd,ed->lte", grad_whole, w_out, preferred_element_type=F32)
    grad_scan = grad_gated * jax.nn.silu(gate_in)
    end_state, pulled, span, dt, source, slope_dt, projected = scan_ends(
        low_rank, sent, got, w_dt, dt_bias[None], decay_log, mixed, grad_scan
    )
    span = span + span_more
    count = lane_count * state_count
    flat = (count, inner_width)
    total = jnp.concatenate(
        [
            end_state.reshape(flat),
            (pulled * carry_mask).reshape(flat),
            span.reshape(lane_count, inner_width),
            jnp.zeros((8 - lane_count, inner_width), F32),
        ],
        axis=0,
    )
    message = jnp.pad(total.astype(BF16), ((0, 8), (0, 0)))
    window = jnp.zeros_like(total)
    for step, bit in enumerate(seq_bits):
        short = (step == len(seq_bits) - 1, step == len(seq_bits) - 2)
        if step == 0:
            w_late = after(w_out, message)
            w_spread = blocks(w_late, 1, near_first)
            w_late = after(w_in, message)
            w_back = jnp.concatenate(
                [w_late[:, k * shard_width : (k + 1) * shard_width] for k in near_first], axis=1
            )
        got = swap(message, "seq", bit)
        message, total, window = join(lane_count, short, ups[step], got, decay_log, total, window)
    window = window.reshape(-1, inner_width)
    begin = window[:count].reshape(end_state.shape)
    last = window[count : 2 * count].reshape(end_state.shape)
    projected, normed_more, w_back, w_spread = lax.optimization_barrier(
        (projected, normed_more, w_back, w_spread)
    )
    y, grad_read, states_all = scan_forward(
        low_rank, row_starts[:, 0], projected, decay_log, dt, source, grad_scan, begin
    )
    scan_out = y + skip_gain * mixed
    gated = (scan_out * jax.nn.silu(gate_in)).astype(BF16)
    grad_gate = (grad_gated * scan_out * silu_slope(gate_in)).astype(BF16)
    half_width = model_width // 2
    first = [over.sent(normed, grad_gate)]
    first.append(over.sent(grad_whole, after(gated, first[0])))
    sum_first = Sum(over, first, (False, False), flags)
    sum_first.kept = [over.kept(after(normed, sum_first.message), grad_gate)]
    sum_first.kept.append(over.kept(grad_whole, after(gated, sum_first.kept[0])))
    turn, pull, part, grad_log = scan_backward(
        low_rank, projected, decay_log, dt, source, grad_scan, last, grad_read, states_all, *sum_first.kept
    )
    grad_slope = (turn + pull * mixed) * slope_dt
    grad_pre = grad_slope.astype(BF16)
    part = part + jnp.einsum("lte,re->ltr", grad_pre, w_dt, preferred_element_type=F32)
    sent = part.astype(BF16)
    for bit in mp_bits[:-1]:
        got = swap(sent, "mp", bit)
        if bit == 1:
            got = after(got, sum_first.next(sent))
        sent = (sent.astype(F32) + got.astype(F32)).astype(BF16)
    got = swap(sent, "mp", mp_bits[-1])
    grad_dt_w = jnp.einsum(
        "ltr,lte->re", projected.astype(BF16), after(grad_pre, sent), preferred_element_type=F32
    )
    grad_projected = after(sent, grad_dt_w).astype(F32) + got.astype(F32)
    grad_projected = grad_projected.astype(BF16)
    grad_mixed = pull * dt + grad_scan * skip_gain + jnp.einsum(
        "ltr,er->lte", grad_projected, w_x, preferred_element_type=F32
    )
    grad_conv = grad_mixed * silu_slope(conv_sum)
    grad_conv_b = jnp.sum(grad_conv, axis=(0, 1))
    grad_conv_w = jnp.stack(
        [
            jnp.sum(grad_conv * padded[:, tap : tap + length], axis=(0, 1))
            for tap in range(tap_count)
        ]
    )
    grad_padded = jnp.pad(conv_weight[0] * grad_conv, ((0, 0), (0, tap_count - 1), (0, 0)))
    for tap in range(1, tap_count):
        grad_padded = grad_padded + jnp.pad(
            conv_weight[tap] * grad_conv, ((0, 0), (tap, tap_count - 1 - tap), (0, 0))
        )
    rim_sent = grad_padded[:, : tap_count - 1] * carry_mask
    rim_fill = jnp.zeros((lane_count, rim_count - (tap_count - 1), inner_width), F32)
    rim_rows = jnp.concatenate([rim_fill, rim_sent], axis=1).astype(BF16)
    grad_main = grad_padded[:, tap_count - 1 :].astype(BF16)
    grad_more = jnp.concatenate(
        [grad_main.reshape(-1, inner_width), rim_rows.reshape(-1, inner_width)], axis=0
    )[None]
    grad_x_w = jnp.einsum("ltr,lte->re", grad_projected, after(mixed_low, rim_sent), preferred_element_type=F32)
    small = [
        (grad_conv_w, tap_count),
        (grad_conv_b[None], 1),
        (jnp.sum(grad_slope, axis=(0, 1))[None], 1),
        (jnp.sum(grad_scan * mixed, axis=(0, 1))[None], 1),
        (grad_log, state_count),
        (grad_dt_w, low_rank),
        (grad_x_w, low_rank + 2 * state_count),
    ]
    sizes = [size for _, size in small]
    small_half = -(-sum(sizes) // (8 * seq_size)) * 4 * seq_size
    inner_sent = over.sent(normed_more, after(grad_more, grad_x_w))
    inner_sent, small_kept = pack(flags[0], inner_sent, [part for part, _ in small], sizes, small_half)
    sum_inner = Sum(over, [inner_sent], (False, True), flags, [half_width, small_half])
    step = sum_first.next(sum_inner.message)
    sum_inner.kept = [over.kept(normed_more, after(grad_more, step)), small_kept]
    rim_back = from_behind(after(rim_sent, step), "seq", -1)
    out_sent = jnp.einsum(
        "lte,ed->ltd", after(gated, sum_inner.kept[0]), w_spread[:, half_width:], preferred_element_type=F32
    ).astype(BF16)
    out_kept = jnp.einsum(
        "lte,ed->ltd", after(gated, out_sent), w_spread[:, :half_width], preferred_element_type=F32
    )
    tail_zeros = jnp.zeros((lane_count, length - (tap_count - 1), inner_width), F32)
    grad_inner = grad_padded[:, tap_count - 1 :] + jnp.concatenate(
        [tail_zeros, after(rim_back, out_kept)], axis=1
    )
    grad_inner = grad_inner.astype(BF16)

    def back(part, cut):
        return jnp.einsum("lte,de->ltd", part[0], w_back[0, cut], preferred_element_type=F32) + jnp.einsum(
            "lte,de->ltd", part[1], w_back[1, cut], preferred_element_type=F32
        )

    back_sent = back((grad_inner, grad_gate), slice(half_width, None)).astype(BF16)
    back_kept = back((after(grad_inner, back_sent), grad_gate), slice(0, half_width))
    row_dot = jnp.sum(
        after(grad_inner, back_kept).astype(F32) * inner_act.astype(F32) + grad_gate.astype(F32) * gate_in,
        axis=2,
    )

    def as_rows(values, width):
        high = values.astype(BF16)
        low = (values - high.astype(F32)).astype(BF16)
        rows = jnp.concatenate([high, low], axis=1).reshape(lane_count, -1, width)
        return jnp.pad(rows, ((0, 0), (0, -rows.shape[1] % 16), (0, 0)))

    message = jnp.concatenate([out_sent, back_sent, as_rows(row_dot, half_width)], axis=1)
    step = sum_inner.next(message)
    step = sum_first.next(step)
    got = swap(after(message, step), "mp", 1)
    far = mp_bits[-1]
    for bit in mp_bits[:-1]:
        if bit == 1:
            step = sum_inner.next(message)
            step = sum_first.next(step)
        message, other, out_kept, back_kept, row_dot = hop(after(got, step), out_kept, back_kept, row_dot)
        if 2 * bit == far:
            got = swap(message, "mp", far)
            out_got = swap(after(other, message), "mp", far)
        else:
            message = jnp.concatenate([other, message], axis=1)
            got = swap(message, "mp", 2 * bit)
    got = after(got, message)
    rows = got[:, length:][:, : 2 * length // shard_width].reshape(lane_count, 2 * length).astype(F32)
    row_dot = row_dot + rows[:, :length] + rows[:, length:]
    grad_own = back_kept + got[:, :length].astype(F32)
    unit_own = inputs * inv_rms
    grad_gain = jnp.sum(grad_own * unit_own, axis=(0, 1))
    input_grad = output_grad + inv_rms * (
        grad_own * gain[:shard_width] - unit_own * (row_dot[:, :, None] / model_width)
    )
    grad_gain = jnp.pad(grad_gain, (0, -shard_width % inner_width)).reshape(-1, inner_width)
    sum_inner.rider = jnp.pad(grad_gain, ((0, -grad_gain.shape[0] % 16), (0, 0)))
    step = sum_inner.next(grad_gain)
    step = sum_first.next(step)
    input_grad = after(input_grad, step)
    step = sum_inner.next(step)
    output = inputs + (out_kept + after(out_got, step).astype(F32))
    step = sum_inner.next(output)
    sum_first.run_out()
    second = 2 + halves
    in_shape, out_shape = (2, model_width, inner_width), out_weight.shape
    half = model_width // 2
    layout = [(0, 1, 0, 0, halves, False, 0, half), (0, 1, 0, 1, halves, False, 0, half)]
    ends = (sum_first.message, after(sum_first.got, step))
    if model_width // seq_size % LANE == 0:
        layout += [(1, None, second, 0, halves, True, half, half), (1, None, second, 1, halves, True, half, half)]
        in_w, out_w = settle(orders, [*ends, *ends], layout, [in_shape, out_shape])
    else:
        (in_w,) = settle(orders, [*ends], layout, [in_shape])
        rows = [p[half:].reshape(halves, -1, inner_width)[orders[second + 2 :]].reshape(half, -1) for p in ends]
        up = over.own(0) == 1
        rows = [jnp.where(up, rows[1], rows[0]), jnp.where(up, rows[0], rows[1])]
        out_w = jnp.concatenate(rows, axis=0).astype(F32).T
    sum_inner.run_out()
    ends = (sum_inner.message, sum_inner.got)
    in_w = settle(orders, ends[:1], [(0, 0, 0, 0, halves, False, 0, half)], [in_shape], [in_w])
    count = small_half
    in_w, *parts, grad_gain = finish(
        orders, flat_order, *ends, [(0, 0, 0, 1, halves, False, 0, half)], half, count, sizes, in_w[0]
    )
    return (
        output,
        input_grad,
        grad_gain[0, :shard_width],
        in_w,
        parts[0],
        parts[1][0],
        parts[6].T,
        parts[5],
        parts[2][0],
        parts[4],
        parts[3][0],
        out_w,
    )


def solution(mesh):
    in_specs = (
        P(None, "seq", "mp"),
        P(None, "seq"),
        P(),
        P(None, None, "mp"),
        P(None, "mp"),
        P("mp"),
        P("mp", None),
        P(None, "mp"),
        P("mp"),
        P(None, "mp"),
        P("mp"),
        P("mp", None),
        P(None, "seq", "mp"),
    )
    out_specs = (
        P(None, "seq", "mp"),
        P(None, "seq", "mp"),
        P("mp"),
        P(None, None, "mp"),
        P(None, "mp"),
        P("mp"),
        P("mp", None),
        P(None, "mp"),
        P("mp"),
        P(None, "mp"),
        P("mp"),
        P("mp", None),
    )
    return jax.shard_map(
        per_device, mesh=mesh, in_specs=in_specs, out_specs=out_specs, check_vma=False
    )
```

```python
import functools

import jax
import jax.numpy as jnp
from jax import lax
from jax.experimental import pallas as pl
from jax.experimental.pallas import tpu as pltpu
from jax.sharding import PartitionSpec as P

F32 = jnp.float32
BF16 = jnp.bfloat16
LOG2E = 1.4426950408889634
CHUNK = 32
ROUND = 4
LANE = 128
FAR = 1.0e4
VMEM = pl.BlockSpec(memory_space=pltpu.VMEM)


def swap(block, axis, bit):
    devices = lax.axis_size(axis)
    return lax.ppermute(block, axis, [(i, i ^ bit) for i in range(devices)])


def from_behind(block, axis, distance):
    devices = range(lax.axis_size(axis))
    route = [(i - distance, i) for i in devices if i - distance in devices]
    return lax.ppermute(block, axis, route)


def bits_of(axis):
    count = lax.axis_size(axis)
    bits = []
    while (1 << len(bits)) < count:
        bits.append(1 << len(bits))
    return bits


def after(array, *others):
    return lax.optimization_barrier((array, *others))[0]


class Reduction:
    def __init__(self):
        self.bits = bits_of("seq")
        self.orders = [list(self.bits), list(self.bits)]
        if len(self.bits) > 1:
            self.orders[1][:2] = self.bits[1], self.bits[0]
        self.index = lax.axis_index("seq")
        self.odd = lax.axis_index("mp") % 2
        self.mp = lax.axis_size("mp")
        self.count = lax.axis_size("seq")

    def own(self, step):
        even = (self.index & self.orders[0][step]) != 0
        odd = (self.index & self.orders[1][step]) != 0
        return jnp.where(self.odd == 1, odd, even).astype(jnp.int32)

    def swap(self, block, step):
        route = []
        for s in range(self.count):
            for m in range(self.mp):
                route.append((s * self.mp + m, (s ^ self.orders[m % 2][step]) * self.mp + m))
        return lax.ppermute(block, ("seq", "mp"), route)

    def halves(self, block, step):
        half = block.shape[0] // 2
        up = self.own(step)
        kept = lax.dynamic_slice_in_dim(block, up * half, half, 0)
        sent = lax.dynamic_slice_in_dim(block, (1 - up) * half, half, 0)
        return kept, sent

    def part(self, left, right, up):
        half = left.shape[2] // 2
        cut = lax.dynamic_slice_in_dim(left, up * half, half, 2)
        return jnp.einsum("lta,ltb->ab", cut, right, preferred_element_type=F32)

    def sent(self, left, right):
        return self.part(left, right, 1 - self.own(0)).astype(BF16)

    def kept(self, left, right):
        return self.part(left, right, self.own(0))

    def place(self):
        place = jnp.int32(0)
        for step in range(1, len(self.bits)):
            place = place * 2 + self.own(step)
        return place

    def order(self, per, turn):
        blocks = self.count // 2
        pieces = blocks // per
        at = jnp.arange(blocks)
        low, high = turn % pieces, turn // pieces
        source = (((at // per) ^ low) * per + at % per) ^ self.place()
        up = self.own(0) ^ high
        return jnp.concatenate([jnp.stack([up * blocks, (1 - up) * blocks]), source]).astype(jnp.int32)

    def flat_order(self):
        blocks = self.count // 2
        place = jnp.int32(0)
        for step in range(len(self.bits) - 1):
            place = place * 2 + self.own(step)
        return (jnp.arange(blocks) ^ place).astype(jnp.int32)


def advance_kernel(plan, flag_ref, *refs):
    refs = list(refs)
    sent_ref, got_ref = refs.pop(0), refs.pop(0)
    inputs, outputs = refs[: plan["inputs"]], refs[plan["inputs"] :]
    message = outputs.pop(0)
    up = flag_ref[0]
    at = 0
    for mode, rows, first in plan["blocks"]:
        if mode == "half":
            kept, new = inputs.pop(0), outputs.pop(0)
            half = rows // 2
            own = pl.multiple_of(up * half, half)
            other = pl.multiple_of((1 - up) * half, half)
            new[...] = kept[pl.ds(own, half), :].astype(F32) + got_ref[pl.ds(first + own, half), :].astype(F32)
            send = kept[pl.ds(other, half), :].astype(F32) + got_ref[pl.ds(first + other, half), :].astype(F32)
            message[at : at + half, :] = send.astype(BF16)
            at += half
        elif mode in ("flat", "sum", "hold"):
            kept = inputs.pop(0)
            total = (kept[...].astype(F32) + got_ref[first : first + rows, :].astype(F32)).astype(BF16)
            if mode != "sum":
                outputs.pop(0)[...] = total
            if mode != "hold":
                message[at : at + rows, :] = total
                at += rows
        elif mode == "enter":
            message[at : at + rows, :] = inputs.pop(0)[...].astype(BF16)
            at += rows
        elif mode == "grow":
            message[at : at + rows, :] = sent_ref[first : first + rows, :]
            message[at + rows : at + 2 * rows, :] = got_ref[first : first + rows, :]
            at += 2 * rows
        else:
            total = sent_ref[first : first + rows, :].astype(F32) + got_ref[first : first + rows, :].astype(F32)
            message[at : at + rows, :] = total.astype(BF16)
            at += rows


def advance(flag, sent, got, blocks, inputs):
    width = sent.shape[1]
    grown = {"half": 0.5, "hold": 0, "grow": 2}
    total = int(sum(rows * grown.get(mode, 1) for mode, rows, _ in blocks))
    shapes = [jax.ShapeDtypeStruct((total, width), BF16)]
    for mode, rows, _ in blocks:
        if mode == "half":
            shapes.append(jax.ShapeDtypeStruct((rows // 2, width), F32))
        elif mode in ("flat", "hold"):
            shapes.append(jax.ShapeDtypeStruct((rows, width), BF16))
    return pl.pallas_call(
        functools.partial(advance_kernel, {"inputs": len(inputs), "blocks": blocks}),
        in_specs=[pl.BlockSpec(memory_space=pltpu.SMEM)] + [VMEM] * (2 + len(inputs)),
        out_specs=[VMEM] * len(shapes),
        out_shape=shapes,
        compiler_params=pltpu.CompilerParams(vmem_limit_bytes=12 << 20),
        name="advance",
    )(flag, sent, got, *inputs)


class Sum:
    def __init__(self, over, sent, flat, flags, rows=None):
        self.over, self.flat, self.flags = over, flat, flags
        self.kept, self.rider, self.count = None, None, 0
        self.rows = rows or [block.shape[0] for block in sent]
        self.message = sent[0] if rows else jnp.concatenate([block.astype(BF16) for block in sent], axis=0)
        self.got = over.swap(self.message, 0)

    def next(self, *earlier):
        steps = len(self.over.bits)
        k = self.count
        got = after(self.got, *earlier) if earlier else self.got
        blocks, inputs, rows, kept, first = [], [], [], [], 0
        for m, size in enumerate(self.rows):
            mode = "half" if k < steps - 1 else "sum" if k == steps - 1 else "grow"
            if self.flat[m]:
                mode = {steps - 2: "flat", steps - 1: "hold", steps: "enter"}.get(k, mode)
            if mode == "enter":
                size = self.kept[m].shape[0]
            blocks.append((mode, size, first))
            if mode != "grow":
                inputs.append(self.kept[m])
            first += 0 if mode == "enter" else size
            rows.append({"half": size // 2, "hold": 0, "grow": 2 * size}.get(mode, size))
        if self.rider is not None and k == steps - 1:
            blocks.append(("enter", self.rider.shape[0], 0))
            inputs.append(self.rider)
        elif self.rider is not None and k >= steps:
            blocks.append(("ride", self.rider.shape[0], first))
        flag = self.flags[min(k + 1, steps - 1)]
        self.message, *kept = advance(flag, self.message, got, blocks, inputs)
        for m, (mode, _, _) in enumerate(blocks[: len(rows)]):
            if mode in ("half", "flat", "hold"):
                self.kept[m] = kept.pop(0)
        self.rows = rows
        self.count = k + 1
        step = self.count if self.count < steps else 2 * steps - 1 - self.count
        self.got = self.over.swap(self.message, step)
        return self.message

    def run_out(self):
        while self.count < 2 * len(self.over.bits) - 1:
            self.next()


def silu_slope(values):
    logistic = jax.nn.sigmoid(values)
    return logistic * (1.0 + values * (1.0 - logistic))


def cost(ops, lanes, length, width, states):
    work = lanes * length * width * states
    return pl.CostEstimate(flops=ops * work * 16, bytes_accessed=work * 2, transcendentals=work)


def settle_kernel(names, layout, order_ref, *refs, starts=True, waits=True):
    parts, outs = refs[: len(layout)], refs[-2 - names : -2]
    wide, sems = refs[-2:]
    copies, at = [], 0
    for part, (out, lead, which, first, blocks, turned, offset, count) in zip(parts, layout, strict=True):
        size = count // blocks
        for b in range(blocks):
            source = order_ref[which + 2 + b]
            goal = pl.multiple_of((order_ref[which + first] + b) * size, size)
            ref = outs[out] if lead is None else outs[out].at[lead]
            if turned:
                spot = wide.at[at : at + part.shape[1], 0:size]
                target = ref.at[:, pl.ds(goal, size)]
            else:
                spot = wide.at[at : at + size, 0 : part.shape[1]]
                target = ref.at[pl.ds(goal, size), :]
            at += part.shape[1] if turned else size
            copies.append(pltpu.make_async_copy(spot, target, sems.at[len(copies)]))
            if starts:
                rows = part[pl.ds(pl.multiple_of(offset + source * size, size), size), :].astype(F32)
                spot[...] = jnp.transpose(rows) if turned else rows
                copies[-1].start()
    for copy in copies:
        if waits:
            copy.wait()


def settle(orders, parts, layout, shapes, into=()):
    any_space = pl.BlockSpec(memory_space=pl.ANY)
    rows = sum(p.shape[1] * l[4] if l[5] else l[7] for p, l in zip(parts, layout, strict=True))
    width = max(l[7] // l[4] if l[5] else p.shape[1] for p, l in zip(parts, layout, strict=True))
    count = sum(l[4] for l in layout)
    return pl.pallas_call(
        functools.partial(settle_kernel, len(shapes), layout),
        in_specs=[pl.BlockSpec(memory_space=pltpu.SMEM)] + [VMEM] * len(parts) + [any_space] * len(into),
        out_specs=[any_space] * len(shapes),
        out_shape=[jax.ShapeDtypeStruct(s, F32) for s in shapes],
        input_output_aliases={1 + len(parts) + k: k for k in range(len(into))},
        scratch_shapes=[pltpu.VMEM((rows, width), F32), pltpu.SemaphoreType.DMA((count,))],
        compiler_params=pltpu.CompilerParams(vmem_limit_bytes=16 << 20),
        name="settle",
    )(orders, *parts, *into)


def deal_rows(sizes, offset, order_ref, own_ref, late_ref, outs, rows):
    blocks = order_ref.shape[0]
    size = rows.shape[0] // blocks
    for b in range(blocks):
        source = order_ref[b]
        for part, first in ((own_ref, 0), (late_ref, blocks // 2)):

            @pl.when(jnp.logical_and(source >= first, source < first + blocks // 2))
            def _():
                at = pl.ds(pl.multiple_of(offset + (source - first) * size, size), size)
                rows[b * size : (b + 1) * size, :] = part[at, :].astype(F32)

    at = 0
    for out, count in zip(outs, sizes, strict=True):
        out[...] = rows[at : at + count, :]
        at += count


def finish_kernel(sizes, layout, offset, last, order_ref, flat_ref, own_ref, late_ref, into_ref, *refs):
    out, small, (total, rows, wide, sems) = refs[0], refs[1:-4], refs[-4:]
    settle_kernel(1, layout, order_ref, late_ref, out, wide, sems, waits=False)
    deal_rows(sizes, offset, flat_ref, own_ref, late_ref, small, rows)
    rider = own_ref[last : last + 16, :].astype(F32) + late_ref[last : last + 16, :].astype(F32)
    total[...] = rider[0:1, : total.shape[1]]
    settle_kernel(1, layout, order_ref, late_ref, out, wide, sems, starts=False)


def finish(orders, flat_order, own, late, layout, offset, count, sizes, gain_width, into):
    width = own.shape[1]
    any_space, smem = pl.BlockSpec(memory_space=pl.ANY), pl.BlockSpec(memory_space=pltpu.SMEM)
    shape = jax.ShapeDtypeStruct
    return pl.pallas_call(
        functools.partial(finish_kernel, sizes, layout, offset, offset + count),
        in_specs=[smem, smem, VMEM, VMEM, any_space],
        out_specs=[any_space] + [VMEM] * (len(sizes) + 1),
        out_shape=[shape(into.shape, F32)] + [shape((n, width), F32) for n in sizes] + [shape((1, gain_width), F32)],
        input_output_aliases={4: 0},
        scratch_shapes=[
            pltpu.VMEM((2 * count, width), F32),
            pltpu.VMEM((layout[0][7], width), F32),
            pltpu.SemaphoreType.DMA((layout[0][4],)),
        ],
        compiler_params=pltpu.CompilerParams(vmem_limit_bytes=16 << 20),
        name="finish",
    )(orders, flat_order, own, late, into)


def hop_kernel(got_ref, out_ref, back_ref, row_ref, message, other, out_new, back_new, row_new):
    lanes, length, width = out_ref.shape
    half = width // 2
    for l in range(lanes):
        for m, (kept, new, sent) in enumerate(((out_ref, out_new, other), (back_ref, back_new, message))):
            o = slice(m * length, (m + 1) * length)
            new[l] = kept[l, :, :half] + got_ref[l, o, :half].astype(F32)
            send = kept[l, :, half:] + got_ref[l, o, half:].astype(F32)
            sent[l, :length, :] = send.astype(BF16)
        rows = got_ref[l, 2 * length :, :].astype(F32)
        came = jnp.concatenate([rows[r : r + 1] for r in range(2 * length // width)], axis=1)
        total = row_ref[l : l + 1, :] + came[:, :length] + came[:, length:]
        row_new[l : l + 1, :] = total
        high = total.astype(BF16).astype(F32)
        both = jnp.concatenate([high, total - high], axis=1)
        pieces = [both[:, at : at + half] for at in range(0, 2 * length, half)]
        pieces.append(jnp.zeros((message.shape[1] - length - len(pieces), half), F32))
        message[l, length:, :] = jnp.concatenate(pieces, axis=0).astype(BF16)


def hop(got, out_kept, back_kept, row_dot):
    lanes, length, width = out_kept.shape
    shape = jax.ShapeDtypeStruct
    half = shape((lanes, length, width // 2), F32)
    rows = length - (-(4 * length // width) // 16) * 16
    return pl.pallas_call(
        hop_kernel,
        in_specs=[VMEM] * 4,
        out_specs=[VMEM] * 5,
        out_shape=[
            shape((lanes, rows, width // 2), BF16),
            shape((lanes, length, width // 2), BF16),
            half,
            half,
            shape(row_dot.shape, F32),
        ],
        compiler_params=pltpu.CompilerParams(vmem_limit_bytes=12 << 20),
        name="hop",
    )(got, out_kept, back_kept, row_dot)


def product_kernel(flag_ref, left_ref, right_ref, more_ref, message):
    half = message.shape[0] - more_ref.shape[0]
    at = pl.multiple_of((1 - flag_ref[0]) * half, half)
    for block in range(0, half, min(half, 256)):
        size = min(half, 256)
        cut = left_ref[:, pl.ds(pl.multiple_of(at + block, size), size)]
        total = lax.dot_general(cut, right_ref[...], (((0,), (0,)), ((), ())), preferred_element_type=F32)
        message[block : block + size, :] = total.astype(BF16)
    message[half:, :] = more_ref[...].astype(BF16)


def sent_product(flag, left, right, more):
    half, width = left.shape[1] // 2, right.shape[1]
    return pl.pallas_call(
        product_kernel,
        in_specs=[pl.BlockSpec(memory_space=pltpu.SMEM)] + [VMEM] * 3,
        out_specs=VMEM,
        out_shape=jax.ShapeDtypeStruct((half + more.shape[0], width), BF16),
        compiler_params=pltpu.CompilerParams(vmem_limit_bytes=16 << 20),
        name="sent_product",
    )(flag, left, right, more)


def pack_kernel(sizes, flag_ref, sent_ref, *refs):
    parts, (message, kept, rows) = refs[:-3], refs[-3:]
    at = 0
    for part, size in zip(parts, sizes, strict=True):
        if part.ndim == 3:
            total = part[0]
            for l in range(1, part.shape[0]):
                total = total + part[l]
            rows[at : at + size, :] = total
        else:
            rows[at : at + size, :] = part[0:size, :]
        at += size
    rows[at:, :] = jnp.zeros((rows.shape[0] - at, rows.shape[1]), F32)
    half, first = kept.shape[0], sent_ref.shape[0]
    up = flag_ref[0]
    kept[...] = rows[pl.ds(pl.multiple_of(up * half, half), half), :]
    message[0:first, :] = sent_ref[...]
    message[first:, :] = rows[pl.ds(pl.multiple_of((1 - up) * half, half), half), :].astype(BF16)


def pack(flag, sent, parts, sizes, half):
    width = sent.shape[1]
    shape = jax.ShapeDtypeStruct
    return pl.pallas_call(
        functools.partial(pack_kernel, sizes),
        in_specs=[pl.BlockSpec(memory_space=pltpu.SMEM)] + [VMEM] * (1 + len(parts)),
        out_specs=[VMEM] * 2,
        out_shape=[shape((sent.shape[0] + half, width), BF16), shape((half, width), F32)],
        scratch_shapes=[pltpu.VMEM((2 * half, width), F32)],
        compiler_params=pltpu.CompilerParams(vmem_limit_bytes=8 << 20),
        name="pack",
    )(flag, sent, *parts)


def join_kernel(lanes, short, up_ref, got_ref, log_ref, total_ref, window_ref, message, total, window):
    states, width = log_ref.shape
    rate = -jnp.exp(log_ref[...]) * LOG2E
    upper = up_ref[0] != 0
    count = lanes * states
    spans = got_ref[got_ref.shape[0] - 16 :, :].astype(F32)
    upper_next = up_ref[1] != 0
    sums, befores, behinds = [], [], []
    for l in range(lanes):
        s = slice(l * states, (l + 1) * states)
        g = slice(count + l * states, count + (l + 1) * states)
        span, came = total_ref[2 * count + l : 2 * count + l + 1, :], spans[l : l + 1]
        before = window_ref[2 * count + l : 2 * count + l + 1, :]
        behind = window_ref[2 * count + lanes + l : 2 * count + lanes + l + 1, :]
        through, through_came = jnp.exp2(span * rate), jnp.exp2(came * rate)
        end, pull = total_ref[s, :], total_ref[g, :]
        end_came = got_ref[s, :].astype(F32)
        pull_came = end_came if short[0] else got_ref[g, :].astype(F32)
        end_new = jnp.where(upper, end + through * end_came, end_came + through_came * end)
        pull_new = jnp.where(upper, pull_came + through_came * pull, pull + through * pull_came)
        total[s, :], total[g, :] = end_new, pull_new
        if short[1]:
            message[s, :] = jnp.where(upper_next, pull_new, end_new).astype(BF16)
        else:
            message[s, :], message[g, :] = end_new.astype(BF16), pull_new.astype(BF16)
        enter = window_ref[s, :] + jnp.exp2(before * rate) * end_came
        leave = window_ref[g, :] + jnp.exp2(behind * rate) * pull_came
        window[s, :] = jnp.where(upper, enter, window_ref[s, :])
        window[g, :] = jnp.where(upper, window_ref[g, :], leave)
        sums.append(span + came)
        befores.append(jnp.where(upper, before + came, before))
        behinds.append(jnp.where(upper, behind, behind + came))
    fill = jnp.zeros((8 - lanes, width), F32)
    rows = jnp.concatenate([*sums, fill], axis=0)
    total[2 * count :, :] = rows
    message[message.shape[0] - 16 :, :] = jnp.concatenate([rows, jnp.zeros((8, width), F32)], axis=0).astype(BF16)
    fill = jnp.zeros((8 - 2 * lanes, width), F32)
    window[2 * count :, :] = jnp.concatenate([*befores, *behinds, fill], axis=0)


def join(lanes, short, up, got, log, total, window):
    shape = jax.ShapeDtypeStruct
    rows = 16 + lanes * log.shape[0] * (1 if short[1] else 2)
    return pl.pallas_call(
        functools.partial(join_kernel, lanes, short),
        in_specs=[pl.BlockSpec(memory_space=pltpu.SMEM)] + [VMEM] * 4,
        out_specs=[VMEM] * 3,
        out_shape=[shape((rows, got.shape[1]), BF16), shape(total.shape, F32), shape(window.shape, F32)],
        compiler_params=pltpu.CompilerParams(vmem_limit_bytes=8 << 20),
        name="join",
    )(up, got, log, total, window)


def iota(shape, dim):
    return lax.broadcasted_iota(jnp.int32, shape, dim)


def widen(part, width):
    return jnp.concatenate([part] * (width // part.shape[1]), axis=1)


def dot(a, b):
    return jnp.dot(a, b, preferred_element_type=F32)


def dot_t(a, b):
    return lax.dot_general(a, b, (((1,), (1,)), ((), ())), preferred_element_type=F32)


def row_of(ref, t, count):
    return jnp.broadcast_to(ref[pl.ds(t, 1), :], (count, ref.shape[1]))


def rows_of(i, count):
    return pl.ds(pl.multiple_of(i * count, count), count)


def chunk_columns(ref, i):
    per = LANE // CHUNK
    tile = ref[:, rows_of(i // per, LANE)]
    return pltpu.roll(tile, LANE - (i % per) * CHUNK, 1)


def spread_column(tile, j, width):
    part = jnp.broadcast_to(tile[:, j : j + 1], (tile.shape[0], LANE))
    return widen(part, width)


def selectors(states):
    wide = CHUNK * states
    per_state = iota((states, wide), 1) % states == iota((states, wide), 0)
    per_step = iota((CHUNK, wide), 1) // states == iota((CHUNK, wide), 0)
    return per_state.astype(F32), per_step.astype(F32)


def from_lanes(first, states):
    shape = (LANE, CHUNK * states)
    return (iota(shape, 0) == first + iota(shape, 1) % states).astype(BF16)


def to_lanes(first, states):
    shape = (CHUNK * states, LANE)
    return (iota(shape, 1) == first + iota(shape, 0) % states).astype(BF16)


def by_step(proj, lanes, per_step):
    spread = dot(proj, lanes)
    return spread * jnp.concatenate([per_step] * (spread.shape[0] // CHUNK), axis=0)


def ends_kernel(
    low_rank, sent_ref, got_ref, wdt_ref, bias_ref, log_ref, mixed_ref, gy_ref,
    end_ref, pull_ref, span_ref, dt_ref, u_ref, proj_ref,
    ahead, behind, left_b, left_c, xa, xb, ya, yb,
):
    length, width = dt_ref.shape
    states = log_ref.shape[0]
    rate = -jnp.exp(log_ref[...]) * LOG2E
    per_state, per_step = selectors(states)
    chunks = length // CHUNK
    upto = (iota((length, length), 1) <= iota((length, length), 0)).astype(BF16)
    after = (iota((length, length), 1) > iota((length, length), 0)).astype(BF16)
    proj = sent_ref[...].astype(F32) + got_ref[...].astype(F32)
    proj_ref[...] = proj
    proj = proj.astype(BF16)
    for first, left in ((low_rank, left_b), (low_rank + states, left_c)):
        spread = by_step(proj, from_lanes(first, states), per_step)
        for i in range(chunks):
            flat = jnp.sum(spread[i * CHUNK : (i + 1) * CHUNK], axis=0, keepdims=True)
            left[i * states : (i + 1) * states, :] = (flat * per_state).astype(BF16)
    block = min(128, length)
    for i in range(length // block):
        o = slice(i * block, (i + 1) * block)
        pre = dot(proj[o], wdt_ref[...]) + bias_ref[...]
        small = jnp.exp(-jnp.abs(pre))
        one = 1.0 + small
        series = small * (1.0 - small * (0.5 - small * (1.0 / 3.0)))
        dt = jnp.maximum(pre, 0.0) + jnp.where(small < 1e-3, series, jnp.log(one))
        dt_ref[o, :] = dt
        u_ref[o, :] = dt * mixed_ref[o, :]
    dt = dt_ref[...]
    high = dt.astype(BF16)
    low = (dt - high.astype(F32)).astype(BF16)
    ahead[...] = dot(upto, high) + dot(upto, low)
    behind[...] = dot(after, high) + dot(after, low)
    span_ref[...] = ahead[length - 1 : length, :]
    xb[...] = jnp.zeros(xb.shape, BF16)
    yb[...] = jnp.zeros(yb.shape, BF16)

    def flush(i, x, y, sums):
        o = rows_of(jnp.maximum(i, 0), states)
        return sums[0] + dot(left_b[o, :], x[...]), sums[1] + dot(left_c[o, :], y[...])

    def fill(i, x, y):
        for j in range(CHUNK):
            t = i * CHUNK + j
            s = slice(j * states, (j + 1) * states)
            to_end = jnp.exp2(row_of(behind, t, states) * rate)
            x[s, :] = (to_end * row_of(u_ref, t, states)).astype(BF16)
            to_here = jnp.exp2(row_of(ahead, t, states) * rate)
            y[s, :] = (to_here * row_of(gy_ref, t, states)).astype(BF16)

    def body(k, sums):
        for i in range(0, ROUND, 2):
            at = ROUND * k + i
            sums = flush(at - 1, xb, yb, sums)
            fill(at, xa, ya)
            sums = flush(at, xa, ya, sums)
            fill(at + 1, xb, yb)
        return sums

    zero = jnp.zeros((states, width), F32)
    sums = lax.fori_loop(0, chunks // ROUND, body, (zero, zero))
    sums = flush(chunks - 1, xb, yb, sums)
    end_ref[...] = sums[0]
    pull_ref[...] = sums[1]


def lane_spec(*shape):
    return pl.BlockSpec((None, *shape), lambda l: (l,) + (0,) * len(shape))


def whole_spec(*shape):
    return pl.BlockSpec(shape, lambda l: (0,) * len(shape))


def scan_ends(low_rank, sent, got, w_dt, bias, log, mixed, gy):
    lanes, length, width = mixed.shape
    states = log.shape[0]
    shape = jax.ShapeDtypeStruct
    token = shape((lanes, length, width), F32)
    state = shape((lanes, states, width), F32)
    tokens, state_spec, narrow = lane_spec(length, width), lane_spec(states, width), lane_spec(length, LANE)
    return pl.pallas_call(
        functools.partial(ends_kernel, low_rank),
        grid=(lanes,),
        in_specs=[
            narrow,
            narrow,
            whole_spec(*w_dt.shape),
            whole_spec(1, width),
            whole_spec(states, width),
            tokens,
            tokens,
        ],
        out_specs=[state_spec, state_spec, lane_spec(1, width), tokens, tokens, narrow],
        out_shape=[state, state, shape((lanes, 1, width), F32)]
        + [pltpu.HBM((lanes, length, width), F32)] * 2
        + [shape(sent.shape, F32)],
        scratch_shapes=[pltpu.VMEM((length, width), F32)] * 2
        + [pltpu.VMEM((length // CHUNK * states, CHUNK * states), BF16)] * 2
        + [pltpu.VMEM((CHUNK * states, width), BF16)] * 4,
        compiler_params=pltpu.CompilerParams(vmem_limit_bytes=14 << 20),
        cost_estimate=cost(8, lanes, length, width, states),
        name="scan_ends",
    )(sent, got, w_dt, bias, log, mixed, gy)


def forward_kernel(
    low_rank, lanes, starts_ref, proj_ref, log_ref, dt_ref, u_ref, gy_ref, begin_ref,
    y_ref, gc_ref, hs_ref,
    kept, pa, pb, cols, left_c, masked, sems,
):
    length, width = dt_ref.shape
    states = log_ref.shape[0]
    l = pl.program_id(0)
    rate = -jnp.exp(log_ref[...]) * LOG2E
    _, per_step = selectors(states)
    wide = CHUNK * states
    chunks = length // CHUNK

    half = chunks // 2 * wide

    def leave(slot, part):
        rows = pl.ds(part * half, half)
        return pltpu.make_async_copy(kept.at[slot, rows, :], hs_ref.at[slot, rows, :], sems.at[slot, part])

    begin = jnp.where(starts_ref[l] != 0, 0.0, begin_ref[...])
    proj = proj_ref[...]
    cols[...] = jnp.transpose(proj)[low_rank : low_rank + states]
    spread = by_step(proj.astype(BF16), from_lanes(low_rank + states, states), per_step)
    left_c[...] = spread.astype(BF16)

    def flush(i, p):
        o = rows_of(jnp.maximum(i, 0), CHUNK)
        h = p[...]
        y_ref[o, :] = dot(left_c[o, :], h)
        masked[o, :] = (dot_t(gy_ref[o, :].astype(BF16), h) * per_step).astype(BF16)

    def fill(i, state, p):
        b_tile = chunk_columns(cols, i)
        low = state.astype(BF16)
        for j in range(CHUNK):
            t = i * CHUNK + j
            b = spread_column(b_tile, j, width)
            decay = jnp.exp2(row_of(dt_ref, t, states) * rate)
            state = decay * state + row_of(u_ref, t, states) * b
            kept[l, rows_of(t, states), :] = low
            low = state.astype(BF16)
            p[j * states : (j + 1) * states, :] = low
        return state

    def body(k, state):
        for i in range(0, ROUND, 2):
            at = ROUND * k + i
            flush(at - 1, pb)
            state = fill(at, state, pa)
            flush(at, pa)
            state = fill(at + 1, state, pb)
        return state

    rounds = chunks // ROUND
    state = lax.fori_loop(0, rounds // 2, body, begin)
    leave(l, 0).start()
    lax.fori_loop(rounds // 2, rounds, body, state)
    leave(l, 1).start()
    flush(chunks - 1, pb)
    gc_ref[...] = dot(masked[...], to_lanes(low_rank + states, states))

    @pl.when(l == lanes - 1)
    def _():
        for slot in range(lanes):
            for part in range(2):
                leave(slot, part).wait()


def scan_forward(low_rank, starts, proj, log, dt, u, gy, begin):
    lanes, length, width = dt.shape
    states = log.shape[0]
    shape = jax.ShapeDtypeStruct
    tokens, state_spec, narrow = lane_spec(length, width), lane_spec(states, width), lane_spec(length, LANE)
    return pl.pallas_call(
        functools.partial(forward_kernel, low_rank, lanes),
        grid=(lanes,),
        in_specs=[
            pl.BlockSpec(memory_space=pltpu.SMEM),
            narrow,
            whole_spec(states, width),
            tokens,
            tokens,
            tokens,
            state_spec,
        ],
        out_specs=[tokens, narrow, pl.BlockSpec(memory_space=pltpu.HBM)],
        out_shape=[
            shape((lanes, length, width), F32),
            shape(proj.shape, F32),
            shape((lanes, length * states, width), BF16),
        ],
        scratch_shapes=[pltpu.VMEM((lanes, length * states, width), BF16)]
        + [pltpu.VMEM((CHUNK * states, width), BF16)] * 2
        + [
            pltpu.VMEM((states, length), F32),
            pltpu.VMEM((length, CHUNK * states), BF16),
            pltpu.VMEM((length, CHUNK * states), BF16),
            pltpu.SemaphoreType.DMA((lanes, 2)),
        ],
        compiler_params=pltpu.CompilerParams(vmem_limit_bytes=20 << 20),
        cost_estimate=cost(8, lanes, length, width, states),
        name="scan_forward",
    )(starts, proj, log, dt, u, gy, begin)


def backward_kernel(
    low_rank, lanes, proj_ref, log_ref, dt_ref, u_ref, gy_ref, last_ref, gc_ref, hs_ref, *refs
):
    (turn_ref, pull_ref, gbc_ref, ga_ref,
     kept, pa, pb, qa, qb, ra, rb, cols, left_b, masked, sems) = refs[-15:]
    length, width = dt_ref.shape
    states = log_ref.shape[0]
    l = pl.program_id(0)
    plain = -jnp.exp(log_ref[...])
    rate = plain * LOG2E
    rate_low = plain.astype(BF16)
    per_state, per_step = selectors(states)
    per_state_low, per_step_low = per_state.astype(BF16), per_step.astype(BF16)
    chunks = length // CHUNK

    half = length // 2 * states

    def enter(slot, part):
        rows = pl.ds(part * half, half)
        return pltpu.make_async_copy(hs_ref.at[slot, rows, :], kept.at[slot, rows, :], sems.at[slot, part])

    @pl.when(l == 0)
    def _():
        for slot in range(lanes):
            for part in (1, 0):
                enter(slot, part).start()

    for ref in (pb, qb, rb):
        ref[...] = jnp.zeros(ref.shape, BF16)
    proj = proj_ref[...]
    cols[...] = jnp.transpose(proj)[low_rank + states : low_rank + 2 * states]
    left_b[...] = by_step(proj.astype(BF16), from_lanes(low_rank, states), per_step).astype(BF16)

    def flush(i, p, q, r, ga):
        o = rows_of(jnp.minimum(i, chunks - 1), CHUNK)
        grad = p[...]
        pull_ref[o, :] = dot(left_b[o, :], grad)
        masked[o, :] = (dot_t(u_ref[o, :].astype(BF16), grad) * per_step).astype(BF16)
        turn_ref[o, :] = dot(per_step_low, q[...])
        return ga + dot(per_state_low, r[...])

    def fill(i, carry, p, q, r):
        c_tile = chunk_columns(cols, i)
        for j in reversed(range(CHUNK)):
            t = i * CHUNK + j
            s = slice(j * states, (j + 1) * states)
            c = spread_column(c_tile, j, width)
            dt = row_of(dt_ref, t, states)
            grad = carry + row_of(gy_ref, t, states) * c
            carry = jnp.exp2(dt * rate) * grad
            p[s, :] = grad.astype(BF16)
            turn = carry.astype(BF16) * kept[l, rows_of(t, states), :] * rate_low
            q[s, :] = turn
            r[s, :] = turn * dt.astype(BF16)
        return carry

    def body(k, carried):
        carry, ga = carried
        for i in range(0, ROUND, 2):
            at = chunks - 1 - ROUND * k - i
            ga = flush(at + 1, pb, qb, rb, ga)
            carry = fill(at, carry, pa, qa, ra)
            ga = flush(at, pa, qa, ra, ga)
            carry = fill(at - 1, carry, pb, qb, rb)
        return carry, ga

    rounds = chunks // ROUND
    carried = (last_ref[...], jnp.zeros((states, width), F32))
    enter(l, 1).wait()
    carried = lax.fori_loop(0, rounds // 2, body, carried)
    enter(l, 0).wait()
    _, ga = lax.fori_loop(rounds // 2, rounds, body, carried)
    ga_ref[...] = flush(0, pb, qb, rb, ga)
    gbc_ref[...] = gc_ref[...] + dot(masked[...], to_lanes(low_rank, states))


def scan_backward(low_rank, proj, log, dt, u, gy, last, gc, hs, *earlier):
    lanes, length, width = dt.shape
    states = log.shape[0]
    shape = jax.ShapeDtypeStruct
    tokens, state_spec, narrow = lane_spec(length, width), lane_spec(states, width), lane_spec(length, LANE)
    token = shape((lanes, length, width), F32)
    return pl.pallas_call(
        functools.partial(backward_kernel, low_rank, lanes),
        grid=(lanes,),
        in_specs=[narrow, whole_spec(states, width), tokens, tokens, tokens, state_spec, narrow]
        + [pl.BlockSpec(memory_space=pltpu.HBM)]
        + [pl.BlockSpec(memory_space=pl.ANY)] * len(earlier),
        out_specs=[tokens, tokens, narrow, state_spec],
        out_shape=[token, token, shape(proj.shape, F32), shape((lanes, states, width), F32)],
        scratch_shapes=[pltpu.VMEM((lanes, length * states, width), BF16)]
        + [pltpu.VMEM((CHUNK * states, width), BF16)] * 6
        + [
            pltpu.VMEM((states, length), F32),
            pltpu.VMEM((length, CHUNK * states), BF16),
            pltpu.VMEM((length, CHUNK * states), BF16),
            pltpu.SemaphoreType.DMA((lanes, 2)),
        ],
        compiler_params=pltpu.CompilerParams(vmem_limit_bytes=22 << 20),
        cost_estimate=cost(12, lanes, length, width, states),
        name="scan_backward",
    )(proj, log, dt, u, gy, last, gc, hs, *earlier)


def per_device(
    inputs,
    row_starts,
    norm_gain,
    in_weight,
    conv_weight,
    conv_bias,
    xproj_weight,
    dtproj_weight,
    dt_bias,
    decay_log,
    skip_gain,
    out_weight,
    output_grad,
):
    lane_count, length, shard_width = inputs.shape
    low_rank = dtproj_weight.shape[0]
    state_count = decay_log.shape[0]
    tap_count = conv_weight.shape[0]
    inner_width = conv_bias.shape[0]
    model_width = norm_gain.shape[0]
    starts = row_starts.astype(F32)
    carry_mask = (1.0 - starts)[:, :, None]
    mp_index, mp_size = lax.axis_index("mp"), lax.axis_size("mp")
    seq_index, seq_size = lax.axis_index("seq"), lax.axis_size("seq")
    mp_bits, seq_bits = bits_of("mp"), bits_of("seq")
    near_first = [int(format(k, "0%db" % len(mp_bits))[::-1], 2) for k in range(mp_size)]

    def blocks(array, axis, order):
        parts = [
            lax.dynamic_slice_in_dim(array, (mp_index ^ k) * shard_width, shard_width, axis) for k in order
        ]
        return jnp.concatenate(parts, axis=axis)

    x_parts, grad_parts = {0: inputs.astype(BF16)}, {}
    square = jnp.sum(jnp.square(inputs), axis=2)
    for bit in reversed(mp_bits):
        for k in list(x_parts):
            x_parts[k | bit] = swap(x_parts[k], "mp", bit)
        square = square + swap(square, "mp", bit)
    grad_parts[0] = after(output_grad.astype(BF16), x_parts[mp_bits[-1]])
    for bit in reversed(mp_bits[1:]):
        for k in list(grad_parts):
            grad_parts[k | bit] = swap(grad_parts[k], "mp", bit)
    near = list(range(mp_size))
    over = Reduction()
    per = shard_width * seq_size // model_width
    halves = seq_size // 2
    ups = ((seq_index & jnp.array([*seq_bits, 0])) != 0).astype(jnp.int32)
    ups = [ups[step : step + 2] for step in range(len(seq_bits))]
    orders = jnp.concatenate([over.order(per, mp_index), over.order(1, 0)])
    flat_order = over.flat_order()
    flags = [over.own(step)[None] for step in range(len(seq_bits))]
    span_more = FAR * starts[:, :, None]
    w_in = blocks(in_weight, 1, near).astype(BF16)
    w_out = lax.optimization_barrier(out_weight.astype(BF16))
    gain = blocks(norm_gain, 0, near)
    w_x = jnp.pad(xproj_weight.astype(BF16), ((0, 0), (0, -xproj_weight.shape[1] % LANE)))
    w_dt = jnp.pad(dtproj_weight.astype(BF16), ((0, -low_rank % LANE), (0, 0)))
    w_dt = lax.optimization_barrier(w_dt)
    inv_rms = lax.rsqrt(square[:, :, None] / model_width + 1e-05)
    x_parts[near[-1]] = after(x_parts[near[-1]], orders, flat_order, span_more, *flags, *ups, w_out, w_dt)
    x_whole = jnp.concatenate([x_parts[k] for k in near], axis=2)
    normed = (x_whole.astype(F32) * inv_rms * gain).astype(BF16)
    rim_count = 8
    rim_normed = from_behind(normed[:, length - rim_count :, :], "seq", 1)
    inner_act = jnp.einsum("ltd,de->lte", normed, w_in[0], preferred_element_type=F32).astype(BF16)
    rim_rows = jnp.einsum("ltd,de->lte", rim_normed, w_in[0], preferred_element_type=F32).astype(BF16)
    rim_rows = after(rim_rows, *grad_parts.values())
    rim_rows = (rim_rows.astype(F32) * carry_mask)[:, rim_count - (tap_count - 1) :]
    padded = jnp.concatenate([rim_rows, inner_act.astype(F32)], axis=1)
    conv_sum = conv_bias + conv_weight[0] * padded[:, 0:length]
    for tap in range(1, tap_count):
        conv_sum = conv_sum + conv_weight[tap] * padded[:, tap : tap + length]
    mixed = jax.nn.silu(conv_sum)
    mixed_low = mixed.astype(BF16)
    sent = jnp.einsum("lte,er->ltr", mixed_low, w_x, preferred_element_type=F32).astype(BF16)
    for bit in mp_bits[:-1]:
        sent = (sent.astype(F32) + swap(sent, "mp", bit).astype(F32)).astype(BF16)
    got = swap(sent, "mp", mp_bits[-1])
    gate_in = jnp.einsum("ltd,de->lte", after(normed, sent), w_in[1], preferred_element_type=F32)
    for k in list(grad_parts):
        grad_parts[k] = after(grad_parts[k], sent)
        grad_parts[k | 1] = swap(grad_parts[k], "mp", 1)
    normed_more = jnp.concatenate(
        [after(normed, sent).reshape(-1, model_width), rim_normed.reshape(-1, model_width)], axis=0
    )[None]
    grad_whole = jnp.concatenate(
        [
            sum(jnp.where(k == (mp_index ^ block), grad_parts[k], 0) for k in range(mp_size))
            for block in range(mp_size)
        ],
        axis=2,
    )
    grad_gated = jnp.einsum("ltd,ed->lte", grad_whole, w_out, preferred_element_type=F32)
    grad_scan = grad_gated * jax.nn.silu(gate_in)
    end_state, pulled, span, dt, source, projected = scan_ends(
        low_rank, sent, got, w_dt, dt_bias[None], decay_log, mixed, grad_scan
    )
    span = span + span_more
    count = lane_count * state_count
    flat = (count, inner_width)
    total = jnp.concatenate(
        [
            end_state.reshape(flat),
            (pulled * carry_mask).reshape(flat),
            span.reshape(lane_count, inner_width),
            jnp.zeros((8 - lane_count, inner_width), F32),
        ],
        axis=0,
    )
    message = jnp.pad(total.astype(BF16), ((0, 8), (0, 0)))
    window = jnp.zeros_like(total)
    for step, bit in enumerate(seq_bits):
        short = (step == len(seq_bits) - 1, step == len(seq_bits) - 2)
        if step == 0:
            w_late = after(w_out, message)
            w_spread = blocks(w_late, 1, near_first)
            w_late = after(w_in, message)
            w_back = jnp.concatenate(
                [w_late[:, k * shard_width : (k + 1) * shard_width] for k in near_first], axis=1
            )
        got = swap(message, "seq", bit)
        message, total, window = join(lane_count, short, ups[step], got, decay_log, total, window)
    window = window.reshape(-1, inner_width)
    begin = window[:count].reshape(end_state.shape)
    last = window[count : 2 * count].reshape(end_state.shape)
    projected, normed_more, w_back, w_spread = lax.optimization_barrier(
        (projected, normed_more, w_back, w_spread)
    )
    y, grad_read, states_all = scan_forward(
        low_rank, row_starts[:, 0], projected, decay_log, dt, source, grad_scan, begin
    )
    scan_out = y + skip_gain * mixed
    gated = (scan_out * jax.nn.silu(gate_in)).astype(BF16)
    grad_gate = (grad_gated * scan_out * silu_slope(gate_in)).astype(BF16)
    half_width = model_width // 2
    first = [over.sent(normed, grad_gate)]
    first.append(over.sent(grad_whole, after(gated, first[0])))
    sum_first = Sum(over, first, (False, False), flags)
    sum_first.kept = [over.kept(after(normed, sum_first.message), grad_gate)]
    sum_first.kept.append(over.kept(grad_whole, after(gated, sum_first.kept[0])))
    turn, pull, part, grad_log = scan_backward(
        low_rank, projected, decay_log, dt, source, grad_scan, last, grad_read, states_all, *sum_first.kept
    )
    grad_slope = (turn + pull * mixed) * -jnp.expm1(-dt)
    grad_pre = grad_slope.astype(BF16)
    part = part + jnp.einsum("lte,re->ltr", grad_pre, w_dt, preferred_element_type=F32)
    sent = part.astype(BF16)
    for bit in mp_bits[:-1]:
        got = swap(sent, "mp", bit)
        if bit == 1:
            got = after(got, sum_first.next(sent))
        sent = (sent.astype(F32) + got.astype(F32)).astype(BF16)
    got = swap(sent, "mp", mp_bits[-1])
    grad_dt_w = jnp.einsum(
        "ltr,lte->re", projected.astype(BF16), after(grad_pre, sent), preferred_element_type=F32
    )
    grad_projected = after(sent, grad_dt_w).astype(F32) + got.astype(F32)
    grad_projected = grad_projected.astype(BF16)
    grad_mixed = pull * dt + grad_scan * skip_gain + jnp.einsum(
        "ltr,er->lte", grad_projected, w_x, preferred_element_type=F32
    )
    grad_conv = grad_mixed * silu_slope(conv_sum)
    grad_conv_b = jnp.sum(grad_conv, axis=(0, 1))
    grad_conv_w = jnp.stack(
        [
            jnp.sum(grad_conv * padded[:, tap : tap + length], axis=(0, 1))
            for tap in range(tap_count)
        ]
    )
    grad_padded = jnp.pad(conv_weight[0] * grad_conv, ((0, 0), (0, tap_count - 1), (0, 0)))
    for tap in range(1, tap_count):
        grad_padded = grad_padded + jnp.pad(
            conv_weight[tap] * grad_conv, ((0, 0), (tap, tap_count - 1 - tap), (0, 0))
        )
    rim_sent = grad_padded[:, : tap_count - 1] * carry_mask
    rim_fill = jnp.zeros((lane_count, rim_count - (tap_count - 1), inner_width), F32)
    rim_rows = jnp.concatenate([rim_fill, rim_sent], axis=1).astype(BF16)
    grad_main = grad_padded[:, tap_count - 1 :].astype(BF16)
    grad_more = jnp.concatenate(
        [grad_main.reshape(-1, inner_width), rim_rows.reshape(-1, inner_width)], axis=0
    )[None]
    grad_x_w = jnp.einsum("ltr,lte->re", grad_projected, after(mixed_low, rim_sent), preferred_element_type=F32)
    small = [
        (grad_conv_w, tap_count),
        (grad_conv_b[None], 1),
        (jnp.sum(grad_slope, axis=(0, 1))[None], 1),
        (jnp.sum(grad_scan * mixed, axis=(0, 1))[None], 1),
        (grad_log, state_count),
        (grad_dt_w, low_rank),
        (grad_x_w, low_rank + 2 * state_count),
    ]
    sizes = [size for _, size in small]
    small_half = -(-sum(sizes) // (8 * seq_size)) * 4 * seq_size
    inner_sent = over.sent(normed_more, after(grad_more, grad_x_w))
    inner_sent, small_kept = pack(flags[0], inner_sent, [part for part, _ in small], sizes, small_half)
    sum_inner = Sum(over, [inner_sent], (False, True), flags, [half_width, small_half])
    step = sum_first.next(sum_inner.message)
    sum_inner.kept = [over.kept(normed_more, after(grad_more, step)), small_kept]
    rim_back = from_behind(after(rim_sent, step), "seq", -1)
    out_sent = jnp.einsum(
        "lte,ed->ltd", after(gated, sum_inner.kept[0]), w_spread[:, half_width:], preferred_element_type=F32
    ).astype(BF16)
    out_kept = jnp.einsum(
        "lte,ed->ltd", after(gated, out_sent), w_spread[:, :half_width], preferred_element_type=F32
    )
    tail_zeros = jnp.zeros((lane_count, length - (tap_count - 1), inner_width), F32)
    grad_inner = grad_padded[:, tap_count - 1 :] + jnp.concatenate(
        [tail_zeros, after(rim_back, out_kept)], axis=1
    )
    grad_inner = grad_inner.astype(BF16)

    def back(part, cut):
        return jnp.einsum("lte,de->ltd", part[0], w_back[0, cut], preferred_element_type=F32) + jnp.einsum(
            "lte,de->ltd", part[1], w_back[1, cut], preferred_element_type=F32
        )

    back_sent = back((grad_inner, grad_gate), slice(half_width, None)).astype(BF16)
    back_kept = back((after(grad_inner, back_sent), grad_gate), slice(0, half_width))
    row_dot = jnp.sum(
        after(grad_inner, back_kept).astype(F32) * inner_act.astype(F32) + grad_gate.astype(F32) * gate_in,
        axis=2,
    )

    def as_rows(values, width):
        high = values.astype(BF16)
        low = (values - high.astype(F32)).astype(BF16)
        rows = jnp.concatenate([high, low], axis=1).reshape(lane_count, -1, width)
        return jnp.pad(rows, ((0, 0), (0, -rows.shape[1] % 16), (0, 0)))

    message = jnp.concatenate([out_sent, back_sent, as_rows(row_dot, half_width)], axis=1)
    step = sum_inner.next(message)
    step = sum_first.next(step)
    got = swap(after(message, step), "mp", 1)
    far = mp_bits[-1]
    for bit in mp_bits[:-1]:
        if bit == 1:
            step = sum_inner.next(message)
            step = sum_first.next(step)
        message, other, out_kept, back_kept, row_dot = hop(after(got, step), out_kept, back_kept, row_dot)
        if 2 * bit == far:
            got = swap(message, "mp", far)
            out_got = swap(after(other, message), "mp", far)
        else:
            message = jnp.concatenate([other, message], axis=1)
            got = swap(message, "mp", 2 * bit)
    got = after(got, message)
    rows = got[:, length:][:, : 2 * length // shard_width].reshape(lane_count, 2 * length).astype(F32)
    row_dot = row_dot + rows[:, :length] + rows[:, length:]
    grad_own = back_kept + got[:, :length].astype(F32)
    unit_own = inputs * inv_rms
    grad_gain = jnp.sum(grad_own * unit_own, axis=(0, 1))
    input_grad = output_grad + inv_rms * (
        grad_own * gain[:shard_width] - unit_own * (row_dot[:, :, None] / model_width)
    )
    grad_gain = jnp.pad(grad_gain, (0, -shard_width % inner_width)).reshape(-1, inner_width)
    sum_inner.rider = jnp.pad(grad_gain, ((0, -grad_gain.shape[0] % 16), (0, 0)))
    step = sum_inner.next(grad_gain)
    step = sum_first.next(step)
    input_grad = after(input_grad, step)
    step = sum_inner.next(step)
    output = inputs + (out_kept + after(out_got, step).astype(F32))
    step = sum_inner.next(output)
    sum_first.run_out()
    second = 2 + halves
    in_shape, out_shape = (2, model_width, inner_width), out_weight.shape
    half = model_width // 2
    layout = [(0, 1, 0, 0, halves, False, 0, half), (0, 1, 0, 1, halves, False, 0, half)]
    ends = (sum_first.message, after(sum_first.got, step))
    if model_width // seq_size % LANE == 0:
        layout += [(1, None, second, 0, halves, True, half, half), (1, None, second, 1, halves, True, half, half)]
        in_w, out_w = settle(orders, [*ends, *ends], layout, [in_shape, out_shape])
    else:
        (in_w,) = settle(orders, [*ends], layout, [in_shape])
        rows = [p[half:].reshape(halves, -1, inner_width)[orders[second + 2 :]].reshape(half, -1) for p in ends]
        up = over.own(0) == 1
        rows = [jnp.where(up, rows[1], rows[0]), jnp.where(up, rows[0], rows[1])]
        out_w = jnp.concatenate(rows, axis=0).astype(F32).T
    sum_inner.run_out()
    ends = (sum_inner.message, sum_inner.got)
    in_w = settle(orders, ends[:1], [(0, 0, 0, 0, halves, False, 0, half)], [in_shape], [in_w])
    count = small_half
    in_w, *parts, grad_gain = finish(
        orders, flat_order, *ends, [(0, 0, 0, 1, halves, False, 0, half)], half, count, sizes, shard_width, in_w[0]
    )
    return (
        output,
        input_grad,
        grad_gain[0],
        in_w,
        parts[0],
        parts[1][0],
        parts[6].T,
        parts[5],
        parts[2][0],
        parts[4],
        parts[3][0],
        out_w,
    )


def solution(mesh):
    in_specs = (
        P(None, "seq", "mp"),
        P(None, "seq"),
        P(),
        P(None, None, "mp"),
        P(None, "mp"),
        P("mp"),
        P("mp", None),
        P(None, "mp"),
        P("mp"),
        P(None, "mp"),
        P("mp"),
        P("mp", None),
        P(None, "seq", "mp"),
    )
    out_specs = (
        P(None, "seq", "mp"),
        P(None, "seq", "mp"),
        P("mp"),
        P(None, None, "mp"),
        P(None, "mp"),
        P("mp"),
        P("mp", None),
        P(None, "mp"),
        P("mp"),
        P(None, "mp"),
        P("mp"),
        P("mp", None),
    )
    return jax.shard_map(
        per_device, mesh=mesh, in_specs=in_specs, out_specs=out_specs, check_vma=False
    )
```

```python
import functools

import jax
import jax.numpy as jnp
from jax import lax
from jax.experimental import pallas as pl
from jax.experimental.pallas import tpu as pltpu
from jax.sharding import PartitionSpec as P

F32 = jnp.float32
BF16 = jnp.bfloat16
LOG2E = 1.4426950408889634
CHUNK = 32
ROUND = 4
LANE = 128
FAR = 1.0e4
VMEM = pl.BlockSpec(memory_space=pltpu.VMEM)


def swap(block, axis, bit):
    devices = lax.axis_size(axis)
    return lax.ppermute(block, axis, [(i, i ^ bit) for i in range(devices)])


def from_behind(block, axis, distance):
    devices = range(lax.axis_size(axis))
    route = [(i - distance, i) for i in devices if i - distance in devices]
    return lax.ppermute(block, axis, route)


def bits_of(axis):
    count = lax.axis_size(axis)
    bits = []
    while (1 << len(bits)) < count:
        bits.append(1 << len(bits))
    return bits


def after(array, *others):
    return lax.optimization_barrier((array, *others))[0]


class Reduction:
    def __init__(self):
        self.bits = bits_of("seq")
        self.orders = [list(self.bits), list(self.bits)]
        if len(self.bits) > 1:
            self.orders[1][:2] = self.bits[1], self.bits[0]
        self.index = lax.axis_index("seq")
        self.odd = lax.axis_index("mp") % 2
        self.mp = lax.axis_size("mp")
        self.count = lax.axis_size("seq")

    def own(self, step):
        even = (self.index & self.orders[0][step]) != 0
        odd = (self.index & self.orders[1][step]) != 0
        return jnp.where(self.odd == 1, odd, even).astype(jnp.int32)

    def swap(self, block, step):
        route = []
        for s in range(self.count):
            for m in range(self.mp):
                route.append((s * self.mp + m, (s ^ self.orders[m % 2][step]) * self.mp + m))
        return lax.ppermute(block, ("seq", "mp"), route)

    def halves(self, block, step):
        half = block.shape[0] // 2
        up = self.own(step)
        kept = lax.dynamic_slice_in_dim(block, up * half, half, 0)
        sent = lax.dynamic_slice_in_dim(block, (1 - up) * half, half, 0)
        return kept, sent

    def part(self, left, right, up):
        half = left.shape[2] // 2
        cut = lax.dynamic_slice_in_dim(left, up * half, half, 2)
        return jnp.einsum("lta,ltb->ab", cut, right, preferred_element_type=F32)

    def sent(self, left, right):
        return self.part(left, right, 1 - self.own(0)).astype(BF16)

    def kept(self, left, right):
        return self.part(left, right, self.own(0))

    def place(self):
        place = jnp.int32(0)
        for step in range(1, len(self.bits)):
            place = place * 2 + self.own(step)
        return place

    def order(self, per, turn):
        blocks = self.count // 2
        pieces = blocks // per
        at = jnp.arange(blocks)
        low, high = turn % pieces, turn // pieces
        source = (((at // per) ^ low) * per + at % per) ^ self.place()
        up = self.own(0) ^ high
        return jnp.concatenate([jnp.stack([up * blocks, (1 - up) * blocks]), source]).astype(jnp.int32)

    def flat_order(self):
        blocks = self.count // 2
        place = jnp.int32(0)
        for step in range(len(self.bits) - 1):
            place = place * 2 + self.own(step)
        return (jnp.arange(blocks) ^ place).astype(jnp.int32)


def advance_kernel(plan, flag_ref, *refs):
    refs = list(refs)
    sent_ref, got_ref = refs.pop(0), refs.pop(0)
    inputs, outputs = refs[: plan["inputs"]], refs[plan["inputs"] :]
    message = outputs.pop(0)
    up = flag_ref[0]
    at = 0
    for mode, rows, first in plan["blocks"]:
        if mode == "half":
            kept, new = inputs.pop(0), outputs.pop(0)
            half = rows // 2
            own = pl.multiple_of(up * half, half)
            other = pl.multiple_of((1 - up) * half, half)
            new[...] = kept[pl.ds(own, half), :].astype(F32) + got_ref[pl.ds(first + own, half), :].astype(F32)
            send = kept[pl.ds(other, half), :].astype(F32) + got_ref[pl.ds(first + other, half), :].astype(F32)
            message[at : at + half, :] = send.astype(BF16)
            at += half
        elif mode in ("flat", "sum", "hold"):
            kept = inputs.pop(0)
            total = (kept[...].astype(F32) + got_ref[first : first + rows, :].astype(F32)).astype(BF16)
            if mode != "sum":
                outputs.pop(0)[...] = total
            if mode != "hold":
                message[at : at + rows, :] = total
                at += rows
        elif mode == "enter":
            message[at : at + rows, :] = inputs.pop(0)[...].astype(BF16)
            at += rows
        elif mode == "grow":
            message[at : at + rows, :] = sent_ref[first : first + rows, :]
            message[at + rows : at + 2 * rows, :] = got_ref[first : first + rows, :]
            at += 2 * rows
        else:
            total = sent_ref[first : first + rows, :].astype(F32) + got_ref[first : first + rows, :].astype(F32)
            message[at : at + rows, :] = total.astype(BF16)
            at += rows


def advance(flag, sent, got, blocks, inputs):
    width = sent.shape[1]
    grown = {"half": 0.5, "hold": 0, "grow": 2}
    total = int(sum(rows * grown.get(mode, 1) for mode, rows, _ in blocks))
    shapes = [jax.ShapeDtypeStruct((total, width), BF16)]
    for mode, rows, _ in blocks:
        if mode == "half":
            shapes.append(jax.ShapeDtypeStruct((rows // 2, width), F32))
        elif mode in ("flat", "hold"):
            shapes.append(jax.ShapeDtypeStruct((rows, width), BF16))
    return pl.pallas_call(
        functools.partial(advance_kernel, {"inputs": len(inputs), "blocks": blocks}),
        in_specs=[pl.BlockSpec(memory_space=pltpu.SMEM)] + [VMEM] * (2 + len(inputs)),
        out_specs=[VMEM] * len(shapes),
        out_shape=shapes,
        compiler_params=pltpu.CompilerParams(vmem_limit_bytes=12 << 20),
        name="advance",
    )(flag, sent, got, *inputs)


class Sum:
    def __init__(self, over, sent, flat, flags, rows=None):
        self.over, self.flat, self.flags = over, flat, flags
        self.kept, self.rider, self.count = None, None, 0
        self.rows = rows or [block.shape[0] for block in sent]
        self.message = sent[0] if rows else jnp.concatenate([block.astype(BF16) for block in sent], axis=0)
        self.got = over.swap(self.message, 0)

    def next(self, *earlier):
        steps = len(self.over.bits)
        k = self.count
        got = after(self.got, *earlier) if earlier else self.got
        blocks, inputs, rows, kept, first = [], [], [], [], 0
        for m, size in enumerate(self.rows):
            mode = "half" if k < steps - 1 else "sum" if k == steps - 1 else "grow"
            if self.flat[m]:
                mode = {steps - 2: "flat", steps - 1: "hold", steps: "enter"}.get(k, mode)
            if mode == "enter":
                size = self.kept[m].shape[0]
            blocks.append((mode, size, first))
            if mode != "grow":
                inputs.append(self.kept[m])
            first += 0 if mode == "enter" else size
            rows.append({"half": size // 2, "hold": 0, "grow": 2 * size}.get(mode, size))
        if self.rider is not None and k == steps - 1:
            blocks.append(("enter", self.rider.shape[0], 0))
            inputs.append(self.rider)
        elif self.rider is not None and k >= steps:
            blocks.append(("ride", self.rider.shape[0], first))
        flag = self.flags[min(k + 1, steps - 1)]
        self.message, *kept = advance(flag, self.message, got, blocks, inputs)
        for m, (mode, _, _) in enumerate(blocks[: len(rows)]):
            if mode in ("half", "flat", "hold"):
                self.kept[m] = kept.pop(0)
        self.rows = rows
        self.count = k + 1
        step = self.count if self.count < steps else 2 * steps - 1 - self.count
        self.got = self.over.swap(self.message, step)
        return self.message

    def run_out(self):
        while self.count < 2 * len(self.over.bits) - 1:
            self.next()


def silu_slope(values):
    logistic = jax.nn.sigmoid(values)
    return logistic * (1.0 + values * (1.0 - logistic))


def cost(ops, lanes, length, width, states):
    work = lanes * length * width * states
    return pl.CostEstimate(flops=ops * work * 16, bytes_accessed=work * 2, transcendentals=work)


def settle_kernel(names, layout, order_ref, *refs, starts=True, waits=True):
    parts, outs = refs[: len(layout)], refs[-2 - names : -2]
    wide, sems = refs[-2:]
    copies, at = [], 0
    for part, (out, lead, which, first, blocks, turned, offset, count) in zip(parts, layout, strict=True):
        size = count // blocks
        for b in range(blocks):
            source = order_ref[which + 2 + b]
            goal = pl.multiple_of((order_ref[which + first] + b) * size, size)
            ref = outs[out] if lead is None else outs[out].at[lead]
            if turned:
                spot = wide.at[at : at + part.shape[1], 0:size]
                target = ref.at[:, pl.ds(goal, size)]
            else:
                spot = wide.at[at : at + size, 0 : part.shape[1]]
                target = ref.at[pl.ds(goal, size), :]
            at += part.shape[1] if turned else size
            copies.append(pltpu.make_async_copy(spot, target, sems.at[len(copies)]))
            if starts:
                rows = part[pl.ds(pl.multiple_of(offset + source * size, size), size), :].astype(F32)
                spot[...] = jnp.transpose(rows) if turned else rows
                copies[-1].start()
    for copy in copies:
        if waits:
            copy.wait()


def settle(orders, parts, layout, shapes, into=()):
    any_space = pl.BlockSpec(memory_space=pl.ANY)
    rows = sum(p.shape[1] * l[4] if l[5] else l[7] for p, l in zip(parts, layout, strict=True))
    width = max(l[7] // l[4] if l[5] else p.shape[1] for p, l in zip(parts, layout, strict=True))
    count = sum(l[4] for l in layout)
    return pl.pallas_call(
        functools.partial(settle_kernel, len(shapes), layout),
        in_specs=[pl.BlockSpec(memory_space=pltpu.SMEM)] + [VMEM] * len(parts) + [any_space] * len(into),
        out_specs=[any_space] * len(shapes),
        out_shape=[jax.ShapeDtypeStruct(s, F32) for s in shapes],
        input_output_aliases={1 + len(parts) + k: k for k in range(len(into))},
        scratch_shapes=[pltpu.VMEM((rows, width), F32), pltpu.SemaphoreType.DMA((count,))],
        compiler_params=pltpu.CompilerParams(vmem_limit_bytes=16 << 20),
        name="settle",
    )(orders, *parts, *into)


def deal_rows(sizes, offset, order_ref, own_ref, late_ref, outs, rows):
    blocks = order_ref.shape[0]
    size = rows.shape[0] // blocks
    for b in range(blocks):
        source = order_ref[b]
        for part, first in ((own_ref, 0), (late_ref, blocks // 2)):

            @pl.when(jnp.logical_and(source >= first, source < first + blocks // 2))
            def _():
                at = pl.ds(pl.multiple_of(offset + (source - first) * size, size), size)
                rows[b * size : (b + 1) * size, :] = part[at, :].astype(F32)

    at = 0
    for out, count in zip(outs, sizes, strict=True):
        out[...] = rows[at : at + count, :]
        at += count


def finish_kernel(sizes, layout, offset, last, order_ref, flat_ref, own_ref, late_ref, into_ref, *refs):
    out, small, (total, rows, wide, sems) = refs[0], refs[1:-4], refs[-4:]
    settle_kernel(1, layout, order_ref, late_ref, out, wide, sems, waits=False)
    deal_rows(sizes, offset, flat_ref, own_ref, late_ref, small, rows)
    rider = own_ref[last : last + 16, :].astype(F32) + late_ref[last : last + 16, :].astype(F32)
    total[...] = rider[0:1, : total.shape[1]]
    settle_kernel(1, layout, order_ref, late_ref, out, wide, sems, starts=False)


def finish(orders, flat_order, own, late, layout, offset, count, sizes, gain_width, into):
    width = own.shape[1]
    any_space, smem = pl.BlockSpec(memory_space=pl.ANY), pl.BlockSpec(memory_space=pltpu.SMEM)
    shape = jax.ShapeDtypeStruct
    return pl.pallas_call(
        functools.partial(finish_kernel, sizes, layout, offset, offset + count),
        in_specs=[smem, smem, VMEM, VMEM, any_space],
        out_specs=[any_space] + [VMEM] * (len(sizes) + 1),
        out_shape=[shape(into.shape, F32)] + [shape((n, width), F32) for n in sizes] + [shape((1, gain_width), F32)],
        input_output_aliases={4: 0},
        scratch_shapes=[
            pltpu.VMEM((2 * count, width), F32),
            pltpu.VMEM((layout[0][7], width), F32),
            pltpu.SemaphoreType.DMA((layout[0][4],)),
        ],
        compiler_params=pltpu.CompilerParams(vmem_limit_bytes=16 << 20),
        name="finish",
    )(orders, flat_order, own, late, into)


def hop_kernel(got_ref, out_ref, back_ref, row_ref, message, other, out_new, back_new, row_new):
    lanes, length, width = out_ref.shape
    half = width // 2
    for l in range(lanes):
        for m, (kept, new, sent) in enumerate(((out_ref, out_new, other), (back_ref, back_new, message))):
            o = slice(m * length, (m + 1) * length)
            new[l] = kept[l, :, :half] + got_ref[l, o, :half].astype(F32)
            send = kept[l, :, half:] + got_ref[l, o, half:].astype(F32)
            sent[l, :length, :] = send.astype(BF16)
        rows = got_ref[l, 2 * length :, :].astype(F32)
        came = jnp.concatenate([rows[r : r + 1] for r in range(2 * length // width)], axis=1)
        total = row_ref[l : l + 1, :] + came[:, :length] + came[:, length:]
        row_new[l : l + 1, :] = total
        high = total.astype(BF16).astype(F32)
        both = jnp.concatenate([high, total - high], axis=1)
        pieces = [both[:, at : at + half] for at in range(0, 2 * length, half)]
        pieces.append(jnp.zeros((message.shape[1] - length - len(pieces), half), F32))
        message[l, length:, :] = jnp.concatenate(pieces, axis=0).astype(BF16)


def hop(got, out_kept, back_kept, row_dot):
    lanes, length, width = out_kept.shape
    shape = jax.ShapeDtypeStruct
    half = shape((lanes, length, width // 2), F32)
    rows = length - (-(4 * length // width) // 16) * 16
    return pl.pallas_call(
        hop_kernel,
        in_specs=[VMEM] * 4,
        out_specs=[VMEM] * 5,
        out_shape=[
            shape((lanes, rows, width // 2), BF16),
            shape((lanes, length, width // 2), BF16),
            half,
            half,
            shape(row_dot.shape, F32),
        ],
        compiler_params=pltpu.CompilerParams(vmem_limit_bytes=12 << 20),
        name="hop",
    )(got, out_kept, back_kept, row_dot)


def product_kernel(flag_ref, left_ref, right_ref, more_ref, message):
    half = message.shape[0] - more_ref.shape[0]
    at = pl.multiple_of((1 - flag_ref[0]) * half, half)
    for block in range(0, half, min(half, 256)):
        size = min(half, 256)
        cut = left_ref[:, pl.ds(pl.multiple_of(at + block, size), size)]
        total = lax.dot_general(cut, right_ref[...], (((0,), (0,)), ((), ())), preferred_element_type=F32)
        message[block : block + size, :] = total.astype(BF16)
    message[half:, :] = more_ref[...].astype(BF16)


def sent_product(flag, left, right, more):
    half, width = left.shape[1] // 2, right.shape[1]
    return pl.pallas_call(
        product_kernel,
        in_specs=[pl.BlockSpec(memory_space=pltpu.SMEM)] + [VMEM] * 3,
        out_specs=VMEM,
        out_shape=jax.ShapeDtypeStruct((half + more.shape[0], width), BF16),
        compiler_params=pltpu.CompilerParams(vmem_limit_bytes=16 << 20),
        name="sent_product",
    )(flag, left, right, more)


def pack_kernel(sizes, flag_ref, sent_ref, *refs):
    parts, (message, kept, rows) = refs[:-3], refs[-3:]
    at = 0
    for part, size in zip(parts, sizes, strict=True):
        if part.ndim == 3:
            total = part[0]
            for l in range(1, part.shape[0]):
                total = total + part[l]
            rows[at : at + size, :] = total
        else:
            rows[at : at + size, :] = part[0:size, :]
        at += size
    rows[at:, :] = jnp.zeros((rows.shape[0] - at, rows.shape[1]), F32)
    half, first = kept.shape[0], sent_ref.shape[0]
    up = flag_ref[0]
    kept[...] = rows[pl.ds(pl.multiple_of(up * half, half), half), :]
    message[0:first, :] = sent_ref[...]
    message[first:, :] = rows[pl.ds(pl.multiple_of((1 - up) * half, half), half), :].astype(BF16)


def pack(flag, sent, parts, sizes, half):
    width = sent.shape[1]
    shape = jax.ShapeDtypeStruct
    return pl.pallas_call(
        functools.partial(pack_kernel, sizes),
        in_specs=[pl.BlockSpec(memory_space=pltpu.SMEM)] + [VMEM] * (1 + len(parts)),
        out_specs=[VMEM] * 2,
        out_shape=[shape((sent.shape[0] + half, width), BF16), shape((half, width), F32)],
        scratch_shapes=[pltpu.VMEM((2 * half, width), F32)],
        compiler_params=pltpu.CompilerParams(vmem_limit_bytes=8 << 20),
        name="pack",
    )(flag, sent, *parts)


def join_kernel(lanes, short, up_ref, got_ref, log_ref, total_ref, window_ref, message, total, window):
    states, width = log_ref.shape
    rate = -jnp.exp(log_ref[...]) * LOG2E
    upper = up_ref[0] != 0
    count = lanes * states
    spans = got_ref[got_ref.shape[0] - 16 :, :].astype(F32)
    upper_next = up_ref[1] != 0
    sums, befores, behinds = [], [], []
    for l in range(lanes):
        s = slice(l * states, (l + 1) * states)
        g = slice(count + l * states, count + (l + 1) * states)
        span, came = total_ref[2 * count + l : 2 * count + l + 1, :], spans[l : l + 1]
        before = window_ref[2 * count + l : 2 * count + l + 1, :]
        behind = window_ref[2 * count + lanes + l : 2 * count + lanes + l + 1, :]
        through, through_came = jnp.exp2(span * rate), jnp.exp2(came * rate)
        end, pull = total_ref[s, :], total_ref[g, :]
        end_came = got_ref[s, :].astype(F32)
        pull_came = end_came if short[0] else got_ref[g, :].astype(F32)
        end_new = jnp.where(upper, end + through * end_came, end_came + through_came * end)
        pull_new = jnp.where(upper, pull_came + through_came * pull, pull + through * pull_came)
        total[s, :], total[g, :] = end_new, pull_new
        if short[1]:
            message[s, :] = jnp.where(upper_next, pull_new, end_new).astype(BF16)
        else:
            message[s, :], message[g, :] = end_new.astype(BF16), pull_new.astype(BF16)
        enter = window_ref[s, :] + jnp.exp2(before * rate) * end_came
        leave = window_ref[g, :] + jnp.exp2(behind * rate) * pull_came
        window[s, :] = jnp.where(upper, enter, window_ref[s, :])
        window[g, :] = jnp.where(upper, window_ref[g, :], leave)
        sums.append(span + came)
        befores.append(jnp.where(upper, before + came, before))
        behinds.append(jnp.where(upper, behind, behind + came))
    fill = jnp.zeros((8 - lanes, width), F32)
    rows = jnp.concatenate([*sums, fill], axis=0)
    total[2 * count :, :] = rows
    message[message.shape[0] - 16 :, :] = jnp.concatenate([rows, jnp.zeros((8, width), F32)], axis=0).astype(BF16)
    fill = jnp.zeros((8 - 2 * lanes, width), F32)
    window[2 * count :, :] = jnp.concatenate([*befores, *behinds, fill], axis=0)


def join(lanes, short, up, got, log, total, window):
    shape = jax.ShapeDtypeStruct
    rows = 16 + lanes * log.shape[0] * (1 if short[1] else 2)
    return pl.pallas_call(
        functools.partial(join_kernel, lanes, short),
        in_specs=[pl.BlockSpec(memory_space=pltpu.SMEM)] + [VMEM] * 4,
        out_specs=[VMEM] * 3,
        out_shape=[shape((rows, got.shape[1]), BF16), shape(total.shape, F32), shape(window.shape, F32)],
        compiler_params=pltpu.CompilerParams(vmem_limit_bytes=8 << 20),
        name="join",
    )(up, got, log, total, window)


def iota(shape, dim):
    return lax.broadcasted_iota(jnp.int32, shape, dim)


def widen(part, width):
    return jnp.concatenate([part] * (width // part.shape[1]), axis=1)


def dot(a, b):
    return jnp.dot(a, b, preferred_element_type=F32)


def dot_t(a, b):
    return lax.dot_general(a, b, (((1,), (1,)), ((), ())), preferred_element_type=F32)


def row_of(ref, t, count):
    return jnp.broadcast_to(ref[pl.ds(t, 1), :], (count, ref.shape[1]))


def rows_of(i, count):
    return pl.ds(pl.multiple_of(i * count, count), count)


def chunk_columns(ref, i):
    per = LANE // CHUNK
    tile = ref[:, rows_of(i // per, LANE)]
    return pltpu.roll(tile, LANE - (i % per) * CHUNK, 1)


def spread_column(tile, j, width):
    part = jnp.broadcast_to(tile[:, j : j + 1], (tile.shape[0], LANE))
    return widen(part, width)


def selectors(states):
    wide = CHUNK * states
    per_state = iota((states, wide), 1) % states == iota((states, wide), 0)
    per_step = iota((CHUNK, wide), 1) // states == iota((CHUNK, wide), 0)
    return per_state.astype(F32), per_step.astype(F32)


def from_lanes(first, states):
    shape = (LANE, CHUNK * states)
    return (iota(shape, 0) == first + iota(shape, 1) % states).astype(BF16)


def to_lanes(first, states):
    shape = (CHUNK * states, LANE)
    return (iota(shape, 1) == first + iota(shape, 0) % states).astype(BF16)


def by_step(proj, lanes, per_step):
    spread = dot(proj, lanes)
    return spread * jnp.concatenate([per_step] * (spread.shape[0] // CHUNK), axis=0)


def ends_kernel(
    low_rank, sent_ref, got_ref, wdt_ref, bias_ref, log_ref, mixed_ref, gy_ref,
    end_ref, pull_ref, span_ref, dt_ref, u_ref, proj_ref,
    ahead, behind, left_b, left_c, xa, xb, ya, yb,
):
    length, width = dt_ref.shape
    states = log_ref.shape[0]
    rate = -jnp.exp(log_ref[...]) * LOG2E
    per_state, per_step = selectors(states)
    chunks = length // CHUNK
    upto = (iota((length, length), 1) <= iota((length, length), 0)).astype(BF16)
    after = (iota((length, length), 1) > iota((length, length), 0)).astype(BF16)
    proj = sent_ref[...].astype(F32) + got_ref[...].astype(F32)
    proj_ref[...] = proj
    proj = proj.astype(BF16)
    for first, left in ((low_rank, left_b), (low_rank + states, left_c)):
        spread = by_step(proj, from_lanes(first, states), per_step)
        for i in range(chunks):
            flat = jnp.sum(spread[i * CHUNK : (i + 1) * CHUNK], axis=0, keepdims=True)
            left[i * states : (i + 1) * states, :] = (flat * per_state).astype(BF16)
    block = min(128, length)
    for i in range(length // block):
        o = slice(i * block, (i + 1) * block)
        pre = dot(proj[o], wdt_ref[...]) + bias_ref[...]
        small = jnp.exp(-jnp.abs(pre))
        one = 1.0 + small
        series = small * (1.0 - small * (0.5 - small * (1.0 / 3.0)))
        dt = jnp.maximum(pre, 0.0) + jnp.where(small < 1e-3, series, jnp.log(one))
        dt_ref[o, :] = dt
        u_ref[o, :] = dt * mixed_ref[o, :]
    dt = dt_ref[...]
    high = dt.astype(BF16)
    low = (dt - high.astype(F32)).astype(BF16)
    ahead[...] = dot(upto, high) + dot(upto, low)
    behind[...] = dot(after, high) + dot(after, low)
    span_ref[...] = ahead[length - 1 : length, :]
    xb[...] = jnp.zeros(xb.shape, BF16)
    yb[...] = jnp.zeros(yb.shape, BF16)

    def flush(i, x, y, sums):
        o = rows_of(jnp.maximum(i, 0), states)
        return sums[0] + dot(left_b[o, :], x[...]), sums[1] + dot(left_c[o, :], y[...])

    def fill(i, x, y):
        for j in range(CHUNK):
            t = i * CHUNK + j
            s = slice(j * states, (j + 1) * states)
            to_end = jnp.exp2(row_of(behind, t, states) * rate)
            x[s, :] = (to_end * row_of(u_ref, t, states)).astype(BF16)
            to_here = jnp.exp2(row_of(ahead, t, states) * rate)
            y[s, :] = (to_here * row_of(gy_ref, t, states)).astype(BF16)

    def body(k, sums):
        for i in range(0, chunks, 2):
            at = chunks * k + i
            sums = flush(at - 1, xb, yb, sums)
            fill(at, xa, ya)
            sums = flush(at, xa, ya, sums)
            fill(at + 1, xb, yb)
        return sums

    zero = jnp.zeros((states, width), F32)
    sums = body(0, (zero, zero))
    sums = flush(chunks - 1, xb, yb, sums)
    end_ref[...] = sums[0]
    pull_ref[...] = sums[1]


def lane_spec(*shape):
    return pl.BlockSpec((None, *shape), lambda l: (l,) + (0,) * len(shape))


def whole_spec(*shape):
    return pl.BlockSpec(shape, lambda l: (0,) * len(shape))


def scan_ends(low_rank, sent, got, w_dt, bias, log, mixed, gy):
    lanes, length, width = mixed.shape
    states = log.shape[0]
    shape = jax.ShapeDtypeStruct
    token = shape((lanes, length, width), F32)
    state = shape((lanes, states, width), F32)
    tokens, state_spec, narrow = lane_spec(length, width), lane_spec(states, width), lane_spec(length, LANE)
    return pl.pallas_call(
        functools.partial(ends_kernel, low_rank),
        grid=(lanes,),
        in_specs=[
            narrow,
            narrow,
            whole_spec(*w_dt.shape),
            whole_spec(1, width),
            whole_spec(states, width),
            tokens,
            tokens,
        ],
        out_specs=[state_spec, state_spec, lane_spec(1, width), tokens, tokens, narrow],
        out_shape=[state, state, shape((lanes, 1, width), F32)]
        + [pltpu.HBM((lanes, length, width), F32)] * 2
        + [shape(sent.shape, F32)],
        scratch_shapes=[pltpu.VMEM((length, width), F32)] * 2
        + [pltpu.VMEM((length // CHUNK * states, CHUNK * states), BF16)] * 2
        + [pltpu.VMEM((CHUNK * states, width), BF16)] * 4,
        compiler_params=pltpu.CompilerParams(vmem_limit_bytes=14 << 20),
        cost_estimate=cost(8, lanes, length, width, states),
        name="scan_ends",
    )(sent, got, w_dt, bias, log, mixed, gy)


def forward_kernel(
    low_rank, lanes, starts_ref, proj_ref, log_ref, dt_ref, u_ref, gy_ref, begin_ref,
    y_ref, gc_ref, hs_ref,
    kept, pa, pb, cols, left_c, masked, sems,
):
    length, width = dt_ref.shape
    states = log_ref.shape[0]
    l = pl.program_id(0)
    rate = -jnp.exp(log_ref[...]) * LOG2E
    _, per_step = selectors(states)
    wide = CHUNK * states
    chunks = length // CHUNK

    half = chunks // 2 * wide

    def leave(slot, part):
        rows = pl.ds(part * half, half)
        return pltpu.make_async_copy(kept.at[slot, rows, :], hs_ref.at[slot, rows, :], sems.at[slot, part])

    begin = jnp.where(starts_ref[l] != 0, 0.0, begin_ref[...])
    proj = proj_ref[...]
    cols[...] = jnp.transpose(proj)[low_rank : low_rank + states]
    spread = by_step(proj.astype(BF16), from_lanes(low_rank + states, states), per_step)
    left_c[...] = spread.astype(BF16)

    def flush(i, p):
        o = rows_of(jnp.maximum(i, 0), CHUNK)
        h = p[...]
        y_ref[o, :] = dot(left_c[o, :], h)
        masked[o, :] = (dot_t(gy_ref[o, :].astype(BF16), h) * per_step).astype(BF16)

    def fill(i, state, p):
        b_tile = chunk_columns(cols, i)
        low = state.astype(BF16)
        for j in range(CHUNK):
            t = i * CHUNK + j
            b = spread_column(b_tile, j, width)
            decay = jnp.exp2(row_of(dt_ref, t, states) * rate)
            state = decay * state + row_of(u_ref, t, states) * b
            kept[l, rows_of(t, states), :] = low
            low = state.astype(BF16)
            p[j * states : (j + 1) * states, :] = low
        return state

    def body(k, state):
        for i in range(0, ROUND, 2):
            at = ROUND * k + i
            flush(at - 1, pb)
            state = fill(at, state, pa)
            flush(at, pa)
            state = fill(at + 1, state, pb)
        return state

    rounds = chunks // ROUND
    state = lax.fori_loop(0, rounds // 2, body, begin)
    leave(l, 0).start()
    lax.fori_loop(rounds // 2, rounds, body, state)
    leave(l, 1).start()
    flush(chunks - 1, pb)
    gc_ref[...] = dot(masked[...], to_lanes(low_rank + states, states))

    @pl.when(l == lanes - 1)
    def _():
        for slot in range(lanes):
            for part in range(2):
                leave(slot, part).wait()


def scan_forward(low_rank, starts, proj, log, dt, u, gy, begin):
    lanes, length, width = dt.shape
    states = log.shape[0]
    shape = jax.ShapeDtypeStruct
    tokens, state_spec, narrow = lane_spec(length, width), lane_spec(states, width), lane_spec(length, LANE)
    return pl.pallas_call(
        functools.partial(forward_kernel, low_rank, lanes),
        grid=(lanes,),
        in_specs=[
            pl.BlockSpec(memory_space=pltpu.SMEM),
            narrow,
            whole_spec(states, width),
            tokens,
            tokens,
            tokens,
            state_spec,
        ],
        out_specs=[tokens, narrow, pl.BlockSpec(memory_space=pltpu.HBM)],
        out_shape=[
            shape((lanes, length, width), F32),
            shape(proj.shape, F32),
            shape((lanes, length * states, width), BF16),
        ],
        scratch_shapes=[pltpu.VMEM((lanes, length * states, width), BF16)]
        + [pltpu.VMEM((CHUNK * states, width), BF16)] * 2
        + [
            pltpu.VMEM((states, length), F32),
            pltpu.VMEM((length, CHUNK * states), BF16),
            pltpu.VMEM((length, CHUNK * states), BF16),
            pltpu.SemaphoreType.DMA((lanes, 2)),
        ],
        compiler_params=pltpu.CompilerParams(vmem_limit_bytes=20 << 20),
        cost_estimate=cost(8, lanes, length, width, states),
        name="scan_forward",
    )(starts, proj, log, dt, u, gy, begin)


def backward_kernel(
    low_rank, lanes, proj_ref, log_ref, dt_ref, u_ref, gy_ref, last_ref, gc_ref, hs_ref, *refs
):
    (turn_ref, pull_ref, gbc_ref, ga_ref,
     kept, pa, pb, qa, qb, ra, rb, cols, left_b, masked, sems) = refs[-15:]
    length, width = dt_ref.shape
    states = log_ref.shape[0]
    l = pl.program_id(0)
    plain = -jnp.exp(log_ref[...])
    rate = plain * LOG2E
    rate_low = plain.astype(BF16)
    per_state, per_step = selectors(states)
    per_state_low, per_step_low = per_state.astype(BF16), per_step.astype(BF16)
    chunks = length // CHUNK

    half = length // 2 * states

    def enter(slot, part):
        rows = pl.ds(part * half, half)
        return pltpu.make_async_copy(hs_ref.at[slot, rows, :], kept.at[slot, rows, :], sems.at[slot, part])

    @pl.when(l == 0)
    def _():
        for slot in range(lanes):
            for part in (1, 0):
                enter(slot, part).start()

    for ref in (pb, qb, rb):
        ref[...] = jnp.zeros(ref.shape, BF16)
    proj = proj_ref[...]
    cols[...] = jnp.transpose(proj)[low_rank + states : low_rank + 2 * states]
    left_b[...] = by_step(proj.astype(BF16), from_lanes(low_rank, states), per_step).astype(BF16)

    def flush(i, p, q, r, ga):
        o = rows_of(jnp.minimum(i, chunks - 1), CHUNK)
        grad = p[...]
        pull_ref[o, :] = dot(left_b[o, :], grad)
        masked[o, :] = (dot_t(u_ref[o, :].astype(BF16), grad) * per_step).astype(BF16)
        turn_ref[o, :] = dot(per_step_low, q[...])
        return ga + dot(per_state_low, r[...])

    def fill(i, carry, p, q, r):
        c_tile = chunk_columns(cols, i)
        for j in reversed(range(CHUNK)):
            t = i * CHUNK + j
            s = slice(j * states, (j + 1) * states)
            c = spread_column(c_tile, j, width)
            dt = row_of(dt_ref, t, states)
            grad = carry + row_of(gy_ref, t, states) * c
            carry = jnp.exp2(dt * rate) * grad
            p[s, :] = grad.astype(BF16)
            turn = carry.astype(BF16) * kept[l, rows_of(t, states), :] * rate_low
            q[s, :] = turn
            r[s, :] = turn * dt.astype(BF16)
        return carry

    def body(k, carried):
        carry, ga = carried
        for i in range(0, ROUND, 2):
            at = chunks - 1 - ROUND * k - i
            ga = flush(at + 1, pb, qb, rb, ga)
            carry = fill(at, carry, pa, qa, ra)
            ga = flush(at, pa, qa, ra, ga)
            carry = fill(at - 1, carry, pb, qb, rb)
        return carry, ga

    rounds = chunks // ROUND
    carried = (last_ref[...], jnp.zeros((states, width), F32))
    enter(l, 1).wait()
    carried = lax.fori_loop(0, rounds // 2, body, carried)
    enter(l, 0).wait()
    _, ga = lax.fori_loop(rounds // 2, rounds, body, carried)
    ga_ref[...] = flush(0, pb, qb, rb, ga)
    gbc_ref[...] = gc_ref[...] + dot(masked[...], to_lanes(low_rank, states))


def scan_backward(low_rank, proj, log, dt, u, gy, last, gc, hs, *earlier):
    lanes, length, width = dt.shape
    states = log.shape[0]
    shape = jax.ShapeDtypeStruct
    tokens, state_spec, narrow = lane_spec(length, width), lane_spec(states, width), lane_spec(length, LANE)
    token = shape((lanes, length, width), F32)
    return pl.pallas_call(
        functools.partial(backward_kernel, low_rank, lanes),
        grid=(lanes,),
        in_specs=[narrow, whole_spec(states, width), tokens, tokens, tokens, state_spec, narrow]
        + [pl.BlockSpec(memory_space=pltpu.HBM)]
        + [pl.BlockSpec(memory_space=pl.ANY)] * len(earlier),
        out_specs=[tokens, tokens, narrow, state_spec],
        out_shape=[token, token, shape(proj.shape, F32), shape((lanes, states, width), F32)],
        scratch_shapes=[pltpu.VMEM((lanes, length * states, width), BF16)]
        + [pltpu.VMEM((CHUNK * states, width), BF16)] * 6
        + [
            pltpu.VMEM((states, length), F32),
            pltpu.VMEM((length, CHUNK * states), BF16),
            pltpu.VMEM((length, CHUNK * states), BF16),
            pltpu.SemaphoreType.DMA((lanes, 2)),
        ],
        compiler_params=pltpu.CompilerParams(vmem_limit_bytes=22 << 20),
        cost_estimate=cost(12, lanes, length, width, states),
        name="scan_backward",
    )(proj, log, dt, u, gy, last, gc, hs, *earlier)


def per_device(
    inputs,
    row_starts,
    norm_gain,
    in_weight,
    conv_weight,
    conv_bias,
    xproj_weight,
    dtproj_weight,
    dt_bias,
    decay_log,
    skip_gain,
    out_weight,
    output_grad,
):
    lane_count, length, shard_width = inputs.shape
    low_rank = dtproj_weight.shape[0]
    state_count = decay_log.shape[0]
    tap_count = conv_weight.shape[0]
    inner_width = conv_bias.shape[0]
    model_width = norm_gain.shape[0]
    starts = row_starts.astype(F32)
    carry_mask = (1.0 - starts)[:, :, None]
    mp_index, mp_size = lax.axis_index("mp"), lax.axis_size("mp")
    seq_index, seq_size = lax.axis_index("seq"), lax.axis_size("seq")
    mp_bits, seq_bits = bits_of("mp"), bits_of("seq")
    near_first = [int(format(k, "0%db" % len(mp_bits))[::-1], 2) for k in range(mp_size)]

    def blocks(array, axis, order):
        parts = [
            lax.dynamic_slice_in_dim(array, (mp_index ^ k) * shard_width, shard_width, axis) for k in order
        ]
        return jnp.concatenate(parts, axis=axis)

    x_parts, grad_parts = {0: inputs.astype(BF16)}, {}
    square = jnp.sum(jnp.square(inputs), axis=2)
    for bit in reversed(mp_bits):
        for k in list(x_parts):
            x_parts[k | bit] = swap(x_parts[k], "mp", bit)
        square = square + swap(square, "mp", bit)
    grad_parts[0] = after(output_grad.astype(BF16), x_parts[mp_bits[-1]])
    for bit in reversed(mp_bits[1:]):
        for k in list(grad_parts):
            grad_parts[k | bit] = swap(grad_parts[k], "mp", bit)
    near = list(range(mp_size))
    over = Reduction()
    per = shard_width * seq_size // model_width
    halves = seq_size // 2
    ups = ((seq_index & jnp.array([*seq_bits, 0])) != 0).astype(jnp.int32)
    ups = [ups[step : step + 2] for step in range(len(seq_bits))]
    orders = jnp.concatenate([over.order(per, mp_index), over.order(1, 0)])
    flat_order = over.flat_order()
    flags = [over.own(step)[None] for step in range(len(seq_bits))]
    span_more = FAR * starts[:, :, None]
    w_in = blocks(in_weight, 1, near).astype(BF16)
    w_out = lax.optimization_barrier(out_weight.astype(BF16))
    gain = blocks(norm_gain, 0, near)
    w_x = jnp.pad(xproj_weight.astype(BF16), ((0, 0), (0, -xproj_weight.shape[1] % LANE)))
    w_dt = jnp.pad(dtproj_weight.astype(BF16), ((0, -low_rank % LANE), (0, 0)))
    w_dt = lax.optimization_barrier(w_dt)
    inv_rms = lax.rsqrt(square[:, :, None] / model_width + 1e-05)
    x_parts[near[-1]] = after(x_parts[near[-1]], orders, flat_order, span_more, *flags, *ups, w_out, w_dt)
    x_whole = jnp.concatenate([x_parts[k] for k in near], axis=2)
    normed = (x_whole.astype(F32) * inv_rms * gain).astype(BF16)
    rim_count = 8
    rim_normed = from_behind(normed[:, length - rim_count :, :], "seq", 1)
    inner_act = jnp.einsum("ltd,de->lte", normed, w_in[0], preferred_element_type=F32).astype(BF16)
    rim_rows = jnp.einsum("ltd,de->lte", rim_normed, w_in[0], preferred_element_type=F32).astype(BF16)
    rim_rows = after(rim_rows, *grad_parts.values())
    rim_rows = (rim_rows.astype(F32) * carry_mask)[:, rim_count - (tap_count - 1) :]
    padded = jnp.concatenate([rim_rows, inner_act.astype(F32)], axis=1)
    conv_sum = conv_bias + conv_weight[0] * padded[:, 0:length]
    for tap in range(1, tap_count):
        conv_sum = conv_sum + conv_weight[tap] * padded[:, tap : tap + length]
    mixed = jax.nn.silu(conv_sum)
    mixed_low = mixed.astype(BF16)
    sent = jnp.einsum("lte,er->ltr", mixed_low, w_x, preferred_element_type=F32).astype(BF16)
    for bit in mp_bits[:-1]:
        sent = (sent.astype(F32) + swap(sent, "mp", bit).astype(F32)).astype(BF16)
    got = swap(sent, "mp", mp_bits[-1])
    gate_in = jnp.einsum("ltd,de->lte", after(normed, sent), w_in[1], preferred_element_type=F32)
    for k in list(grad_parts):
        grad_parts[k] = after(grad_parts[k], sent)
        grad_parts[k | 1] = swap(grad_parts[k], "mp", 1)
    normed_more = jnp.concatenate(
        [after(normed, sent).reshape(-1, model_width), rim_normed.reshape(-1, model_width)], axis=0
    )[None]
    grad_whole = jnp.concatenate(
        [
            sum(jnp.where(k == (mp_index ^ block), grad_parts[k], 0) for k in range(mp_size))
            for block in range(mp_size)
        ],
        axis=2,
    )
    grad_gated = jnp.einsum("ltd,ed->lte", grad_whole, w_out, preferred_element_type=F32)
    grad_scan = grad_gated * jax.nn.silu(gate_in)
    end_state, pulled, span, dt, source, projected = scan_ends(
        low_rank, sent, got, w_dt, dt_bias[None], decay_log, mixed, grad_scan
    )
    span = span + span_more
    count = lane_count * state_count
    flat = (count, inner_width)
    total = jnp.concatenate(
        [
            end_state.reshape(flat),
            (pulled * carry_mask).reshape(flat),
            span.reshape(lane_count, inner_width),
            jnp.zeros((8 - lane_count, inner_width), F32),
        ],
        axis=0,
    )
    message = jnp.pad(total.astype(BF16), ((0, 8), (0, 0)))
    window = jnp.zeros_like(total)
    for step, bit in enumerate(seq_bits):
        short = (step == len(seq_bits) - 1, step == len(seq_bits) - 2)
        if step == 0:
            w_late = after(w_out, message)
            w_spread = blocks(w_late, 1, near_first)
            w_late = after(w_in, message)
            w_back = jnp.concatenate(
                [w_late[:, k * shard_width : (k + 1) * shard_width] for k in near_first], axis=1
            )
        got = swap(message, "seq", bit)
        message, total, window = join(lane_count, short, ups[step], got, decay_log, total, window)
    window = window.reshape(-1, inner_width)
    begin = window[:count].reshape(end_state.shape)
    last = window[count : 2 * count].reshape(end_state.shape)
    projected, normed_more, w_back, w_spread = lax.optimization_barrier(
        (projected, normed_more, w_back, w_spread)
    )
    y, grad_read, states_all = scan_forward(
        low_rank, row_starts[:, 0], projected, decay_log, dt, source, grad_scan, begin
    )
    scan_out = y + skip_gain * mixed
    gated = (scan_out * jax.nn.silu(gate_in)).astype(BF16)
    grad_gate = (grad_gated * scan_out * silu_slope(gate_in)).astype(BF16)
    half_width = model_width // 2
    first = [over.sent(normed, grad_gate)]
    first.append(over.sent(grad_whole, after(gated, first[0])))
    sum_first = Sum(over, first, (False, False), flags)
    sum_first.kept = [over.kept(after(normed, sum_first.message), grad_gate)]
    sum_first.kept.append(over.kept(grad_whole, after(gated, sum_first.kept[0])))
    turn, pull, part, grad_log = scan_backward(
        low_rank, projected, decay_log, dt, source, grad_scan, last, grad_read, states_all, *sum_first.kept
    )
    grad_slope = (turn + pull * mixed) * -jnp.expm1(-dt)
    grad_pre = grad_slope.astype(BF16)
    part = part + jnp.einsum("lte,re->ltr", grad_pre, w_dt, preferred_element_type=F32)
    sent = part.astype(BF16)
    for bit in mp_bits[:-1]:
        got = swap(sent, "mp", bit)
        if bit == 1:
            got = after(got, sum_first.next(sent))
        sent = (sent.astype(F32) + got.astype(F32)).astype(BF16)
    got = swap(sent, "mp", mp_bits[-1])
    grad_dt_w = jnp.einsum(
        "ltr,lte->re", projected.astype(BF16), after(grad_pre, sent), preferred_element_type=F32
    )
    grad_projected = after(sent, grad_dt_w).astype(F32) + got.astype(F32)
    grad_projected = grad_projected.astype(BF16)
    grad_mixed = pull * dt + grad_scan * skip_gain + jnp.einsum(
        "ltr,er->lte", grad_projected, w_x, preferred_element_type=F32
    )
    grad_conv = grad_mixed * silu_slope(conv_sum)
    grad_conv_b = jnp.sum(grad_conv, axis=(0, 1))
    grad_conv_w = jnp.stack(
        [
            jnp.sum(grad_conv * padded[:, tap : tap + length], axis=(0, 1))
            for tap in range(tap_count)
        ]
    )
    grad_padded = jnp.pad(conv_weight[0] * grad_conv, ((0, 0), (0, tap_count - 1), (0, 0)))
    for tap in range(1, tap_count):
        grad_padded = grad_padded + jnp.pad(
            conv_weight[tap] * grad_conv, ((0, 0), (tap, tap_count - 1 - tap), (0, 0))
        )
    rim_sent = grad_padded[:, : tap_count - 1] * carry_mask
    rim_fill = jnp.zeros((lane_count, rim_count - (tap_count - 1), inner_width), F32)
    rim_rows = jnp.concatenate([rim_fill, rim_sent], axis=1).astype(BF16)
    grad_main = grad_padded[:, tap_count - 1 :].astype(BF16)
    grad_more = jnp.concatenate(
        [grad_main.reshape(-1, inner_width), rim_rows.reshape(-1, inner_width)], axis=0
    )[None]
    grad_x_w = jnp.einsum("ltr,lte->re", grad_projected, after(mixed_low, rim_sent), preferred_element_type=F32)
    small = [
        (grad_conv_w, tap_count),
        (grad_conv_b[None], 1),
        (jnp.sum(grad_slope, axis=(0, 1))[None], 1),
        (jnp.sum(grad_scan * mixed, axis=(0, 1))[None], 1),
        (grad_log, state_count),
        (grad_dt_w, low_rank),
        (grad_x_w, low_rank + 2 * state_count),
    ]
    sizes = [size for _, size in small]
    small_half = -(-sum(sizes) // (8 * seq_size)) * 4 * seq_size
    inner_sent = over.sent(normed_more, after(grad_more, grad_x_w))
    inner_sent, small_kept = pack(flags[0], inner_sent, [part for part, _ in small], sizes, small_half)
    sum_inner = Sum(over, [inner_sent], (False, True), flags, [half_width, small_half])
    step = sum_first.next(sum_inner.message)
    sum_inner.kept = [over.kept(normed_more, after(grad_more, step)), small_kept]
    rim_back = from_behind(after(rim_sent, step), "seq", -1)
    out_sent = jnp.einsum(
        "lte,ed->ltd", after(gated, sum_inner.kept[0]), w_spread[:, half_width:], preferred_element_type=F32
    ).astype(BF16)
    out_kept = jnp.einsum(
        "lte,ed->ltd", after(gated, out_sent), w_spread[:, :half_width], preferred_element_type=F32
    )
    tail_zeros = jnp.zeros((lane_count, length - (tap_count - 1), inner_width), F32)
    grad_inner = grad_padded[:, tap_count - 1 :] + jnp.concatenate(
        [tail_zeros, after(rim_back, out_kept)], axis=1
    )
    grad_inner = grad_inner.astype(BF16)

    def back(part, cut):
        return jnp.einsum("lte,de->ltd", part[0], w_back[0, cut], preferred_element_type=F32) + jnp.einsum(
            "lte,de->ltd", part[1], w_back[1, cut], preferred_element_type=F32
        )

    back_sent = back((grad_inner, grad_gate), slice(half_width, None)).astype(BF16)
    back_kept = back((after(grad_inner, back_sent), grad_gate), slice(0, half_width))
    row_dot = jnp.sum(
        after(grad_inner, back_kept).astype(F32) * inner_act.astype(F32) + grad_gate.astype(F32) * gate_in,
        axis=2,
    )

    def as_rows(values, width):
        high = values.astype(BF16)
        low = (values - high.astype(F32)).astype(BF16)
        rows = jnp.concatenate([high, low], axis=1).reshape(lane_count, -1, width)
        return jnp.pad(rows, ((0, 0), (0, -rows.shape[1] % 16), (0, 0)))

    message = jnp.concatenate([out_sent, back_sent, as_rows(row_dot, half_width)], axis=1)
    step = sum_inner.next(message)
    step = sum_first.next(step)
    got = swap(after(message, step), "mp", 1)
    far = mp_bits[-1]
    for bit in mp_bits[:-1]:
        if bit == 1:
            step = sum_inner.next(message)
            step = sum_first.next(step)
        message, other, out_kept, back_kept, row_dot = hop(after(got, step), out_kept, back_kept, row_dot)
        if 2 * bit == far:
            got = swap(message, "mp", far)
            out_got = swap(after(other, message), "mp", far)
        else:
            message = jnp.concatenate([other, message], axis=1)
            got = swap(message, "mp", 2 * bit)
    got = after(got, message)
    rows = got[:, length:][:, : 2 * length // shard_width].reshape(lane_count, 2 * length).astype(F32)
    row_dot = row_dot + rows[:, :length] + rows[:, length:]
    grad_own = back_kept + got[:, :length].astype(F32)
    unit_own = inputs * inv_rms
    grad_gain = jnp.sum(grad_own * unit_own, axis=(0, 1))
    input_grad = output_grad + inv_rms * (
        grad_own * gain[:shard_width] - unit_own * (row_dot[:, :, None] / model_width)
    )
    grad_gain = jnp.pad(grad_gain, (0, -shard_width % inner_width)).reshape(-1, inner_width)
    sum_inner.rider = jnp.pad(grad_gain, ((0, -grad_gain.shape[0] % 16), (0, 0)))
    step = sum_inner.next(grad_gain)
    step = sum_first.next(step)
    input_grad = after(input_grad, step)
    step = sum_inner.next(step)
    output = inputs + (out_kept + after(out_got, step).astype(F32))
    step = sum_inner.next(output)
    sum_first.run_out()
    second = 2 + halves
    in_shape, out_shape = (2, model_width, inner_width), out_weight.shape
    half = model_width // 2
    layout = [(0, 1, 0, 0, halves, False, 0, half), (0, 1, 0, 1, halves, False, 0, half)]
    ends = (sum_first.message, after(sum_first.got, step))
    if model_width // seq_size % LANE == 0:
        layout += [(1, None, second, 0, halves, True, half, half), (1, None, second, 1, halves, True, half, half)]
        in_w, out_w = settle(orders, [*ends, *ends], layout, [in_shape, out_shape])
    else:
        (in_w,) = settle(orders, [*ends], layout, [in_shape])
        rows = [p[half:].reshape(halves, -1, inner_width)[orders[second + 2 :]].reshape(half, -1) for p in ends]
        up = over.own(0) == 1
        rows = [jnp.where(up, rows[1], rows[0]), jnp.where(up, rows[0], rows[1])]
        out_w = jnp.concatenate(rows, axis=0).astype(F32).T
    sum_inner.run_out()
    ends = (sum_inner.message, sum_inner.got)
    in_w = settle(orders, ends[:1], [(0, 0, 0, 0, halves, False, 0, half)], [in_shape], [in_w])
    count = small_half
    in_w, *parts, grad_gain = finish(
        orders, flat_order, *ends, [(0, 0, 0, 1, halves, False, 0, half)], half, count, sizes, shard_width, in_w[0]
    )
    return (
        output,
        input_grad,
        grad_gain[0],
        in_w,
        parts[0],
        parts[1][0],
        parts[6].T,
        parts[5],
        parts[2][0],
        parts[4],
        parts[3][0],
        out_w,
    )


def solution(mesh):
    in_specs = (
        P(None, "seq", "mp"),
        P(None, "seq"),
        P(),
        P(None, None, "mp"),
        P(None, "mp"),
        P("mp"),
        P("mp", None),
        P(None, "mp"),
        P("mp"),
        P(None, "mp"),
        P("mp"),
        P("mp", None),
        P(None, "seq", "mp"),
    )
    out_specs = (
        P(None, "seq", "mp"),
        P(None, "seq", "mp"),
        P("mp"),
        P(None, None, "mp"),
        P(None, "mp"),
        P("mp"),
        P("mp", None),
        P(None, "mp"),
        P("mp"),
        P(None, "mp"),
        P("mp"),
        P("mp", None),
    )
    return jax.shard_map(
        per_device, mesh=mesh, in_specs=in_specs, out_specs=out_specs, check_vma=False
    )
```
